256 devices in a mesh: lon: 64 (over y_lo, z, x), lat: 4 (over y_hi, core).
Axes of the slice: x: 4, y: 4 (y_hi: 2, y_lo: 2; y = y_hi * 2 + y_lo), z: 8, core: 2. Of those that a mesh axis runs over, the one named last changes fastest.
Arguments:
- tokens: bfloat16 [2, 24, 3072, 384], P(None, 'lat', 'lon'), may hold values from -6 to 6
- cotangent: bfloat16 [2, 24, 3072, 384], P(None, 'lat', 'lon'), may hold values from -40 to 40
- mask_ids: int32 [2, 24], P(None, 'lat'), may hold values from 0 to 1
- band_type: int32 [4], replicated, may hold values from 0 to 3, each once
- bias_table: bfloat16 [4, 12, 3312], replicated, may hold values from -4 to 4
- w_qkv: bfloat16 [384, 1152], replicated, may hold values from -0.3125 to 0.3125
- w_proj: bfloat16 [384, 384], replicated, may hold values from -0.3125 to 0.3125
- ln_gain: float32 [384], replicated, may hold values from 0.5 to 1.5
- ln_shift: float32 [384], replicated, may hold values from -1.5 to 1.5
Outputs:
- grad_tokens: bfloat16 [2, 24, 3072, 384], P(None, 'lat', 'lon')
- grad_qkv: bfloat16 [384, 1152], replicated
- grad_proj: bfloat16 [384, 384], replicated
- grad_gain: float32 [384], replicated
- grad_shift: float32 [384], replicated
- grad_table: bfloat16 [4, 12, 3312], replicated
The draws below stay inside these ranges and needn't reach their ends.
All inputs are finite; a program needn't handle non-finite values.
Results may differ from the reference program's by a relative error of at most 0.0089.
Values may be sent and summed in bfloat16 or wider, within the bound.
A program may use at most 128 MiB of HBM per device.

```python
import jax
import jax.numpy as jnp
from jax import lax

C = 384
HEADS = 12
WPL = 2
WLAT = 6
WLON = 12
PL = 2
NLON = 96
COLUMNS = 3072
NLAT = 24
BANDS = 4
TYPES = 4
POS = 3312


def draw_cotangent(key, part):
    key = jax.random.fold_in(key, 7)
    key_base, key_rows = jax.random.split(key, 2)
    shape = (PL, NLAT, COLUMNS, C)
    along = 1.0 + 2.0 * jnp.arange(COLUMNS, dtype=jnp.float32) / (COLUMNS - 1)
    row_scale = jnp.exp(jax.random.uniform(key_rows, (PL, NLAT, 1, 1), jnp.float32, -1.15, 1.15))
    base = jnp.clip(jax.random.normal(key_base, shape, jnp.float32), -4.0, 4.0)
    return (base * row_scale * along[None, None, :, None]).astype(jnp.bfloat16)


def with_ends(array, stream_key, smallest, largest):
    longest = array.shape.index(max(array.shape))
    spots = []
    for shift in (0, 1):
        where = [jax.random.randint(jax.random.fold_in(stream_key, axis), (), 0, length) for axis, length in enumerate(array.shape)]
        where[longest] = (where[longest] + shift) % array.shape[longest]
        spots.append(tuple(where))
    return array.at[spots[0]].set(smallest).at[spots[1]].set(largest)


def levels(key, extent, cuts, least, top_value):
    loudness = 1.0
    for dim, blocks in cuts:
        steps = jax.random.uniform(jax.random.fold_in(jax.random.fold_in(key, 6), dim), (blocks,), jnp.float32, least / len(cuts), top_value / len(cuts))
        loudness = loudness * jnp.repeat(jnp.exp(steps), extent[dim] // blocks).reshape((-1,) + (1,) * (len(extent) - 1 - dim))
    return loudness


def gaussian(own_key, dims, scale, most, shards=(), kind=jnp.bfloat16):
    values = jax.random.normal(own_key, dims, jnp.float32) * scale
    if len(shards) > 0:
        values = levels(own_key, dims, shards, -0.22, 0.18) * values
    return jnp.clip(values, min=-most, max=most).astype(kind)


def setup_inputs(seed: int = 0) -> dict:
    streams_of = jax.random.split(jax.random.key(seed), 10)
    tokens = gaussian(streams_of[0], (PL, NLAT, COLUMNS, C), 1.0, 6.0, ((1, 4), (2, 64)))
    cotangent = draw_cotangent(jax.random.fold_in(streams_of[9], 71), 0)
    mask_ids = with_ends(jax.random.randint(streams_of[2], (PL, NLAT), 0, 2), jax.random.fold_in(streams_of[2], 1), 0, 1).astype(jnp.int32)
    band_type = jax.random.permutation(streams_of[3], BANDS).astype(jnp.int32)
    bias_table = gaussian(streams_of[4], (TYPES, HEADS, POS), 0.5, 4.0)
    w_qkv = gaussian(streams_of[5], (C, 3 * C), C ** -0.5, 0.3125)
    w_proj = gaussian(streams_of[6], (C, C), C ** -0.5, 0.3125)
    ln_gain = jnp.clip(1.0 + 0.1 * jax.random.normal(streams_of[7], (C,), jnp.float32), 0.5, 1.5)
    ln_shift = gaussian(streams_of[8], (C,), 0.3, 1.5, (), jnp.float32)
    return dict(tokens=tokens, cotangent=cotangent, mask_ids=mask_ids, band_type=band_type, bias_table=bias_table, w_qkv=w_qkv, w_proj=w_proj, ln_gain=ln_gain, ln_shift=ln_shift)


EPSILON = 1e-05

def offset_table():
    spread = 2 * WLON - 1
    first = jnp.arange(WLON, dtype=jnp.int32)
    pairs = (first[:, None] - first[None, :] + WLON - 1).reshape(-1)
    return (jnp.arange(spread, dtype=jnp.int32)[:, None] == pairs[None, :]).astype(jnp.float32)

def expand_bias(bias_rows):
    outer = bias_rows.shape[:3]
    grouped = bias_rows.reshape(outer + (WPL * WPL * WLAT * WLAT, 2 * WLON - 1))
    spread_out = jnp.einsum('pahsd,de->pahse', grouped, offset_table(), precision=lax.Precision.HIGHEST)
    spread_out = spread_out.reshape(outer + (WPL, WPL, WLAT, WLAT, WLON, WLON))
    spread_out = spread_out.transpose(0, 1, 2, 3, 5, 7, 4, 6, 8)
    window = WPL * WLAT * WLON
    return spread_out.reshape(outer + (window, window))

def fold_bias(d_bias):
    outer = d_bias.shape[:3]
    split_up = d_bias.reshape(outer + (WPL, WLAT, WLON, WPL, WLAT, WLON)).transpose(0, 1, 2, 3, 6, 4, 7, 5, 8)
    split_up = split_up.reshape(outer + (WPL * WPL * WLAT * WLAT, WLON * WLON))
    folded = jnp.einsum('pahse,de->pahsd', split_up, offset_table(), precision=lax.Precision.HIGHEST)
    return folded.reshape(outer + (-1,))

def to_windows(grid):
    planes, lat_rows, lon_cols, channels = grid.shape
    split_up = grid.reshape(planes // WPL, WPL, lat_rows // WLAT, WLAT, lon_cols // WLON, WLON, channels)
    split_up = split_up.transpose(0, 2, 4, 1, 3, 5, 6)
    return split_up.reshape(planes // WPL, lat_rows // WLAT, lon_cols // WLON, WPL * WLAT * WLON, channels)

def from_windows(windows, planes, lat_rows, lon_cols):
    channels = windows.shape[-1]
    split_up = windows.reshape(planes // WPL, lat_rows // WLAT, lon_cols // WLON, WPL, WLAT, WLON, channels)
    return split_up.transpose(0, 3, 1, 4, 2, 5, 6).reshape(planes, lat_rows, lon_cols, channels)

def batched(form, left, right):
    return jnp.einsum(form, left.astype(jnp.float32), right.astype(jnp.float32))

def roll_samples(grid, offsets):
    planes, lat_rows, lon_cols, channels = grid.shape
    split_up = grid.reshape(planes, lat_rows, lon_cols // NLON, NLON, channels)
    rolled = jnp.roll(split_up, offsets, (0, 1, 3))
    return rolled.reshape(planes, lat_rows, lon_cols, channels)

def block_backward(shifted, shifted_cot, region_ids, bias_rows, w_qkv, w_proj, ln_gain, ln_shift):
    planes, lat_rows, lon_cols, channels = shifted.shape
    head_count = bias_rows.shape[2]
    head_dim = channels // head_count
    window = WPL * WLAT * WLON
    score_scale = head_dim ** (-0.5)
    flat_in = shifted.reshape(-1, channels).astype(jnp.float32)
    average = lax.optimization_barrier(jnp.mean(flat_in, axis=1, keepdims=True))
    centred = flat_in - average
    variance = lax.optimization_barrier(jnp.mean(centred * centred, axis=1, keepdims=True))
    inv_std = lax.rsqrt(variance + EPSILON)
    normed = centred * inv_std
    ln_out = (normed * ln_gain + ln_shift).astype(jnp.bfloat16)
    qkv = jnp.dot(ln_out, w_qkv, preferred_element_type=jnp.float32).astype(jnp.bfloat16)
    qkv_win = to_windows(qkv.reshape(planes, lat_rows, lon_cols, 3 * channels))
    lead = qkv_win.shape[:3]
    queries = qkv_win[..., :channels].reshape(lead + (window, head_count, head_dim))
    keys = qkv_win[..., channels:2 * channels].reshape(lead + (window, head_count, head_dim))
    values = qkv_win[..., 2 * channels:].reshape(lead + (window, head_count, head_dim))
    bias = expand_bias(bias_rows)
    ids_grid = region_ids.reshape(planes // WPL, WPL, lat_rows // WLAT, WLAT).transpose(0, 2, 1, 3)
    ids_win = jnp.broadcast_to(ids_grid[..., None], ids_grid.shape + (WLON,)).reshape(planes // WPL, lat_rows // WLAT, window)
    allowed = (ids_win[:, :, :, None] == ids_win[:, :, None, :])[:, :, None, None]
    scores = batched('pawqhd,pawkhd->pawhqk', queries, keys) * score_scale + bias[:, :, None]
    raised = jnp.where(allowed, jnp.exp(scores), 0.0)
    probs = raised / lax.optimization_barrier(jnp.sum(raised, axis=-1, keepdims=True))
    probs_b = probs.astype(jnp.bfloat16)
    attended = batched('pawhqk,pawkhd->pawqhd', probs_b, values).astype(jnp.bfloat16)
    attended = attended.reshape(-1, channels)
    cot_win = to_windows(shifted_cot)
    cot_flat = cot_win.reshape(-1, channels)
    grad_proj = lax.dot_general(attended, cot_flat, (((0,), (0,)), ((), ())), preferred_element_type=jnp.float32)
    d_attended = lax.dot_general(cot_flat, w_proj, (((1,), (1,)), ((), ())), preferred_element_type=jnp.float32)
    d_attended = d_attended.astype(jnp.bfloat16).reshape(lead + (window, head_count, head_dim))
    d_probs = batched('pawqhd,pawkhd->pawhqk', d_attended, values)
    d_values = batched('pawhqk,pawqhd->pawkhd', probs_b, d_attended)
    d_scores = probs * (d_probs - lax.optimization_barrier(jnp.sum(probs * d_probs, axis=-1, keepdims=True)))
    d_scores_b = d_scores.astype(jnp.bfloat16)
    d_queries = batched('pawhqk,pawkhd->pawqhd', d_scores_b, keys) * score_scale
    d_keys = batched('pawhqk,pawqhd->pawkhd', d_scores_b, queries) * score_scale
    d_qkv_win = jnp.concatenate([d_queries.reshape(lead + (window, channels)), d_keys.reshape(lead + (window, channels)), d_values.reshape(lead + (window, channels))], axis=-1).astype(jnp.bfloat16)
    d_qkv = from_windows(d_qkv_win, planes, lat_rows, lon_cols).reshape(-1, 3 * channels)
    grad_qkv = lax.dot_general(ln_out, d_qkv, (((0,), (0,)), ((), ())), preferred_element_type=jnp.float32)
    d_ln = lax.dot_general(d_qkv, w_qkv, (((1,), (1,)), ((), ())), preferred_element_type=jnp.float32)
    grad_gain = lax.optimization_barrier(jnp.sum(d_ln * normed, axis=0))
    grad_shift = lax.optimization_barrier(jnp.sum(d_ln, axis=0))
    scaled = d_ln * ln_gain
    d_flat = inv_std * (scaled - lax.optimization_barrier(jnp.mean(scaled, axis=1, keepdims=True)) - normed * lax.optimization_barrier(jnp.mean(scaled * normed, axis=1, keepdims=True)))
    d_shifted = d_flat.astype(jnp.bfloat16).reshape(planes, lat_rows, lon_cols, channels)
    d_rows = fold_bias(lax.optimization_barrier(jnp.sum(d_scores, axis=2)))
    return (d_shifted, grad_qkv, grad_proj, grad_gain, grad_shift, d_rows)

def reference(tokens, cotangent, mask_ids, band_type, bias_table, w_qkv, w_proj, ln_gain, ln_shift):
    offsets = (-(WPL // 2), -(WLAT // 2), -(WLON // 2))
    shifted = roll_samples(tokens, offsets)
    shifted_cot = roll_samples(cotangent, offsets)
    level_bands = PL // WPL
    type_ids = band_type[None, :] * level_bands + jnp.arange(level_bands, dtype=jnp.int32)[:, None]
    bias_rows = bias_table[type_ids].astype(jnp.float32)
    channels = tokens.shape[-1]
    head_count = bias_table.shape[1]
    block_count = tokens.shape[2] // WLON

    def one_block(carry, block_index):
        start = (block_index * WLON).astype(jnp.int32)
        piece = lax.dynamic_slice_in_dim(shifted, start, WLON, 2)
        cot_piece = lax.dynamic_slice_in_dim(shifted_cot, start, WLON, 2)
        d_piece, g_qkv, g_proj, g_gain, g_shift, g_rows = block_backward(piece, cot_piece, mask_ids, bias_rows, w_qkv, w_proj, ln_gain, ln_shift)
        updated = (carry[0] + g_qkv, carry[1] + g_proj, carry[2] + g_gain, carry[3] + g_shift, carry[4] + g_rows)
        return (updated, d_piece)
    start_sums = (jnp.zeros((channels, 3 * channels), jnp.float32), jnp.zeros((channels, channels), jnp.float32), jnp.zeros((channels,), jnp.float32), jnp.zeros((channels,), jnp.float32), jnp.zeros(bias_rows.shape, jnp.float32))
    sums, pieces = lax.scan(one_block, start_sums, jnp.arange(block_count, dtype=jnp.int32))
    d_shifted = pieces.transpose(1, 2, 0, 3, 4).reshape(tokens.shape)
    back = roll_samples(d_shifted, (WPL // 2, WLAT // 2, WLON // 2))
    grad_tokens = (cotangent.astype(jnp.float32) + back.astype(jnp.float32)).astype(jnp.bfloat16)
    grad_table = jnp.zeros(bias_table.shape, jnp.float32).at[type_ids.reshape(-1)].add(sums[4].reshape(-1, head_count, bias_table.shape[2]))
    return (grad_tokens, sums[0].astype(jnp.bfloat16), sums[1].astype(jnp.bfloat16), sums[2], sums[3], grad_table.astype(jnp.bfloat16))
```

```python
import jax
import jax.numpy as jnp
import numpy as np
from jax import lax
from jax.experimental import pallas as pl
from jax.experimental.pallas import tpu as pltpu
from jax.sharding import PartitionSpec as P

WPL, WLAT, WLON = 2, 6, 12
WINDOW = WPL * WLAT * WLON
ROWS = WPL * WLAT
SPREAD = 2 * WLON - 1
EDGE = 16
GROUP = 4
EPSILON = 1e-05
LOG2E = 1.4426950408889634
BF = jnp.bfloat16
F32 = jnp.float32


def token_route(lon_cols):
    half_lat, half_lon = WLAT // 2, WLON // 2
    windows = lon_cols // WLON
    near = WPL * half_lat * lon_cols
    far = WPL * half_lat * EDGE
    route = np.zeros((windows * WINDOW, 2 * near + 2 * far), np.float32)
    for w in range(windows):
        for o in range(WLON):
            for l in range(WPL):
                for a in range(WLAT):
                    level = (l + 1) % WPL
                    col = w * WLON + o + half_lon
                    row = level * half_lat + a % half_lat
                    if col < lon_cols:
                        source = row * lon_cols + col + (near if a >= half_lat else 0)
                    else:
                        source = 2 * near + row * EDGE + col - lon_cols
                        source += far if a >= half_lat else 0
                    route[w * WINDOW + o * ROWS + l * WLAT + a, source] = 1.0
    return route


def head_order():
    perm = np.zeros((GROUP * WINDOW, GROUP * WINDOW), np.float32)
    for o in range(WLON):
        for h in range(GROUP):
            for r in range(ROWS):
                perm[(o * GROUP + h) * ROWS + r, (h * WLON + o) * ROWS + r] = 1.0
    return perm


def table_order():
    order = np.zeros((SPREAD * ROWS, ROWS * SPREAD), np.float32)
    for d in range(SPREAD):
        for r in range(ROWS):
            order[(SPREAD - 1 - d) * ROWS + r, r * SPREAD + d] = 1.0
    return order


def head_blocks(head_dim):
    rows = np.arange(GROUP * head_dim)[:, None] // head_dim
    cols = np.arange(GROUP * WINDOW)[None, :] // WINDOW
    return (rows == cols).astype(np.float32)


def gather_heads():
    return np.tile(np.eye(WINDOW, dtype=np.float32), (1, GROUP))


def nn(a, b):
    return lax.dot_general(a, b, (((1,), (0,)), ((), ())), preferred_element_type=F32)


def nt(a, b):
    return lax.dot_general(a, b, (((1,), (1,)), ((), ())), preferred_element_type=F32)


def tn(a, b):
    return lax.dot_general(a, b, (((0,), (0,)), ((), ())), preferred_element_type=F32)


def block_kernel(
    ids, near_x, near_c, lat_x, lat_c, lon_x, lon_c, dia_x, dia_c, route, unroute, perm, order, blocks, gather,
    table, w_qkv, w_proj, gain, shift,
    d_cat, g_weights, g_table, g_small,
    cat, normed, inv, ln, cot, qkv, d_att, att, d_qkv, bias, d_bias, folded,
):
    half_lat = WLAT // 2
    lon_cols = near_x.shape[2]
    channels = near_x.shape[3]
    near = WPL * half_lat * lon_cols
    far = WPL * half_lat * EDGE
    groups = channels // 128
    windows = lon_cols // WLON
    span = GROUP * WINDOW
    head_dim = 128 // GROUP
    scale = head_dim ** -0.5

    lane = lax.rem(lax.broadcasted_iota(jnp.int32, (1, span), 1), ROWS)
    sub = lax.rem(lax.broadcasted_iota(jnp.int32, (WINDOW, 1), 0), ROWS)
    id_q = jnp.zeros((1, span), jnp.int32)
    id_k = jnp.zeros((WINDOW, 1), jnp.int32)
    for l in range(WPL):
        for a in range(WLAT):
            value = ids[l, a]
            id_q = jnp.where(lane == l * WLAT + a, value, id_q)
            id_k = jnp.where(sub == l * WLAT + a, value, id_k)
    masked = jnp.where(id_k == id_q, 0.0, -1e30)
    folded[...] = nt(order[...], table[...])
    for g in range(groups):
        pieces = [
            folded[(WLON - 1 - o) * ROWS : (WLON - 1 - o) * ROWS + WINDOW, g * GROUP * ROWS : (g + 1) * GROUP * ROWS]
            for o in range(WLON)
        ]
        spread = jnp.concatenate(pieces, axis=1).astype(BF)
        bias[g] = nn(spread, perm[...]) * LOG2E + masked
    d_bias[...] = jnp.zeros_like(d_bias)

    for source, x, c in ((0, near_x, near_c),):
        for l in range(WPL):
            rows = pl.ds(l * half_lat * lon_cols, half_lat * lon_cols)
            cat[rows, :channels] = x[l, half_lat:].reshape(half_lat * lon_cols, channels)
            cat[rows, channels:] = c[l, half_lat:].reshape(half_lat * lon_cols, channels)
    for start, size, x, c in (
        (near, near, lat_x, lat_c), (2 * near, far, lon_x, lon_c), (2 * near + far, far, dia_x, dia_c)
    ):
        cat[start : start + size, :channels] = x[...].reshape(size, channels)
        cat[start : start + size, channels:] = c[...].reshape(size, channels)
    moved = nn(route[...], cat[...])
    x = moved[:, :channels]
    cot[...] = moved[:, channels:].astype(BF)
    average = jnp.mean(x, axis=1, keepdims=True)
    centred = x - average
    variance = jnp.mean(centred * centred, axis=1, keepdims=True)
    inv_std = lax.rsqrt(variance + EPSILON)
    inv[...] = inv_std
    norm = centred * inv_std
    normed[...] = norm
    ln[...] = (norm * gain[...] + shift[...]).astype(BF)
    qkv[...] = nn(ln[...], w_qkv[...]).astype(BF)
    d_att[...] = nt(cot[...], w_proj[...]).astype(BF)

    lanes = lax.broadcasted_iota(jnp.int32, (1, 128), 1) // head_dim
    own = [(lanes == h).astype(F32).astype(BF) for h in range(GROUP)]
    eye = (
        lax.broadcasted_iota(jnp.int32, (128, 128), 0) == lax.broadcasted_iota(jnp.int32, (128, 128), 1)
    ).astype(F32).astype(BF)

    def one_window(w, carry):
        rows = pl.ds(pl.multiple_of(w * WINDOW, WINDOW), WINDOW)
        for g in range(groups):
            cols = slice(g * 128, (g + 1) * 128)
            q = qkv[rows, g * 128 : (g + 1) * 128]
            k = qkv[rows, channels + g * 128 : channels + (g + 1) * 128]
            v = qkv[rows, 2 * channels + g * 128 : 2 * channels + (g + 1) * 128]
            da = d_att[rows, cols]
            q_heads = jnp.concatenate([q * own[h] for h in range(GROUP)], axis=0)
            da_heads = jnp.concatenate([da * own[h] for h in range(GROUP)], axis=0)
            raised = jnp.exp2(nt(k, q_heads) * (scale * LOG2E) + bias[g])
            probs = raised * (1.0 / jnp.sum(raised, axis=0, keepdims=True))
            probs_b = probs.astype(BF)
            v_t = nt(eye, v).astype(BF)
            k_t = nt(eye, k).astype(BF)
            d_probs = nt(v, da_heads)
            weighted = probs * d_probs
            d_scores = weighted - probs * jnp.sum(weighted, axis=0, keepdims=True)
            d_bias[g] += d_scores
            d_scores_b = d_scores.astype(BF)
            mask = blocks[...]
            att_t = nn(v_t, probs_b).astype(BF) * mask
            att[rows, cols] = nt(gather[...], att_t).astype(BF)
            dq_t = (nn(k_t, d_scores_b) * scale).astype(BF) * mask
            d_qkv[rows, g * 128 : (g + 1) * 128] = nt(gather[...], dq_t).astype(BF)
            d_qkv[rows, channels + g * 128 : channels + (g + 1) * 128] = (
                nn(d_scores_b, q_heads) * scale
            ).astype(BF)
            d_qkv[rows, 2 * channels + g * 128 : 2 * channels + (g + 1) * 128] = nn(probs_b, da_heads).astype(BF)
        return carry

    lax.fori_loop(0, windows, one_window, 0)

    for b in range(3):
        g_weights[b] = tn(ln[...], d_qkv[:, b * channels : (b + 1) * channels]).astype(BF)
    g_weights[3] = tn(att[...], cot[...]).astype(BF)
    d_ln = nt(d_qkv[...], w_qkv[...])
    norm = normed[...]
    g_small[...] = jnp.zeros_like(g_small)
    for g in range(groups):
        cols = slice(g * 128, (g + 1) * 128)
        g_small[g : g + 1] = jnp.sum(d_ln[:, cols] * norm[:, cols], axis=0, keepdims=True)
        g_small[groups + g : groups + g + 1] = jnp.sum(d_ln[:, cols], axis=0, keepdims=True)
    scaled = d_ln * gain[...]
    d_flat = inv[...] * (
        scaled
        - jnp.mean(scaled, axis=1, keepdims=True)
        - norm * jnp.mean(scaled * norm, axis=1, keepdims=True)
    )
    d_cat[...] = nn(unroute[...], d_flat.astype(BF)).astype(BF)

    folded[...] = jnp.zeros_like(folded)
    parts = []
    for g in range(groups):
        high = d_bias[g].astype(BF)
        low = (d_bias[g] - high.astype(F32)).astype(BF)
        parts.append(nt(high, perm[...]) + nt(low, perm[...]))
    for o in range(WLON):
        piece = jnp.concatenate([p[:, o * GROUP * ROWS : (o + 1) * GROUP * ROWS] for p in parts], axis=1)
        folded[(WLON - 1 - o) * ROWS : (WLON - 1 - o) * ROWS + WINDOW, :] += piece
    high = folded[...].astype(BF)
    low = (folded[...] - high.astype(F32)).astype(BF)
    rows = tn(high, order[...]) + tn(low, order[...])
    tail = rows[:, 256:]
    g_table[...] = jnp.concatenate(
        [
            rows[:, :128],
            rows[:, 128:256],
            jnp.concatenate([tail, jnp.zeros((tail.shape[0], 128 - tail.shape[1]), F32)], axis=1),
            jnp.zeros((PLANE * PART - 3 * rows.shape[0], 128), F32),
        ],
        axis=0,
    ).astype(BF)


def block_backward(ids, pieces, rows, w_qkv, w_proj, gain, shift):
    lon_cols, channels = pieces[0].shape[2:]
    tokens = WPL * WLAT * lon_cols
    near = WPL * (WLAT // 2) * lon_cols
    far = WPL * (WLAT // 2) * EDGE
    groups = channels // 128
    span = GROUP * WINDOW
    route = token_route(lon_cols)
    constants = [
        jnp.asarray(c, BF)
        for c in (route, route.T, head_order(), table_order(), head_blocks(128 // GROUP), gather_heads())
    ]
    vmem = pl.BlockSpec(memory_space=pltpu.VMEM)
    arrays = [*pieces, *constants, rows, w_qkv, w_proj, gain[None], shift[None]]
    return pl.pallas_call(
        block_kernel,
        out_shape=(
            jax.ShapeDtypeStruct((2 * near + 2 * far, channels), BF),
            jax.ShapeDtypeStruct((4, channels, channels), BF),
            jax.ShapeDtypeStruct((PLANE * PART, 128), BF),
            jax.ShapeDtypeStruct((8, 128), F32),
        ),
        in_specs=[pl.BlockSpec(memory_space=pltpu.SMEM)] + [vmem] * len(arrays),
        out_specs=(vmem,) * 4,
        scratch_shapes=[
            pltpu.VMEM((2 * near + 2 * far, 2 * channels), BF),
            pltpu.VMEM((tokens, channels), F32),
            pltpu.VMEM((tokens, 1), F32),
            pltpu.VMEM((tokens, channels), BF),
            pltpu.VMEM((tokens, channels), BF),
            pltpu.VMEM((tokens, 3 * channels), BF),
            pltpu.VMEM((tokens, channels), BF),
            pltpu.VMEM((tokens, channels), BF),
            pltpu.VMEM((tokens, 3 * channels), BF),
            pltpu.VMEM((groups, WINDOW, span), F32),
            pltpu.VMEM((groups, WINDOW, span), F32),
            pltpu.VMEM((SPREAD * ROWS, groups * GROUP * ROWS), F32),
        ],
        compiler_params=pltpu.CompilerParams(vmem_limit_bytes=56 * 1024 * 1024),
        cost_estimate=pl.CostEstimate(flops=6_000_000_000, bytes_accessed=10_000_000, transcendentals=1_000_000),
    )(ids, *arrays)


X_SIZE, Z_SIZE = 4, 8
PLANE = 16
USED = 7
CHUNK = 48
WEIGHT = 3 * CHUNK
PART = 32
SMALL = 16
MESH = pl.DeviceIdType.MESH


def place():
    lon = lax.axis_index("lon")
    lat = lax.axis_index("lat")
    x = lax.rem(lon, X_SIZE)
    z = lax.rem(lon // X_SIZE, Z_SIZE)
    y_lo = lon // (X_SIZE * Z_SIZE)
    y_hi = lat // 2
    core = lax.rem(lat, 2)
    return x, y_lo, y_hi, z, core


def device(plane, z, core):
    x = lax.rem(plane, X_SIZE)
    y_lo = lax.rem(plane // X_SIZE, 2)
    y_hi = plane // (2 * X_SIZE)
    return ((y_lo * Z_SIZE + z) * X_SIZE + x, y_hi * 2 + core)


def split_small(value):
    high = value.astype(BF).astype(F32)
    return jnp.concatenate([high, value - high], axis=0).astype(BF)


def reduce_kernel(
    weights, table, small,
    o_qkv, o_proj, o_table, o_small,
    small_out, core_in, small_in, plane_out, plane_in, total, z_out, z_in, z_full, full,
    core_s, core_r, small_s, small_r, plane_s, plane_r, z_s, z_r, zg_s, zg_r, pg_s, pg_r, sib_s, sib_r,
):
    x, y_lo, y_hi, z, core = place()
    me = (y_hi * 2 + y_lo) * X_SIZE + x
    sibling = device(me, z, 1 - core)
    barrier = pltpu.get_barrier_semaphore()

    def greet(target):
        pl.semaphore_signal(barrier, inc=1, device_id=target, device_id_type=MESH)

    def greet_plane(i, carry):
        greet(device(lax.rem(me + i, PLANE), z, core))
        return carry

    def greet_line(i, carry):
        greet(device(me, lax.rem(z + i, Z_SIZE), core))
        return carry

    greet(sibling)
    lax.fori_loop(1, PLANE, greet_plane, 0)
    lax.fori_loop(1, Z_SIZE, greet_line, 0)
    small_out[...] = split_small(small[...])
    pl.semaphore_wait(barrier, PLANE + Z_SIZE - 1)

    def remote(src, dst, send, recv, target):
        return pltpu.make_async_remote_copy(
            src_ref=src, dst_ref=dst, send_sem=send, recv_sem=recv, device_id=target, device_id_type=MESH
        )

    small_copy = remote(small_out, small_in, small_s.at[0], small_r.at[0], sibling)
    core_copies = [
        remote(weights.at[2 * (1 - core) + b], core_in.at[b], core_s.at[b], core_r.at[b], sibling) for b in range(2)
    ]
    for copy in core_copies:
        copy.start()
    small_copy.start()

    def plane_copy(peer):
        return remote(
            plane_out.at[peer], plane_in.at[me], plane_s.at[peer], plane_r.at[me], device(peer, z, core)
        )

    small_copy.wait()
    both = small_out[...].astype(F32) + small_in[...].astype(F32)
    small_core = split_small(both[:8] + both[8:])

    for b in range(2):
        core_copies[b].wait()

        def fill(i, carry):
            peer = b * 8 + i
            rows = pl.ds(pl.multiple_of(i * CHUNK, CHUNK), CHUNK)
            for t in range(3):
                lanes = slice(t * 128, (t + 1) * 128)
                added = weights[2 * core + b, rows, lanes].astype(F32) + core_in[b, rows, lanes].astype(F32)
                plane_out[peer, t * CHUNK : (t + 1) * CHUNK] = added.astype(BF)
            plane_out[peer, WEIGHT : WEIGHT + PART] = table[pl.ds(pl.multiple_of(peer * PART, PART), PART)]
            plane_out[peer, WEIGHT + PART :] = small_core

            @pl.when(peer != me)
            def _():
                plane_copy(peer).start()

            return carry

        lax.fori_loop(0, 8, fill, 0)

    total[...] = jnp.zeros_like(total)

    def add(part, source):
        total[:WEIGHT] += part[:WEIGHT].astype(F32)
        hi = source // (2 * X_SIZE)
        rows = pl.ds(pl.multiple_of(WEIGHT + hi * PART, PART // 2), PART)
        total[rows] += part[WEIGHT : WEIGHT + PART].astype(F32)
        total[8 * PART :] += part[WEIGHT + PART :].astype(F32)

    add(plane_out[me], me)

    def collect(i, carry):
        source = lax.rem(me + i, PLANE)
        remote(
            plane_out.at[source], plane_in.at[source], plane_s.at[source], plane_r.at[source], device(source, z, core)
        ).wait_recv()
        add(plane_in[source], source)
        return carry

    lax.fori_loop(1, PLANE, collect, 0)

    summed = total[8 * PART :]
    small_plane = split_small(summed[:8] + summed[8:])

    def z_copy(peer):
        return remote(z_out.at[peer], z_in.at[z], z_s.at[peer], z_r.at[z], device(me, peer, core))

    def fill_line(i, carry):
        peer = lax.rem(z + i, Z_SIZE)
        z_out[peer, :PART] = total[pl.ds(pl.multiple_of(peer * PART, PART), PART)].astype(BF)
        z_out[peer, PART:] = small_plane
        z_copy(peer).start()
        return carry

    lax.fori_loop(1, Z_SIZE, fill_line, 0)
    own = total[pl.ds(pl.multiple_of(z * PART, PART), PART)]
    own_small = small_plane.astype(F32)

    def collect_line(i, carry):
        part, little = carry
        source = lax.rem(z + i, Z_SIZE)
        remote(
            z_out.at[source], z_in.at[source], z_s.at[source], z_r.at[source], device(me, source, core)
        ).wait_recv()
        return part + z_in[source, :PART].astype(F32), little + z_in[source, PART:].astype(F32)

    own, own_small = lax.fori_loop(1, Z_SIZE, collect_line, (own, own_small))
    o_small[...] = own_small[:8] + own_small[8:]

    z_full[z] = own.astype(BF)

    def zg_copy(peer):
        return remote(z_full.at[z], z_full.at[z], zg_s.at[peer], zg_r.at[z], device(me, peer, core))

    def send_line(i, carry):
        zg_copy(lax.rem(z + i, Z_SIZE)).start()
        return carry

    lax.fori_loop(1, Z_SIZE, send_line, 0)

    def take_line(i, carry):
        source = lax.rem(z + i, Z_SIZE)
        remote(
            z_full.at[source], z_full.at[source], zg_s.at[source], zg_r.at[source], device(me, source, core)
        ).wait_recv()
        return carry

    lax.fori_loop(1, Z_SIZE, take_line, 0)
    full[core, me] = z_full[:USED]

    def pg_copy(peer):
        return remote(full.at[core, me], full.at[core, me], pg_s.at[peer], pg_r.at[me], device(peer, z, core))

    def sib_copy(source):
        return remote(full.at[core, source], full.at[core, source], sib_s.at[source], sib_r.at[source], sibling)

    def send_plane(i, carry):
        pg_copy(lax.rem(me + i, PLANE)).start()
        return carry

    lax.fori_loop(1, PLANE, send_plane, 0)
    sib_copy(me).start()

    def take_plane(i, carry):
        source = lax.rem(me + i, PLANE)
        remote(
            full.at[core, source], full.at[core, source], pg_s.at[source], pg_r.at[source], device(source, z, core)
        ).wait_recv()
        sib_copy(source).start()
        return carry

    lax.fori_loop(1, PLANE, take_plane, 0)

    def take_sibling(source, carry):
        remote(
            full.at[1 - core, source], full.at[1 - core, source], sib_s.at[source], sib_r.at[source], sibling
        ).wait_recv()
        return carry

    lax.fori_loop(0, PLANE, take_sibling, 0)

    def write(i, carry):
        rows = pl.ds(pl.multiple_of(i * CHUNK, CHUNK), CHUNK)
        for half in range(2):
            for b in range(2):
                block = 2 * half + b
                part = full[half, b * 8 + i].reshape(USED * PART, 128)
                for t in range(3):
                    lanes = slice((block % 3) * 384 + t * 128, (block % 3) * 384 + (t + 1) * 128)
                    target = o_qkv if block < 3 else o_proj
                    target[rows, lanes] = part[t * CHUNK : (t + 1) * CHUNK]
        return carry

    lax.fori_loop(0, 8, write, 0)

    def write_table(i, carry):
        rows = pl.ds(pl.multiple_of(i * PART, PART), PART)
        for hi in range(2):
            for half in range(2):
                part = full[half, i].reshape(USED * PART, 128)
                o_table[hi * 2 + half, rows] = part[WEIGHT + hi * PART : WEIGHT + (hi + 1) * PART]
        return carry

    lax.fori_loop(0, PLANE, write_table, 0)

    def drain_plane(i, carry):
        peer = lax.rem(me + i, PLANE)
        plane_copy(peer).wait_send()
        pg_copy(peer).wait_send()
        return carry

    def drain_line(i, carry):
        peer = lax.rem(z + i, Z_SIZE)
        z_copy(peer).wait_send()
        zg_copy(peer).wait_send()
        return carry

    def drain_sibling(source, carry):
        sib_copy(source).wait_send()
        return carry

    lax.fori_loop(1, PLANE, drain_plane, 0)
    lax.fori_loop(1, Z_SIZE, drain_line, 0)
    lax.fori_loop(0, PLANE, drain_sibling, 0)


def reduce_all(weights, table, small):
    vmem = pl.BlockSpec(memory_space=pltpu.VMEM)
    dma = pltpu.SemaphoreType.DMA
    return pl.pallas_call(
        reduce_kernel,
        out_shape=(
            jax.ShapeDtypeStruct((384, 1152), BF),
            jax.ShapeDtypeStruct((384, 384), BF),
            jax.ShapeDtypeStruct((4, PLANE * PART, 128), BF),
            jax.ShapeDtypeStruct((8, 128), F32),
        ),
        in_specs=[vmem] * 3,
        out_specs=(vmem,) * 4,
        scratch_shapes=[
            pltpu.VMEM((SMALL, 128), BF),
            pltpu.VMEM((2, 384, 384), BF),
            pltpu.VMEM((SMALL, 128), BF),
            pltpu.VMEM((PLANE, WEIGHT + PART + SMALL, 128), BF),
            pltpu.VMEM((PLANE, WEIGHT + PART + SMALL, 128), BF),
            pltpu.VMEM((Z_SIZE * PART + SMALL, 128), F32),
            pltpu.VMEM((Z_SIZE, PART + SMALL, 128), BF),
            pltpu.VMEM((Z_SIZE, PART + SMALL, 128), BF),
            pltpu.VMEM((Z_SIZE, PART, 128), BF),
            pltpu.VMEM((2, PLANE, USED, PART, 128), BF),
            dma((2,)), dma((2,)), dma((1,)), dma((1,)),
            dma((PLANE,)), dma((PLANE,)), dma((Z_SIZE,)), dma((Z_SIZE,)),
            dma((Z_SIZE,)), dma((Z_SIZE,)), dma((PLANE,)), dma((PLANE,)),
            dma((PLANE,)), dma((PLANE,)),
        ],
        compiler_params=pltpu.CompilerParams(
            collective_id=0, has_side_effects=True, vmem_limit_bytes=40 * 1024 * 1024
        ),
    )(weights, table, small)


def table_rows(table):
    heads = table.shape[0]
    split = table.reshape(heads, WPL, WPL, WLAT, WLAT * SPREAD).transpose(0, 1, 3, 2, 4)
    return split.reshape(heads * ROWS, ROWS * SPREAD)


def table_back(rows):
    heads = rows.shape[-2] // ROWS
    outer = rows.shape[:-2]
    split = rows.reshape(outer + (heads, WPL, WLAT, WPL, WLAT * SPREAD))
    split = jnp.swapaxes(split, -3, -2)
    return split.reshape(outer + (heads, -1))


def to_partner(value):
    count = lax.axis_size("lon")
    return lax.ppermute(value, "lon", [(source, source ^ 1) for source in range(count)])


def to_lat(value, steps):
    count = lax.axis_size("lat")
    return lax.ppermute(value, "lat", [(source, (source + steps) % count) for source in range(count)])


def local(tokens, cotangent, mask_ids, band_type, bias_table, w_qkv, w_proj, ln_gain, ln_shift):
    half_lon, half_lat = WLON // 2, WLAT // 2
    lon_cols = tokens.shape[2]
    channels = tokens.shape[3]
    heads = bias_table.shape[1]
    stacked = jnp.stack([tokens, cotangent])
    from_lat = to_lat(stacked[:, :, :half_lat], -1)
    from_lon = to_partner(stacked[:, :, half_lat:, :EDGE])
    from_both = to_partner(from_lat[:, :, :, :EDGE])
    lat = lax.axis_index("lat")
    own_type = lax.dynamic_index_in_dim(band_type, lat, 0, False)
    rows = table_rows(lax.dynamic_index_in_dim(bias_table, own_type, 0, False))
    pieces = [
        tokens, cotangent, from_lat[0], from_lat[1], from_lon[0], from_lon[1], from_both[0], from_both[1]
    ]
    d_cat, weights, d_rows, small = block_backward(
        mask_ids, pieces, rows, w_qkv, w_proj, ln_gain, ln_shift
    )
    near = WPL * half_lat * lon_cols
    far = WPL * half_lat * EDGE
    own = d_cat[:near].reshape(WPL, half_lat, lon_cols, channels)
    for_lat = d_cat[near : 2 * near].reshape(WPL, half_lat, lon_cols, channels)
    for_lon = d_cat[2 * near : 2 * near + far].reshape(WPL, half_lat, EDGE, channels)
    for_both = d_cat[2 * near + far :].reshape(WPL, half_lat, EDGE, channels)
    back_lon = to_partner(for_lon)
    back_both = to_partner(for_both)
    edge = jnp.arange(lon_cols)[:, None] < half_lon

    def joined(inner, outer):
        wide = jnp.pad(outer, ((0, 0), (0, 0), (0, lon_cols - EDGE), (0, 0)))
        return jnp.where(edge, wide, inner)

    top = to_lat(joined(for_lat, back_both), 1)
    low = joined(own, back_lon)
    back = jnp.concatenate([top, low], axis=1)
    grad_tokens = (cotangent.astype(F32) + back.astype(F32)).astype(BF)
    g_qkv, g_proj, tables, g_small = reduce_all(weights, d_rows, small)
    slots = band_type[None, :] == jnp.arange(band_type.shape[0])[:, None]
    ordered = jnp.take(tables, jnp.argmax(slots, axis=1), axis=0)
    ordered = ordered[:, : 3 * heads * ROWS].reshape(-1, 3, heads * ROWS, 128).swapaxes(1, 2)
    g_table = ordered.reshape(-1, heads * ROWS, 384)[:, :, : ROWS * SPREAD]
    return (
        grad_tokens,
        g_qkv,
        g_proj,
        g_small[:3].reshape(-1),
        g_small[3:6].reshape(-1),
        table_back(g_table),
    )


def solution(mesh):
    placed = (P(None, "lat", "lon", None),) * 2 + (P(None, "lat"),) + (P(),) * 6
    return jax.shard_map(
        local,
        mesh=mesh,
        in_specs=placed,
        out_specs=(P(None, "lat", "lon", None), P(), P(), P(), P(), P()),
        check_vma=False,
    )
```

```python
import jax
import jax.numpy as jnp
import numpy as np
from jax import lax
from jax.experimental import pallas as pl
from jax.experimental.pallas import tpu as pltpu
from jax.sharding import PartitionSpec as P

WPL, WLAT, WLON = 2, 6, 12
WINDOW = WPL * WLAT * WLON
ROWS = WPL * WLAT
SPREAD = 2 * WLON - 1
EDGE = 16
X_SIZE, Y_SIZE, Z_SIZE = 4, 4, 8
PART = 192
PIECE = 48
SLOT = 16
MESH = pl.DeviceIdType.MESH
GROUP = 4
EPSILON = 1e-05
LOG2E = 1.4426950408889634
BF = jnp.bfloat16
F32 = jnp.float32


def token_route(lon_cols):
    half_lat, half_lon = WLAT // 2, WLON // 2
    windows = lon_cols // WLON
    near = WPL * half_lat * lon_cols
    far = WPL * half_lat * EDGE
    route = np.zeros((windows * WINDOW, 2 * near + 2 * far), np.float32)
    for w in range(windows):
        for o in range(WLON):
            for l in range(WPL):
                for a in range(WLAT):
                    level = (l + 1) % WPL
                    col = w * WLON + o + half_lon
                    row = level * half_lat + a % half_lat
                    if col < lon_cols:
                        source = row * lon_cols + col + (near if a >= half_lat else 0)
                    else:
                        source = 2 * near + row * EDGE + col - lon_cols
                        source += far if a >= half_lat else 0
                    route[w * WINDOW + o * ROWS + l * WLAT + a, source] = 1.0
    return route


def head_order():
    perm = np.zeros((GROUP * WINDOW, GROUP * WINDOW), np.float32)
    for o in range(WLON):
        for h in range(GROUP):
            for r in range(ROWS):
                perm[(o * GROUP + h) * ROWS + r, (h * WLON + o) * ROWS + r] = 1.0
    return perm


def table_order():
    order = np.zeros((SPREAD * ROWS, 512), np.float32)
    for d in range(SPREAD):
        for l in range(WPL):
            for a in range(WLAT):
                order[(SPREAD - 1 - d) * ROWS + l * WLAT + a, l * 256 + a * SPREAD + d] = 1.0
    return order


def row_order(heads):
    order = np.zeros((heads * ROWS, heads * ROWS), np.float32)
    for h in range(heads):
        for r in range(ROWS):
            order[r * heads + h, h * ROWS + r] = 1.0
    return order


def head_blocks(head_dim):
    rows = np.arange(GROUP * head_dim)[:, None] // head_dim
    cols = np.arange(GROUP * WINDOW)[None, :] // WINDOW
    return (rows == cols).astype(np.float32)


def gather_heads():
    return np.tile(np.eye(WINDOW, dtype=np.float32), (1, GROUP))


def nn(a, b):
    return lax.dot_general(a, b, (((1,), (0,)), ((), ())), preferred_element_type=F32)


def nt(a, b):
    return lax.dot_general(a, b, (((1,), (1,)), ((), ())), preferred_element_type=F32)


def tn(a, b):
    return lax.dot_general(a, b, (((0,), (0,)), ((), ())), preferred_element_type=F32)


def place():
    lon = lax.axis_index("lon")
    lat = lax.axis_index("lat")
    x = lax.rem(lon, X_SIZE)
    z = lax.rem(lon // X_SIZE, Z_SIZE)
    y = (lat // 2) * 2 + lon // (X_SIZE * Z_SIZE)
    return x, y, z, lax.rem(lat, 2)


def device(x, y, z, core):
    return ((lax.rem(y, 2) * Z_SIZE + z) * X_SIZE + x, (y // 2) * 2 + core)


def whole_kernel(
    ids, types, tokens, cotangent, table_h, w_qkv_h, w_proj_h, gain_v, shift_v,
    route_h, unroute_h, perm_h, order_h, blocks_h, gather_h, reorder_h,
    o_tokens, o_qkv, o_proj, o_table, o_gain, o_shift,
    cat, edge, cot_own, table, w_qkv, w_proj, route, unroute, perm, order, blocks, gather, reorder,
    tall, folded, bias, d_bias, normed, inv, ln, cot, qkv, d_att, att, d_qkv,
    d_main, d_edge, back_main, back_edge,
    grads, tables, core_in, s1_out, s1_in, s2_out, s2_in, z_in, full, small, small_core, small_x, small_y, small_z, wide,
    load_s, halo_s, halo_r, back_s, back_r, core_s, core_r, s1_s, s1_r, s2_s, s2_r, z_s, z_r, g2_s, g2_r, g1_s, g1_r,
    sib_s, sib_r, mc_s, mc_r, mx_s, mx_r, my_s, my_r, mz_s, mz_r,
):
    half_lat = WLAT // 2
    half_lon = WLON // 2
    lon_cols = tokens.shape[2]
    channels = tokens.shape[3]
    main = 2 * WPL * half_lat * lon_cols
    groups = channels // 128
    heads = groups * GROUP
    windows = lon_cols // WLON
    span = GROUP * WINDOW
    head_dim = 128 // GROUP
    scale = head_dim ** -0.5
    x, y, z, core = place()
    other = 1 - core
    beside = x + 1 - 2 * lax.rem(x, 2)
    across = lax.rem(y + 2, Y_SIZE)
    y_up = lax.rem(y + 2 * other, Y_SIZE)
    y_down = lax.rem(y + 2 * core, Y_SIZE)
    sibling = device(x, y, z, other)

    loads = [
        pltpu.make_async_copy(src, dst, load_s.at[i])
        for i, (src, dst) in enumerate((
            (table_h, table), (order_h, order), (reorder_h, reorder), (perm_h, perm),
            (tokens.at[:, pl.ds(half_lat, half_lat)], cat.at[0, :, :, :, pl.ds(0, channels)]),
            (cotangent.at[:, pl.ds(half_lat, half_lat)], cat.at[0, :, :, :, pl.ds(channels, channels)]),
            (route_h, route), (w_qkv_h, w_qkv), (w_proj_h, w_proj), (blocks_h, blocks), (gather_h, gather),
            (unroute_h, unroute), (cotangent, cot_own),
        ))
    ]
    for load in loads:
        load.start()

    barrier = pltpu.get_barrier_semaphore()
    friends = [sibling, device(x, across, z, other), device(beside, y, z, other), device(beside, across, z, other)]
    friends += [device(lax.rem(x + i, X_SIZE), y, z, core) for i in range(1, X_SIZE)]
    friends += [device(x, lax.rem(y + i, Y_SIZE), z, core) for i in range(1, Y_SIZE)]
    friends += [device(x, y, lax.rem(z + i, Z_SIZE), core) for i in range(1, Z_SIZE)]
    for friend in friends:
        pl.semaphore_signal(barrier, inc=1, device_id=friend, device_id_type=MESH)
    pl.semaphore_wait(barrier, len(friends))

    def remote(src, dst, send, recv, target):
        return pltpu.make_async_remote_copy(
            src_ref=src, dst_ref=dst, send_sem=send, recv_sem=recv, device_id=target, device_id_type=MESH
        )

    first, last = pl.ds(0, half_lat), pl.ds(half_lat, half_lat)
    halos = []
    for i, array in enumerate((tokens, cotangent)):
        lanes = pl.ds(i * channels, channels)
        up = device(x, y_up, z, other)
        halos += [
            (array.at[:, first], cat.at[1, :, :, :, lanes], up),
            (array.at[:, last, pl.ds(0, EDGE)], edge.at[0, :, :, :, lanes], device(beside, y, z, core)),
            (array.at[:, first, pl.ds(0, EDGE)], edge.at[1, :, :, :, lanes], device(beside, y_up, z, other)),
        ]
    halos = [remote(src, dst, halo_s.at[i], halo_r.at[i], to) for i, (src, dst, to) in enumerate(halos)]
    for copy in halos:
        copy.start()

    for load in loads[:4]:
        load.wait()
    own_type = types[lax.axis_index("lat")]
    rows_of_type = table[own_type].astype(F32)
    tall[...] = jnp.zeros_like(tall)
    for lq in range(WPL):
        for lk in range(WPL):
            for a in range(WLAT):
                start = ((lq * WPL + lk) * WLAT + a) * WLAT * SPREAD
                row = (lq * WLAT + a) * heads
                tall[row : row + heads, lk * 256 : lk * 256 + WLAT * SPREAD] = rows_of_type[:, start : start + WLAT * SPREAD]
    laid = nt(order[...], tall[...].astype(BF)).astype(BF)
    folded[...] = nn(laid, reorder[...])
    lane = lax.rem(lax.broadcasted_iota(jnp.int32, (1, span), 1), ROWS)
    sub = lax.rem(lax.broadcasted_iota(jnp.int32, (WINDOW, 1), 0), ROWS)
    id_q = jnp.zeros((1, span), jnp.int32)
    id_k = jnp.zeros((WINDOW, 1), jnp.int32)
    for l in range(WPL):
        for a in range(WLAT):
            value = ids[l, a]
            id_q = jnp.where(lane == l * WLAT + a, value, id_q)
            id_k = jnp.where(sub == l * WLAT + a, value, id_k)
    masked = jnp.where(id_k == id_q, 0.0, -1e30)
    for g in range(groups):
        pieces = [
            folded[(WLON - 1 - o) * ROWS : (WLON - 1 - o) * ROWS + WINDOW, g * GROUP * ROWS : (g + 1) * GROUP * ROWS]
            for o in range(WLON)
        ]
        spread = jnp.concatenate(pieces, axis=1).astype(BF)
        bias[g] = nn(spread, perm[...]) * LOG2E + masked

    gain = gain_v[...].reshape(1, channels)
    shift = shift_v[...].reshape(1, channels)
    for load in loads[4:]:
        load.wait()
    for copy in halos:
        copy.wait_recv()
    moved = nn(route[:, :main], cat[...].reshape(main, 2 * channels))
    moved = moved + nn(route[:, main:], edge[...].reshape(-1, 2 * channels))
    x_in = moved[:, :channels]
    cot[...] = moved[:, channels:].astype(BF)
    average = jnp.mean(x_in, axis=1, keepdims=True)
    centred = x_in - average
    variance = jnp.mean(centred * centred, axis=1, keepdims=True)
    inv_std = lax.rsqrt(variance + EPSILON)
    inv[...] = inv_std
    norm = centred * inv_std
    normed[...] = norm
    ln[...] = (norm * gain + shift).astype(BF)
    qkv[...] = nn(ln[...], w_qkv[...]).astype(BF)
    d_att[...] = nt(cot[...], w_proj[...]).astype(BF)

    lanes = lax.broadcasted_iota(jnp.int32, (1, 128), 1) // head_dim
    own = [(lanes == h).astype(F32).astype(BF) for h in range(GROUP)]
    eye = (
        lax.broadcasted_iota(jnp.int32, (128, 128), 0) == lax.broadcasted_iota(jnp.int32, (128, 128), 1)
    ).astype(F32).astype(BF)

    def attend(g, w):
        rows = pl.ds(pl.multiple_of(w * WINDOW, WINDOW), WINDOW)
        q_cols, k_cols, v_cols = (slice(b * channels + g * 128, b * channels + (g + 1) * 128) for b in range(3))
        cols = slice(g * 128, (g + 1) * 128)
        q, k, v, da = qkv[rows, q_cols], qkv[rows, k_cols], qkv[rows, v_cols], d_att[rows, cols]
        q_heads = jnp.concatenate([q * own[h] for h in range(GROUP)], axis=0)
        da_heads = jnp.concatenate([da * own[h] for h in range(GROUP)], axis=0)
        raised = jnp.exp2(nt(k, q_heads) * (scale * LOG2E) + bias[g])
        probs = raised * (1.0 / jnp.sum(raised, axis=0, keepdims=True))
        probs_b = probs.astype(BF)
        v_t = nt(eye, v).astype(BF)
        k_t = nt(eye, k).astype(BF)
        weighted = probs * nt(v, da_heads)
        d_scores = weighted - probs * jnp.sum(weighted, axis=0, keepdims=True)
        d_scores_b = d_scores.astype(BF)
        mask = blocks[...]
        att_t = nn(v_t, probs_b).astype(BF) * mask
        dq_t = (nn(k_t, d_scores_b) * scale).astype(BF) * mask

        def store():
            att[rows, cols] = nt(gather[...], att_t).astype(BF)
            d_qkv[rows, q_cols] = nt(gather[...], dq_t).astype(BF)
            d_qkv[rows, k_cols] = (nn(d_scores_b, q_heads) * scale).astype(BF)
            d_qkv[rows, v_cols] = nn(probs_b, da_heads).astype(BF)

        return d_scores, store

    def two_windows(g, w):
        left, store_left = attend(g, w)
        right, store_right = attend(g, w + 1)
        store_left()
        store_right()
        return left + right

    def gradients(g):
        for b in range(3):
            grads[g, b] = tn(ln[...], d_qkv[:, b * channels + g * 128 : b * channels + (g + 1) * 128]).astype(BF)
        proj = tn(att[:, g * 128 : (g + 1) * 128], cot[...]).astype(BF)
        for t in range(groups):
            grads[g, 3, t * 128 : (t + 1) * 128] = proj[:, t * 128 : (t + 1) * 128]
        high = d_bias[...].astype(BF)
        low = (d_bias[...] - high.astype(F32)).astype(BF)
        spread = nt(high, perm[...]) + nt(low, perm[...])
        folded[:, :128] = jnp.zeros((folded.shape[0], 128), F32)
        for o in range(WLON):
            start = (WLON - 1 - o) * ROWS
            folded[start : start + WINDOW, : GROUP * ROWS] += spread[:, o * GROUP * ROWS : (o + 1) * GROUP * ROWS]
        mine = folded[:, : GROUP * ROWS]
        high = mine.astype(BF)
        low = (mine - high.astype(F32)).astype(BF)
        rows = (tn(high, order[...]) + tn(low, order[...])).astype(BF)
        tables[g] = jnp.zeros(tables.shape[1:], BF)
        for t in range(4):
            part = rows[:, t * 128 : (t + 1) * 128]
            for i in range(3):
                slot = 3 * t + i
                tables[g, slot // 4, slot % 4] = part[i * SLOT : (i + 1) * SLOT]

    p1 = jnp.where(core == 0, x, y)
    p2 = jnp.where(core == 0, y, x)

    def on1(p):
        return device(jnp.where(core == 0, p, x), jnp.where(core == 0, y, p), z, core)

    def on2(p):
        return device(jnp.where(core == 0, x, p), jnp.where(core == 0, p, y), z, core)

    def after1(i):
        return lax.rem(p1 + i, 4)

    def after2(i):
        return lax.rem(p2 + i, 4)

    def core_copy(g):
        return remote(grads.at[g, pl.ds(2 * other, 2)], core_in.at[g], core_s.at[g], core_r.at[g], sibling)

    def s1_copy(g, peer):
        return remote(s1_out.at[g, peer], s1_in.at[g, p1], s1_s.at[g, peer], s1_r.at[g, p1], on1(peer))

    def s1_take(g, peer):
        return remote(s1_out.at[g, peer], s1_in.at[g, peer], s1_s.at[g, peer], s1_r.at[g, peer], on1(peer))

    def s2_copy(g, peer):
        return remote(s2_out.at[g, peer], s2_in.at[g, p2], s2_s.at[g, peer], s2_r.at[g, p2], on2(peer))

    def s2_take(g, peer):
        return remote(s2_out.at[g, peer], s2_in.at[g, peer], s2_s.at[g, peer], s2_r.at[g, peer], on2(peer))

    def z_copy(g, peer, slot):
        return remote(z_in.at[g, slot], z_in.at[g, slot], z_s.at[g, peer], z_r.at[g, slot], device(x, y, peer, core))

    def g2_copy(g, peer, slot):
        here = full.at[g, core, p1, slot]
        return remote(here, here, g2_s.at[g, peer], g2_r.at[g, slot], on2(peer))

    def g1_copy(g, peer, slot):
        here = full.at[g, core, slot]
        return remote(here, here, g1_s.at[g, peer], g1_r.at[g, slot], on1(peer))

    def sib_copy(g, half, slot):
        here = full.at[g, half, slot]
        return remote(here, here, sib_s.at[g, slot], sib_r.at[g, slot], sibling)

    def step0(g):
        core_copy(g).start()

    def step1(g):
        core_copy(g).wait_recv()
        for j in range(4):
            rows = slice((j % 2) * PART, (j % 2 + 1) * PART)
            added = grads[g, 2 * core + j // 2, rows].astype(F32) + core_in[g, j // 2, rows].astype(F32)
            s1_out[g, j, :PART] = added.astype(BF)
            s1_out[g, j, PART:] = tables[g, j].reshape(4 * SLOT, 128)
        for i in (2, 1, 3):
            s1_copy(g, after1(i)).start()

    def step2(g):
        def split(part, source):
            high = jnp.where(core == 0, y, source) // 2
            low_rows = jnp.where(high == 0, part[PART:], jnp.zeros_like(part[PART:]))
            return part[:PART], low_rows, part[PART:] - low_rows

        w, t0, t1 = split(s1_out[g, p1].astype(F32), p1)
        for i in (1, 3, 2):
            source = after1(i)
            s1_take(g, source).wait_recv()
            more = split(s1_in[g, source].astype(F32), source)
            w, t0, t1 = w + more[0], t0 + more[1], t1 + more[2]
        for j in range(4):
            s2_out[g, j] = jnp.concatenate(
                [w[j * PIECE : (j + 1) * PIECE], t0[j * SLOT : (j + 1) * SLOT], t1[j * SLOT : (j + 1) * SLOT]], axis=0
            ).astype(BF)
        for i in (2, 1, 3):
            s2_copy(g, after2(i)).start()

    def step3(g):
        total = s2_out[g, p2].astype(F32)
        for i in (1, 3, 2):
            source = after2(i)
            s2_take(g, source).wait_recv()
            total = total + s2_in[g, source].astype(F32)
        z_in[g, z] = total.astype(BF)
        for i in (4, 3, 5, 2, 6, 1, 7):
            z_copy(g, lax.rem(z + i, Z_SIZE), z).start()

    def step4(g):
        for i in (1, 7, 2, 6, 3, 5, 4):
            source = lax.rem(z + i, Z_SIZE)
            z_copy(g, source, source).wait_recv()
        total = z_in[g, 0].astype(F32)
        for i in range(1, Z_SIZE):
            total = total + z_in[g, i].astype(F32)
        full[g, core, p1, p2] = total.astype(BF)
        for i in (2, 1, 3):
            g2_copy(g, after2(i), p2).start()

    def step5(g):
        for i in (1, 3, 2):
            source = after2(i)
            g2_copy(g, source, source).wait_recv()
        for i in (2, 1, 3):
            g1_copy(g, after1(i), p1).start()
        sib_copy(g, core, p1).start()

    def step6(g):
        for i in (1, 3, 2):
            source = after1(i)
            g1_copy(g, source, source).wait_recv()
            sib_copy(g, core, source).start()

    def step7(g):
        for i in range(4):
            sib_copy(g, other, i).wait_recv()
        for half in range(2):
            for j in range(4):
                for i in range(4):
                    part = full[g, half, j, i, :PIECE]
                    block = 2 * half + j // 2
                    row = (j % 2) * PART + i * PIECE
                    if block < 3:
                        cols = slice(block * channels + g * 128, block * channels + (g + 1) * 128)
                        o_qkv[row : row + PIECE, cols] = part
                    else:
                        for u in range(0, PIECE, SLOT):
                            at = row + u
                            tile = at // 128
                            o_proj[g * 128 + at % 128 : g * 128 + at % 128 + SLOT, tile * 128 : (tile + 1) * 128] = (
                                part[u : u + SLOT]
                            )

    def finish(g):
        core_copy(g).wait_send()
        for i in range(1, 4):
            s1_copy(g, after1(i)).wait_send()
            s2_copy(g, after2(i)).wait_send()
            g2_copy(g, after2(i), p2).wait_send()
            g1_copy(g, after1(i), p1).wait_send()
        for i in range(1, Z_SIZE):
            z_copy(g, lax.rem(z + i, Z_SIZE), z).wait_send()
        for i in range(4):
            sib_copy(g, core, i).wait_send()

    def mc_copy():
        return remote(small, small_core, mc_s.at[0], mc_r.at[0], sibling)

    def mx_copy(peer, slot):
        return remote(small_x.at[slot], small_x.at[slot], mx_s.at[peer], mx_r.at[slot], device(peer, y, z, core))

    def my_copy(peer, slot):
        return remote(small_y.at[slot], small_y.at[slot], my_s.at[peer], my_r.at[slot], device(x, peer, z, core))

    def mz_copy(peer, slot):
        return remote(small_z.at[slot], small_z.at[slot], mz_s.at[peer], mz_r.at[slot], device(x, y, peer, core))

    def small_share(copy, buffer, place_here, size, value):
        buffer[place_here] = value
        for i in range(1, size):
            copy(lax.rem(place_here + i, size), place_here).start()

    def small_sum(copy, buffer, place_here, size):
        for i in range(1, size):
            source = lax.rem(place_here + i, size)
            copy(source, source).wait_recv()
        total = buffer[0]
        for i in range(1, size):
            total = total + buffer[i]
        return total

    def small_finish():
        mc_copy().wait_send()
        for copy, here, size in ((mx_copy, x, X_SIZE), (my_copy, y, Y_SIZE), (mz_copy, z, Z_SIZE)):
            for i in range(1, size):
                copy(lax.rem(here + i, size), here).wait_send()

    def group(g, between, after):
        d_bias[...] = two_windows(g, 0)
        between()
        d_bias[...] += two_windows(g, 2)
        gradients(g)
        step0(g)
        after()

    def mid1():
        step1(0)

    def end1():
        step2(0)

    def mid2():
        step3(0)
        step1(1)

    def end2():
        step4(0)
        step2(1)

    group(0, lambda: None, lambda: None)
    group(1, mid1, end1)
    group(2, mid2, end2)

    d_ln = nt(d_qkv[...], w_qkv[...])
    norm = normed[...]
    small[...] = jnp.zeros_like(small)
    for g in range(groups):
        cols = slice(g * 128, (g + 1) * 128)
        small[g : g + 1] = jnp.sum(d_ln[:, cols] * norm[:, cols], axis=0, keepdims=True)
        small[groups + g : groups + g + 1] = jnp.sum(d_ln[:, cols], axis=0, keepdims=True)
    mc_copy().start()
    step1(2)
    step5(0)
    step3(1)
    scaled = d_ln * gain
    d_flat = inv[...] * (
        scaled
        - jnp.mean(scaled, axis=1, keepdims=True)
        - norm * jnp.mean(scaled * norm, axis=1, keepdims=True)
    )
    d_flat = d_flat.astype(BF)
    d_main[...] = nn(unroute[:main], d_flat).astype(BF).reshape(d_main.shape)
    d_edge[...] = nn(unroute[main:], d_flat).astype(BF).reshape(d_edge.shape)
    backs = [
        remote(d_main.at[1], back_main, back_s.at[0], back_r.at[0], device(x, y_down, z, other)),
        remote(d_edge.at[0], back_edge.at[0], back_s.at[1], back_r.at[1], device(beside, y, z, core)),
        remote(d_edge.at[1], back_edge.at[1], back_s.at[2], back_r.at[2], device(beside, y_down, z, other)),
    ]
    step2(2)
    for copy in backs:
        copy.start()
    mc_copy().wait_recv()
    small_share(mx_copy, small_x, x, X_SIZE, small[...] + small_core[...])
    step6(0)
    step4(1)
    step3(2)
    small_share(my_copy, small_y, y, Y_SIZE, small_sum(mx_copy, small_x, x, X_SIZE))
    step7(0)
    step5(1)
    small_share(mz_copy, small_z, z, Z_SIZE, small_sum(my_copy, small_y, y, Y_SIZE))
    step6(1)
    step4(2)

    for copy in backs:
        copy.wait_recv()
    for l in range(WPL):
        for a in range(WLAT):
            if a < half_lat:
                inner, outer = back_main[l, a], back_edge[1, l, a]
            else:
                inner, outer = d_main[0, l, a - half_lat], back_edge[0, l, a - half_lat]
            value = cot_own[l, a].astype(F32) + inner.astype(F32)
            o_tokens[l, a, EDGE:] = value[EDGE:].astype(BF)
            o_tokens[l, a, :EDGE] = (value[:EDGE] + outer.astype(F32)).astype(BF)
    step7(1)
    step5(2)
    total = small_sum(mz_copy, small_z, z, Z_SIZE)
    for g in range(groups):
        o_gain[:, g * 128 : (g + 1) * 128] = total[g : g + 1]
        o_shift[:, g * 128 : (g + 1) * 128] = total[groups + g : groups + g + 1]
    step6(2)
    step7(2)

    for b in range(4):
        at = PIECE + (b // 2) * SLOT
        stacked = jnp.concatenate(
            [
                jnp.concatenate(
                    [
                        full[g, b % 2, slot // 4, slot % 4, at : at + SLOT]
                        for slot in range(3 * t, 3 * t + 3)
                    ],
                    axis=0,
                )
                for g in range(groups)
                for t in range(4)
            ],
            axis=0,
        )
        stacked = stacked.reshape(groups, 4, 3 * SLOT, 128)
        for t in range(4):
            wide[b, :, t * 128 : (t + 1) * 128] = nn(reorder[...], stacked[:, t].reshape(groups * 3 * SLOT, 128))
    for kind in range(4):
        band = jnp.int32(0)
        for b in range(1, 4):
            band = jnp.where(types[b] == kind, b, band)
        table_rows = wide[band]
        parts = []
        for lq in range(WPL):
            for lk in range(WPL):
                for a in range(WLAT):
                    row = (lq * WLAT + a) * heads
                    parts.append(table_rows[row : row + heads, lk * 256 : lk * 256 + WLAT * SPREAD])
        o_table[kind] = jnp.concatenate(parts, axis=1).astype(BF)

    for copy in halos + backs:
        copy.wait_send()
    for g in range(groups):
        finish(g)
    small_finish()


def local(tokens, cotangent, mask_ids, band_type, bias_table, w_qkv, w_proj, ln_gain, ln_shift):
    lon_cols, channels = tokens.shape[2:]
    groups = channels // 128
    heads = groups * GROUP
    half_lat = WLAT // 2
    count = WPL * WLAT * lon_cols
    span = GROUP * WINDOW
    route = token_route(lon_cols)
    constants = [
        jnp.asarray(c, BF)
        for c in (
            route, route.T, head_order(), table_order(), head_blocks(128 // GROUP), gather_heads(), row_order(heads)
        )
    ]
    anywhere = pl.BlockSpec(memory_space=pl.ANY)
    scalars = pl.BlockSpec(memory_space=pltpu.SMEM)
    vmem = pl.BlockSpec(memory_space=pltpu.VMEM)
    dma = pltpu.SemaphoreType.DMA
    bf = lambda *shape: pltpu.VMEM(shape, BF)
    f32 = lambda *shape: pltpu.VMEM(shape, F32)
    pairs = lambda *shape: [dma(shape), dma(shape)]
    d_tokens, g_qkv, g_proj, g_table, g_gain, g_shift = pl.pallas_call(
        whole_kernel,
        out_shape=(
            jax.ShapeDtypeStruct(tokens.shape, BF),
            jax.ShapeDtypeStruct((channels, 3 * channels), BF),
            jax.ShapeDtypeStruct((channels, channels), BF),
            jax.ShapeDtypeStruct(bias_table.shape, BF),
            jax.ShapeDtypeStruct((1, channels), F32),
            jax.ShapeDtypeStruct((1, channels), F32),
        ),
        in_specs=[scalars] * 2 + [anywhere] * 5 + [vmem] * 2 + [anywhere] * 7,
        out_specs=(vmem,) * 6,
        scratch_shapes=[
            bf(2, WPL, half_lat, lon_cols, 2 * channels),
            bf(2, WPL, half_lat, EDGE, 2 * channels),
            bf(*tokens.shape),
            bf(*bias_table.shape),
            bf(channels, 3 * channels),
            bf(channels, channels),
            *[bf(*c.shape) for c in constants],
            f32(heads * ROWS, 512),
            f32(SPREAD * ROWS, heads * ROWS),
            f32(groups, WINDOW, span),
            f32(WINDOW, span),
            f32(count, channels),
            f32(count, 1),
            bf(count, channels),
            bf(count, channels),
            bf(count, 3 * channels),
            bf(count, channels),
            bf(count, channels),
            bf(count, 3 * channels),
            bf(2, WPL, half_lat, lon_cols, channels),
            bf(2, WPL, half_lat, EDGE, channels),
            bf(WPL, half_lat, lon_cols, channels),
            bf(2, WPL, half_lat, EDGE, channels),
            bf(groups, 4, channels, 128),
            bf(groups, 4, 4, SLOT, 128),
            bf(groups, 2, channels, 128),
            bf(groups, 4, PART + 4 * SLOT, 128),
            bf(groups, 4, PART + 4 * SLOT, 128),
            bf(groups, 4, PIECE + 2 * SLOT, 128),
            bf(groups, 4, PIECE + 2 * SLOT, 128),
            bf(groups, Z_SIZE, PIECE + 2 * SLOT, 128),
            bf(groups, 2, 4, 4, PIECE + 2 * SLOT, 128),
            f32(8, 128),
            f32(8, 128),
            f32(X_SIZE, 8, 128),
            f32(Y_SIZE, 8, 128),
            f32(Z_SIZE, 8, 128),
            f32(4, heads * ROWS, 512),
            dma((13,)),
            *pairs(6), *pairs(3), *pairs(groups), *pairs(groups, 4), *pairs(groups, 4), *pairs(groups, Z_SIZE),
            *pairs(groups, 4), *pairs(groups, 4), *pairs(groups, 4),
            *pairs(1), *pairs(X_SIZE), *pairs(Y_SIZE), *pairs(Z_SIZE),
        ],
        compiler_params=pltpu.CompilerParams(
            collective_id=0, has_side_effects=True, vmem_limit_bytes=56 * 1024 * 1024
        ),
        cost_estimate=pl.CostEstimate(flops=6_000_000_000, bytes_accessed=10_000_000, transcendentals=1_000_000),
    )(mask_ids, band_type, tokens, cotangent, bias_table, w_qkv, w_proj, ln_gain, ln_shift, *constants)
    return d_tokens, g_qkv, g_proj, g_gain.reshape(-1), g_shift.reshape(-1), g_table


def solution(mesh):
    placed = (P(None, "lat", "lon", None),) * 2 + (P(None, "lat"),) + (P(),) * 6
    return jax.shard_map(
        local,
        mesh=mesh,
        in_specs=placed,
        out_specs=(P(None, "lat", "lon", None), P(), P(), P(), P(), P()),
        check_vma=False,
    )
```

```python
import jax
import jax.numpy as jnp
import numpy as np
from jax import lax
from jax.experimental import pallas as pl
from jax.experimental.pallas import tpu as pltpu
from jax.sharding import PartitionSpec as P

WPL, WLAT, WLON = 2, 6, 12
WINDOW = WPL * WLAT * WLON
ROWS = WPL * WLAT
SPREAD = 2 * WLON - 1
EDGE = 16
X_SIZE, Y_SIZE, Z_SIZE = 4, 4, 8
PART = 192
PIECE = 48
SLOT = 16
MESH = pl.DeviceIdType.MESH
GROUP = 4
EPSILON = 1e-05
LOG2E = 1.4426950408889634
BF = jnp.bfloat16
F32 = jnp.float32


def token_route(lon_cols):
    half_lat, half_lon = WLAT // 2, WLON // 2
    windows = lon_cols // WLON
    near = WPL * half_lat * lon_cols
    far = WPL * half_lat * EDGE
    route = np.zeros((windows * WINDOW, 2 * near + 2 * far), np.float32)
    for w in range(windows):
        for o in range(WLON):
            for l in range(WPL):
                for a in range(WLAT):
                    level = (l + 1) % WPL
                    col = w * WLON + o + half_lon
                    row = level * half_lat + a % half_lat
                    if col < lon_cols:
                        source = row * lon_cols + col + (near if a >= half_lat else 0)
                    else:
                        source = 2 * near + row * EDGE + col - lon_cols
                        source += far if a >= half_lat else 0
                    route[w * WINDOW + o * ROWS + l * WLAT + a, source] = 1.0
    return route


def head_order():
    perm = np.zeros((GROUP * WINDOW, GROUP * WINDOW), np.float32)
    for o in range(WLON):
        for h in range(GROUP):
            for r in range(ROWS):
                perm[(o * GROUP + h) * ROWS + r, (h * WLON + o) * ROWS + r] = 1.0
    return perm


def table_order():
    order = np.zeros((SPREAD * ROWS, 512), np.float32)
    for d in range(SPREAD):
        for l in range(WPL):
            for a in range(WLAT):
                order[(SPREAD - 1 - d) * ROWS + l * WLAT + a, l * 256 + a * SPREAD + d] = 1.0
    return order


def row_order(heads):
    order = np.zeros((heads * ROWS, heads * ROWS), np.float32)
    for h in range(heads):
        for r in range(ROWS):
            order[r * heads + h, h * ROWS + r] = 1.0
    return order


def head_blocks(head_dim):
    rows = np.arange(GROUP * head_dim)[:, None] // head_dim
    cols = np.arange(GROUP * WINDOW)[None, :] // WINDOW
    return (rows == cols).astype(np.float32)


def gather_heads():
    return np.tile(np.eye(WINDOW, dtype=np.float32), (1, GROUP))


def nn(a, b):
    return lax.dot_general(a, b, (((1,), (0,)), ((), ())), preferred_element_type=F32)


def nt(a, b):
    return lax.dot_general(a, b, (((1,), (1,)), ((), ())), preferred_element_type=F32)


def tn(a, b):
    return lax.dot_general(a, b, (((0,), (0,)), ((), ())), preferred_element_type=F32)


def place():
    lon = lax.axis_index("lon")
    lat = lax.axis_index("lat")
    x = lax.rem(lon, X_SIZE)
    z = lax.rem(lon // X_SIZE, Z_SIZE)
    y = (lat // 2) * 2 + lon // (X_SIZE * Z_SIZE)
    return x, y, z, lax.rem(lat, 2)


def device(x, y, z, core):
    return ((lax.rem(y, 2) * Z_SIZE + z) * X_SIZE + x, (y // 2) * 2 + core)


def whole_kernel(
    ids, types, tokens, cotangent, table_h, w_qkv_h, w_proj_h, gain_v, shift_v,
    route_h, unroute_h, perm_h, order_h, blocks_h, gather_h, reorder_h,
    o_tokens, o_full, o_small,
    cat, edge, cot_own, joined, table, w_qkv, w_proj, route, unroute, perm, order, blocks, gather, reorder,
    tall, folded, bias, d_bias, normed, inv, ln, ln_t, cot, qkv, d_att, att, d_qkv,
    d_main, d_edge, back_main, back_edge,
    grads, tables, core_in, s1_out, s1_in, s2_out, s2_in, z_in, full, small, small_core, small_x, small_y, small_z,
    load_s, out_s, halo_s, halo_r, back_s, back_r, core_s, core_r, s1_s, s1_r, s2_s, s2_r, z_s, z_r, g2_s, g2_r, g1_s, g1_r,
    sib_s, sib_r, mc_s, mc_r, mx_s, mx_r, my_s, my_r, mz_s, mz_r,
):
    half_lat = WLAT // 2
    half_lon = WLON // 2
    lon_cols = tokens.shape[2]
    channels = tokens.shape[3]
    main = 2 * WPL * half_lat * lon_cols
    groups = channels // 128
    heads = groups * GROUP
    windows = lon_cols // WLON
    span = GROUP * WINDOW
    head_dim = 128 // GROUP
    scale = head_dim ** -0.5
    x, y, z, core = place()
    other = 1 - core
    beside = x + 1 - 2 * lax.rem(x, 2)
    across = lax.rem(y + 2, Y_SIZE)
    y_up = lax.rem(y + 2 * other, Y_SIZE)
    y_down = lax.rem(y + 2 * core, Y_SIZE)
    sibling = device(x, y, z, other)

    loads = [
        pltpu.make_async_copy(src, dst, load_s.at[i])
        for i, (src, dst) in enumerate((
            (table_h, table), (order_h, order), (reorder_h, reorder), (perm_h, perm),
            (tokens.at[:, pl.ds(half_lat, half_lat)], cat.at[0, :, :, :, pl.ds(0, channels)]),
            (cotangent.at[:, pl.ds(half_lat, half_lat)], cat.at[0, :, :, :, pl.ds(channels, channels)]),
            (route_h, route), (w_proj_h, w_proj), (blocks_h, blocks), (gather_h, gather),
            (unroute_h, unroute), (cotangent, cot_own),
            *(
                (
                    w_qkv_h.at[:, pl.ds(b * channels + g * 128, 128)],
                    w_qkv.at[:, pl.ds((3 * g + b) * 128, 128)],
                )
                for g in range(groups)
                for b in range(3)
            ),
        ))
    ]
    for load in loads:
        load.start()

    barrier = pltpu.get_barrier_semaphore()
    friends = [sibling, device(x, across, z, other), device(beside, y, z, other), device(beside, across, z, other)]
    friends += [device(lax.rem(x + i, X_SIZE), y, z, core) for i in range(1, X_SIZE)]
    friends += [device(x, lax.rem(y + i, Y_SIZE), z, core) for i in range(1, Y_SIZE)]
    friends += [device(x, y, lax.rem(z + i, Z_SIZE), core) for i in range(1, Z_SIZE)]
    for friend in friends:
        pl.semaphore_signal(barrier, inc=1, device_id=friend, device_id_type=MESH)
    pl.semaphore_wait(barrier, len(friends))

    def remote(src, dst, send, recv, target):
        return pltpu.make_async_remote_copy(
            src_ref=src, dst_ref=dst, send_sem=send, recv_sem=recv, device_id=target, device_id_type=MESH
        )

    first, last = pl.ds(0, half_lat), pl.ds(half_lat, half_lat)
    halos = []
    for i, array in enumerate((tokens, cotangent)):
        lanes = pl.ds(i * channels, channels)
        up = device(x, y_up, z, other)
        halos += [
            (array.at[:, first], cat.at[1, :, :, :, lanes], up),
            (array.at[:, last, pl.ds(0, EDGE)], edge.at[0, :, :, :, lanes], device(beside, y, z, core)),
            (array.at[:, first, pl.ds(0, EDGE)], edge.at[1, :, :, :, lanes], device(beside, y_up, z, other)),
        ]
    halos = [remote(src, dst, halo_s.at[i], halo_r.at[i], to) for i, (src, dst, to) in enumerate(halos)]
    for copy in halos:
        copy.start()

    for load in loads[:4]:
        load.wait()
    own_type = types[lax.axis_index("lat")]
    picked = (lax.broadcasted_iota(jnp.int32, (1, 4, 1), 1) == own_type).astype(F32)
    rows_of_type = jnp.sum(table[...].astype(F32) * picked, axis=1)
    tall[...] = jnp.zeros_like(tall)
    for lq in range(WPL):
        for lk in range(WPL):
            for a in range(WLAT):
                start = ((lq * WPL + lk) * WLAT + a) * WLAT * SPREAD
                row = (lq * WLAT + a) * heads
                tall[row : row + heads, lk * 256 : lk * 256 + WLAT * SPREAD] = rows_of_type[:, start : start + WLAT * SPREAD]
    laid = nt(order[...], tall[...].astype(BF)).astype(BF)
    folded[...] = nn(laid, reorder[...])
    lane = lax.rem(lax.broadcasted_iota(jnp.int32, (1, span), 1), ROWS)
    sub = lax.rem(lax.broadcasted_iota(jnp.int32, (WINDOW, 1), 0), ROWS)
    id_q = jnp.zeros((1, span), jnp.int32)
    id_k = jnp.zeros((WINDOW, 1), jnp.int32)
    for l in range(WPL):
        for a in range(WLAT):
            value = ids[l, a]
            id_q = jnp.where(lane == l * WLAT + a, value, id_q)
            id_k = jnp.where(sub == l * WLAT + a, value, id_k)
    masked = jnp.where(id_k == id_q, 0.0, -1e30)
    for g in range(groups):
        pieces = [
            folded[(WLON - 1 - o) * ROWS : (WLON - 1 - o) * ROWS + WINDOW, g * GROUP * ROWS : (g + 1) * GROUP * ROWS]
            for o in range(WLON)
        ]
        spread = jnp.concatenate(pieces, axis=1).astype(BF)
        bias[g] = nn(spread, perm[...]) * LOG2E + masked

    gain = gain_v[...].reshape(1, channels)
    shift = shift_v[...].reshape(1, channels)
    for load in loads[4:]:
        load.wait()
    for copy in halos[:3]:
        copy.wait_recv()
    x_in = nn(route[:, :main], cat[..., :channels].reshape(main, channels))
    x_in = x_in + nn(route[:, main:], edge[..., :channels].reshape(-1, channels))
    average = jnp.mean(x_in, axis=1, keepdims=True)
    centred = x_in - average
    variance = jnp.mean(centred * centred, axis=1, keepdims=True)
    inv_std = lax.rsqrt(variance + EPSILON)
    inv[...] = inv_std
    norm = centred * inv_std
    normed[...] = norm
    ln_out = (norm * gain + shift).astype(BF)
    ln[...] = ln_out
    ln_t[...] = ln_out.T
    qkv[...] = nn(ln[...], w_qkv[...]).astype(BF)
    for copy in halos[3:]:
        copy.wait_recv()
    moved = nn(route[:, :main], cat[..., channels:].reshape(main, channels))
    moved = moved + nn(route[:, main:], edge[..., channels:].reshape(-1, channels))
    cot[...] = moved.astype(BF)
    d_att[...] = nt(cot[...], w_proj[...]).astype(BF)

    lanes = lax.broadcasted_iota(jnp.int32, (1, 128), 1) // head_dim
    own = [(lanes == h).astype(F32).astype(BF) for h in range(GROUP)]
    eye = (
        lax.broadcasted_iota(jnp.int32, (128, 128), 0) == lax.broadcasted_iota(jnp.int32, (128, 128), 1)
    ).astype(F32).astype(BF)

    def attend(g, w):
        rows = pl.ds(pl.multiple_of(w * WINDOW, WINDOW), WINDOW)
        q_cols, k_cols, v_cols = (slice((3 * g + b) * 128, (3 * g + b + 1) * 128) for b in range(3))
        cols = slice(g * 128, (g + 1) * 128)
        q, k, v, da = qkv[rows, q_cols], qkv[rows, k_cols], qkv[rows, v_cols], d_att[rows, cols]
        q_heads = jnp.concatenate([q * own[h] for h in range(GROUP)], axis=0)
        da_heads = jnp.concatenate([da * own[h] for h in range(GROUP)], axis=0)
        raised = jnp.exp2(nt(k, q_heads) * (scale * LOG2E) + bias[g])
        probs = raised * (1.0 / jnp.sum(raised, axis=0, keepdims=True))
        probs_b = probs.astype(BF)
        v_t = nt(eye, v).astype(BF)
        k_t = nt(eye, k).astype(BF)
        weighted = probs * nt(v, da_heads)
        d_scores = weighted - probs * jnp.sum(weighted, axis=0, keepdims=True)
        d_scores_b = d_scores.astype(BF)
        mask = blocks[...]
        att_t = nn(v_t, probs_b).astype(BF) * mask
        dq_t = (nn(k_t, d_scores_b) * scale).astype(BF) * mask

        def store():
            att[rows, cols] = nt(gather[...], att_t).astype(BF)
            d_qkv[rows, q_cols] = nt(gather[...], dq_t).astype(BF)
            d_qkv[rows, k_cols] = (nn(d_scores_b, q_heads) * scale).astype(BF)
            d_qkv[rows, v_cols] = nn(probs_b, da_heads).astype(BF)

        return d_scores, store

    def two_windows(g, w):
        left, store_left = attend(g, w)
        right, store_right = attend(g, w + 1)
        store_left()
        store_right()
        return left + right

    def gradients(g):
        weights = nn(ln_t[...], d_qkv[:, 3 * g * 128 : 3 * (g + 1) * 128]).astype(BF)
        for b in range(3):
            grads[g, b] = weights[:, b * 128 : (b + 1) * 128]
        proj = tn(att[:, g * 128 : (g + 1) * 128], cot[...]).astype(BF)
        for t in range(groups):
            grads[g, 3, t * 128 : (t + 1) * 128] = proj[:, t * 128 : (t + 1) * 128]
        high = d_bias[...].astype(BF)
        low = (d_bias[...] - high.astype(F32)).astype(BF)
        spread = nt(high, perm[...]) + nt(low, perm[...])
        folded[:, :128] = jnp.zeros((folded.shape[0], 128), F32)
        for o in range(WLON):
            start = (WLON - 1 - o) * ROWS
            folded[start : start + WINDOW, : GROUP * ROWS] += spread[:, o * GROUP * ROWS : (o + 1) * GROUP * ROWS]
        rows = tn(folded[:, : GROUP * ROWS].astype(BF), order[...]).astype(BF)
        tables[g] = jnp.zeros(tables.shape[1:], BF)
        for t in range(4):
            part = rows[:, t * 128 : (t + 1) * 128]
            for i in range(3):
                slot = 3 * t + i
                tables[g, slot // 4, slot % 4] = part[i * SLOT : (i + 1) * SLOT]

    p1 = jnp.where(core == 0, x, y)
    p2 = jnp.where(core == 0, y, x)

    def on1(p):
        return device(jnp.where(core == 0, p, x), jnp.where(core == 0, y, p), z, core)

    def on2(p):
        return device(jnp.where(core == 0, x, p), jnp.where(core == 0, p, y), z, core)

    def after1(i):
        return lax.rem(p1 + i, 4)

    def after2(i):
        return lax.rem(p2 + i, 4)

    def core_copy(g):
        return remote(grads.at[g, pl.ds(2 * other, 2)], core_in.at[g], core_s.at[g], core_r.at[g], sibling)

    def s1_copy(g, peer):
        return remote(s1_out.at[g, peer], s1_in.at[g, p1], s1_s.at[g, peer], s1_r.at[g, p1], on1(peer))

    def s1_take(g, peer):
        return remote(s1_out.at[g, peer], s1_in.at[g, peer], s1_s.at[g, peer], s1_r.at[g, peer], on1(peer))

    def s2_copy(g, peer):
        return remote(s2_out.at[g, peer], s2_in.at[g, p2], s2_s.at[g, peer], s2_r.at[g, p2], on2(peer))

    def s2_take(g, peer):
        return remote(s2_out.at[g, peer], s2_in.at[g, peer], s2_s.at[g, peer], s2_r.at[g, peer], on2(peer))

    def z_copy(g, peer, slot):
        return remote(z_in.at[g, slot], z_in.at[g, slot], z_s.at[g, peer], z_r.at[g, slot], device(x, y, peer, core))

    def g2_copy(g, peer, slot):
        here = full.at[g, core, p1, slot]
        return remote(here, here, g2_s.at[g, peer], g2_r.at[g, slot], on2(peer))

    def g1_copy(g, peer, slot):
        here = full.at[g, core, slot]
        return remote(here, here, g1_s.at[g, peer], g1_r.at[g, slot], on1(peer))

    def sib_copy(g, half, slot):
        here = full.at[g, half, slot]
        return remote(here, here, sib_s.at[g, slot], sib_r.at[g, slot], sibling)

    def step0(g):
        core_copy(g).start()

    def step1(g):
        core_copy(g).wait_recv()
        for j in range(4):
            rows = slice((j % 2) * PART, (j % 2 + 1) * PART)
            added = grads[g, 2 * core + j // 2, rows].astype(F32) + core_in[g, j // 2, rows].astype(F32)
            s1_out[g, j, :PART] = added.astype(BF)
            s1_out[g, j, PART:] = tables[g, j].reshape(4 * SLOT, 128)
        for i in (2, 1, 3):
            s1_copy(g, after1(i)).start()

    def step2(g):
        def split(part, source):
            high = jnp.where(core == 0, y, source) // 2
            low_rows = jnp.where(high == 0, part[PART:], jnp.zeros_like(part[PART:]))
            return part[:PART], low_rows, part[PART:] - low_rows

        w, t0, t1 = split(s1_out[g, p1].astype(F32), p1)
        for i in (1, 3, 2):
            source = after1(i)
            s1_take(g, source).wait_recv()
            more = split(s1_in[g, source].astype(F32), source)
            w, t0, t1 = w + more[0], t0 + more[1], t1 + more[2]
        for j in range(4):
            s2_out[g, j] = jnp.concatenate(
                [w[j * PIECE : (j + 1) * PIECE], t0[j * SLOT : (j + 1) * SLOT], t1[j * SLOT : (j + 1) * SLOT]], axis=0
            ).astype(BF)
        for i in (2, 1, 3):
            s2_copy(g, after2(i)).start()

    def step3(g):
        total = s2_out[g, p2].astype(F32)
        for i in (1, 3, 2):
            source = after2(i)
            s2_take(g, source).wait_recv()
            total = total + s2_in[g, source].astype(F32)
        z_in[g, z] = total.astype(BF)
        for i in (4, 3, 5, 2, 6, 1, 7):
            z_copy(g, lax.rem(z + i, Z_SIZE), z).start()

    def step4(g):
        for i in (1, 7, 2, 6, 3, 5, 4):
            source = lax.rem(z + i, Z_SIZE)
            z_copy(g, source, source).wait_recv()
        total = z_in[g, 0].astype(F32)
        for i in range(1, Z_SIZE):
            total = total + z_in[g, i].astype(F32)
        full[g, core, p1, p2] = total.astype(BF)
        for i in (2, 1, 3):
            g2_copy(g, after2(i), p2).start()

    def step5(g):
        for i in (1, 3, 2):
            source = after2(i)
            g2_copy(g, source, source).wait_recv()
        for i in (2, 1, 3):
            g1_copy(g, after1(i), p1).start()
        sib_copy(g, core, p1).start()

    def step6(g):
        for i in (1, 3, 2):
            source = after1(i)
            g1_copy(g, source, source).wait_recv()
            sib_copy(g, core, source).start()

    def step7(g):
        for i in range(4):
            sib_copy(g, other, i).wait_recv()
        full_copy(g).start()

    def full_copy(g):
        return pltpu.make_async_copy(full.at[g], o_full.at[g], out_s.at[g])

    def tokens_copy():
        return pltpu.make_async_copy(joined, o_tokens, out_s.at[groups])

    def finish(g):
        core_copy(g).wait_send()
        for i in range(1, 4):
            s1_copy(g, after1(i)).wait_send()
            s2_copy(g, after2(i)).wait_send()
            g2_copy(g, after2(i), p2).wait_send()
            g1_copy(g, after1(i), p1).wait_send()
        for i in range(1, Z_SIZE):
            z_copy(g, lax.rem(z + i, Z_SIZE), z).wait_send()
        for i in range(4):
            sib_copy(g, core, i).wait_send()

    def mc_copy():
        return remote(small, small_core, mc_s.at[0], mc_r.at[0], sibling)

    def mx_copy(peer, slot):
        return remote(small_x.at[slot], small_x.at[slot], mx_s.at[peer], mx_r.at[slot], device(peer, y, z, core))

    def my_copy(peer, slot):
        return remote(small_y.at[slot], small_y.at[slot], my_s.at[peer], my_r.at[slot], device(x, peer, z, core))

    def mz_copy(peer, slot):
        return remote(small_z.at[slot], small_z.at[slot], mz_s.at[peer], mz_r.at[slot], device(x, y, peer, core))

    def small_share(copy, buffer, place_here, size, value):
        buffer[place_here] = value
        for i in range(1, size):
            copy(lax.rem(place_here + i, size), place_here).start()

    def small_sum(copy, buffer, place_here, size):
        for i in range(1, size):
            source = lax.rem(place_here + i, size)
            copy(source, source).wait_recv()
        total = buffer[0]
        for i in range(1, size):
            total = total + buffer[i]
        return total

    def small_finish():
        mc_copy().wait_send()
        for copy, here, size in ((mx_copy, x, X_SIZE), (my_copy, y, Y_SIZE), (mz_copy, z, Z_SIZE)):
            for i in range(1, size):
                copy(lax.rem(here + i, size), here).wait_send()

    def group(g, between):
        d_bias[...] = two_windows(g, 0)
        between()
        d_bias[...] += two_windows(g, 2)
        gradients(g)
        step0(g)

    def mid1():
        step1(0)

    def mid2():
        step1(1)
        step2(0)

    group(0, lambda: None)
    group(1, mid1)
    group(2, mid2)
    step3(0)
    step2(1)
    step1(2)

    d_ln = nt(d_qkv[...], w_qkv[...])
    norm = normed[...]
    small[...] = jnp.zeros_like(small)
    for g in range(groups):
        cols = slice(g * 128, (g + 1) * 128)
        small[g : g + 1] = jnp.sum(d_ln[:, cols] * norm[:, cols], axis=0, keepdims=True)
        small[groups + g : groups + g + 1] = jnp.sum(d_ln[:, cols], axis=0, keepdims=True)
    mc_copy().start()
    scaled = d_ln * gain
    d_flat = inv[...] * (
        scaled
        - jnp.mean(scaled, axis=1, keepdims=True)
        - norm * jnp.mean(scaled * norm, axis=1, keepdims=True)
    )
    d_flat = d_flat.astype(BF)
    d_main[...] = nn(unroute[:main], d_flat).astype(BF).reshape(d_main.shape)
    d_edge[...] = nn(unroute[main:], d_flat).astype(BF).reshape(d_edge.shape)
    backs = [
        remote(d_main.at[1], back_main, back_s.at[0], back_r.at[0], device(x, y_down, z, other)),
        remote(d_edge.at[0], back_edge.at[0], back_s.at[1], back_r.at[1], device(beside, y, z, core)),
        remote(d_edge.at[1], back_edge.at[1], back_s.at[2], back_r.at[2], device(beside, y_down, z, other)),
    ]
    for copy in backs:
        copy.start()
    step3(1)
    step2(2)
    mc_copy().wait_recv()
    small_share(mx_copy, small_x, x, X_SIZE, small[...] + small_core[...])
    step4(0)
    step3(2)
    small_share(my_copy, small_y, y, Y_SIZE, small_sum(mx_copy, small_x, x, X_SIZE))
    step5(0)
    small_share(mz_copy, small_z, z, Z_SIZE, small_sum(my_copy, small_y, y, Y_SIZE))

    for copy in backs:
        copy.wait_recv()
    for l in range(WPL):
        for a in range(WLAT):
            if a < half_lat:
                inner, outer = back_main[l, a], back_edge[1, l, a]
            else:
                inner, outer = d_main[0, l, a - half_lat], back_edge[0, l, a - half_lat]
            value = cot_own[l, a].astype(F32) + inner.astype(F32)
            joined[l, a, EDGE:] = value[EDGE:].astype(BF)
            joined[l, a, :EDGE] = (value[:EDGE] + outer.astype(F32)).astype(BF)
    tokens_copy().start()
    step4(1)
    step6(0)
    step4(2)
    step5(1)
    step7(0)
    o_small[...] = small_sum(mz_copy, small_z, z, Z_SIZE)
    step5(2)
    step6(1)
    step7(1)
    step6(2)
    step7(2)

    for copy in halos + backs:
        copy.wait_send()
    for g in range(groups):
        finish(g)
    small_finish()
    tokens_copy().wait()
    for g in range(groups):
        full_copy(g).wait()


def assemble_kernel(
    types, full_h, joined_h, small, reorder,
    o_tokens, o_qkv, o_proj, o_table, o_gain, o_shift,
    full, wide, typed, sem,
):
    channels = o_proj.shape[0]
    groups = channels // 128
    heads = groups * GROUP
    loads = [pltpu.make_async_copy(full_h.at[g], full.at[g], sem.at[g]) for g in range(groups)]
    through = pltpu.make_async_copy(joined_h, o_tokens, sem.at[groups])
    for load in loads:
        load.start()
    through.start()
    o_gain[...] = jnp.concatenate([small[g : g + 1] for g in range(groups)], axis=1).reshape(channels)
    o_shift[...] = jnp.concatenate([small[g : g + 1] for g in range(groups, 2 * groups)], axis=1).reshape(channels)
    for g in range(groups):
        loads[g].wait()
        for half in range(2):
            for j in range(4):
                for i in range(4):
                    part = full[g, half, j, i, :PIECE]
                    block = 2 * half + j // 2
                    row = (j % 2) * PART + i * PIECE
                    if block < 3:
                        cols = slice(block * channels + g * 128, block * channels + (g + 1) * 128)
                        o_qkv[row : row + PIECE, cols] = part
                    else:
                        for u in range(0, PIECE, SLOT):
                            at = row + u
                            tile = at // 128
                            o_proj[g * 128 + at % 128 : g * 128 + at % 128 + SLOT, tile * 128 : (tile + 1) * 128] = (
                                part[u : u + SLOT]
                            )

    for b in range(4):
        at = PIECE + (b // 2) * SLOT
        for t in range(4):
            stacked = jnp.concatenate(
                [
                    full[g, b % 2, slot // 4, slot % 4, at : at + SLOT]
                    for g in range(groups)
                    for slot in range(3 * t, 3 * t + 3)
                ],
                axis=0,
            )
            wide[b, :, t * 128 : (t + 1) * 128] = nn(reorder[...], stacked)
    for kind in range(4):
        band = jnp.int32(0)
        for b in range(1, 4):
            band = jnp.where(types[b] == kind, b, band)
        table_rows = wide[band]
        parts = []
        for lq in range(WPL):
            for lk in range(WPL):
                for a in range(WLAT):
                    row = (lq * WLAT + a) * heads
                    parts.append(table_rows[row : row + heads, lk * 256 : lk * 256 + WLAT * SPREAD])
        typed[:, kind, :] = jnp.concatenate(parts, axis=1)
    o_table[...] = typed[...].astype(BF)
    through.wait()


def local(tokens, cotangent, mask_ids, band_type, bias_table, w_qkv, w_proj, ln_gain, ln_shift):
    lon_cols, channels = tokens.shape[2:]
    groups = channels // 128
    heads = groups * GROUP
    half_lat = WLAT // 2
    count = WPL * WLAT * lon_cols
    span = GROUP * WINDOW
    route = token_route(lon_cols)
    constants = [
        jnp.asarray(c, BF)
        for c in (
            route, route.T, head_order(), table_order(), head_blocks(128 // GROUP), gather_heads(), row_order(heads)
        )
    ]
    anywhere = pl.BlockSpec(memory_space=pl.ANY)
    scalars = pl.BlockSpec(memory_space=pltpu.SMEM)
    vmem = pl.BlockSpec(memory_space=pltpu.VMEM)
    dma = pltpu.SemaphoreType.DMA
    bf = lambda *shape: pltpu.VMEM(shape, BF)
    f32 = lambda *shape: pltpu.VMEM(shape, F32)
    pairs = lambda *shape: [dma(shape), dma(shape)]
    pieces = (groups, 2, 4, 4, PIECE + 2 * SLOT, 128)
    table = bias_table.transpose(1, 0, 2)
    joined, full, small = pl.pallas_call(
        whole_kernel,
        out_shape=(
            jax.ShapeDtypeStruct(tokens.shape, BF),
            jax.ShapeDtypeStruct(pieces, BF),
            jax.ShapeDtypeStruct((8, 128), F32),
        ),
        in_specs=[scalars] * 2 + [anywhere] * 5 + [vmem] * 2 + [anywhere] * 7,
        out_specs=(anywhere, anywhere, vmem),
        scratch_shapes=[
            bf(2, WPL, half_lat, lon_cols, 2 * channels),
            bf(2, WPL, half_lat, EDGE, 2 * channels),
            bf(*tokens.shape),
            bf(*tokens.shape),
            bf(*table.shape),
            bf(channels, 3 * channels),
            bf(channels, channels),
            *[bf(*c.shape) for c in constants],
            f32(heads * ROWS, 512),
            f32(SPREAD * ROWS, heads * ROWS),
            f32(groups, WINDOW, span),
            f32(WINDOW, span),
            f32(count, channels),
            f32(count, 1),
            bf(count, channels),
            bf(channels, count),
            bf(count, channels),
            bf(count, 3 * channels),
            bf(count, channels),
            bf(count, channels),
            bf(count, 3 * channels),
            bf(2, WPL, half_lat, lon_cols, channels),
            bf(2, WPL, half_lat, EDGE, channels),
            bf(WPL, half_lat, lon_cols, channels),
            bf(2, WPL, half_lat, EDGE, channels),
            bf(groups, 4, channels, 128),
            bf(groups, 4, 4, SLOT, 128),
            bf(groups, 2, channels, 128),
            bf(groups, 4, PART + 4 * SLOT, 128),
            bf(groups, 4, PART + 4 * SLOT, 128),
            bf(groups, 4, PIECE + 2 * SLOT, 128),
            bf(groups, 4, PIECE + 2 * SLOT, 128),
            bf(groups, Z_SIZE, PIECE + 2 * SLOT, 128),
            bf(*pieces),
            f32(8, 128),
            f32(8, 128),
            f32(X_SIZE, 8, 128),
            f32(Y_SIZE, 8, 128),
            f32(Z_SIZE, 8, 128),
            dma((12 + 3 * groups,)),
            dma((groups + 1,)),
            *pairs(6), *pairs(3), *pairs(groups), *pairs(groups, 4), *pairs(groups, 4), *pairs(groups, Z_SIZE),
            *pairs(groups, 4), *pairs(groups, 4), *pairs(groups, 4),
            *pairs(1), *pairs(X_SIZE), *pairs(Y_SIZE), *pairs(Z_SIZE),
        ],
        compiler_params=pltpu.CompilerParams(
            collective_id=0, has_side_effects=True, vmem_limit_bytes=56 * 1024 * 1024
        ),
        cost_estimate=pl.CostEstimate(flops=6_000_000_000, bytes_accessed=10_000_000, transcendentals=1_000_000),
    )(mask_ids, band_type, tokens, cotangent, table, w_qkv, w_proj, ln_gain, ln_shift, *constants)
    d_tokens, g_qkv, g_proj, g_table, g_gain, g_shift = pl.pallas_call(
        assemble_kernel,
        out_shape=(
            jax.ShapeDtypeStruct(tokens.shape, BF),
            jax.ShapeDtypeStruct((channels, 3 * channels), BF),
            jax.ShapeDtypeStruct((channels, channels), BF),
            jax.ShapeDtypeStruct(table.shape, BF),
            jax.ShapeDtypeStruct((channels,), F32),
            jax.ShapeDtypeStruct((channels,), F32),
        ),
        in_specs=[scalars, anywhere, anywhere, vmem, vmem],
        out_specs=(anywhere, vmem, vmem, vmem, vmem, vmem),
        scratch_shapes=[
            bf(*pieces),
            f32(4, heads * ROWS, 512),
            f32(*table.shape),
            dma((groups + 1,)),
        ],
        compiler_params=pltpu.CompilerParams(vmem_limit_bytes=40 * 1024 * 1024),
        cost_estimate=pl.CostEstimate(flops=100_000_000, bytes_accessed=6_000_000, transcendentals=0),
    )(band_type, full, joined, small, constants[-1])
    return d_tokens, g_qkv, g_proj, g_gain, g_shift, g_table.transpose(1, 0, 2)


def solution(mesh):
    placed = (P(None, "lat", "lon", None),) * 2 + (P(None, "lat"),) + (P(),) * 6
    return jax.shard_map(
        local,
        mesh=mesh,
        in_specs=placed,
        out_specs=(P(None, "lat", "lon", None), P(), P(), P(), P(), P()),
        check_vma=False,
    )
```

```python
import jax
import jax.numpy as jnp
import numpy as np
from jax import lax
from jax.experimental import pallas as pl
from jax.experimental.pallas import tpu as pltpu
from jax.sharding import PartitionSpec as P

WPL, WLAT, WLON = 2, 6, 12
WINDOW = WPL * WLAT * WLON
ROWS = WPL * WLAT
SPREAD = 2 * WLON - 1
EDGE = 16
X_SIZE, Y_SIZE, Z_SIZE = 4, 4, 8
PART = 192
PIECE = 48
SLOT = 16
UNIT = 8
MESH = pl.DeviceIdType.MESH
GROUP = 4
EPSILON = 1e-05
LOG2E = 1.4426950408889634
BF = jnp.bfloat16
F32 = jnp.float32


def token_route(lon_cols):
    half_lat, half_lon = WLAT // 2, WLON // 2
    windows = lon_cols // WLON
    near = WPL * half_lat * lon_cols
    far = WPL * half_lat * EDGE
    route = np.zeros((windows * WINDOW, 2 * near + 2 * far), np.float32)
    for w in range(windows):
        for o in range(WLON):
            for l in range(WPL):
                for a in range(WLAT):
                    level = (l + 1) % WPL
                    col = w * WLON + o + half_lon
                    row = level * half_lat + a % half_lat
                    if col < lon_cols:
                        source = row * lon_cols + col + (near if a >= half_lat else 0)
                    else:
                        source = 2 * near + row * EDGE + col - lon_cols
                        source += far if a >= half_lat else 0
                    route[w * WINDOW + o * ROWS + l * WLAT + a, source] = 1.0
    return route


def head_order():
    perm = np.zeros((GROUP * WINDOW, GROUP * WINDOW), np.float32)
    for o in range(WLON):
        for h in range(GROUP):
            for r in range(ROWS):
                perm[(o * GROUP + h) * ROWS + r, (h * WLON + o) * ROWS + r] = 1.0
    return perm


def table_order():
    order = np.zeros((SPREAD * ROWS, 512), np.float32)
    for d in range(SPREAD):
        for l in range(WPL):
            for a in range(WLAT):
                order[(SPREAD - 1 - d) * ROWS + l * WLAT + a, l * 256 + a * SPREAD + d] = 1.0
    return order


def row_order(heads):
    order = np.zeros((heads * ROWS, heads * ROWS), np.float32)
    for h in range(heads):
        for r in range(ROWS):
            order[r * heads + h, h * ROWS + r] = 1.0
    return order


def head_blocks(head_dim):
    rows = np.arange(GROUP * head_dim)[:, None] // head_dim
    cols = np.arange(GROUP * WINDOW)[None, :] // WINDOW
    return (rows == cols).astype(np.float32)


def gather_heads():
    return np.tile(np.eye(WINDOW, dtype=np.float32), (1, GROUP))


def nn(a, b):
    return lax.dot_general(a, b, (((1,), (0,)), ((), ())), preferred_element_type=F32)


def nt(a, b):
    return lax.dot_general(a, b, (((1,), (1,)), ((), ())), preferred_element_type=F32)


def tn(a, b):
    return lax.dot_general(a, b, (((0,), (0,)), ((), ())), preferred_element_type=F32)


def place():
    lon = lax.axis_index("lon")
    lat = lax.axis_index("lat")
    x = lax.rem(lon, X_SIZE)
    z = lax.rem(lon // X_SIZE, Z_SIZE)
    y = (lat // 2) * 2 + lon // (X_SIZE * Z_SIZE)
    return x, y, z, lax.rem(lat, 2)


def device(x, y, z, core):
    return ((lax.rem(y, 2) * Z_SIZE + z) * X_SIZE + x, (y // 2) * 2 + core)


def whole_kernel(
    ids, types, tokens, cotangent, table_h, w_qkv_h, w_proj_h, gain_v, shift_v,
    route_h, unroute_h, perm_h, order_h, blocks_h, gather_h, reorder_h,
    o_tokens, o_full, o_small,
    cat, edge, cot_own, joined, table, w_qkv, w_proj, route, unroute, perm, order, blocks, gather, reorder,
    tall, folded, bias, d_bias, normed, inv, ln, ln_t, cot, qkv, d_att, att, d_qkv,
    d_main, d_edge, back_main, back_edge,
    grads, tables, core_in, s1_out, s1_in, s2_out, s2_in, z_in, full, small, small_core, small_x, small_y, small_z,
    load_s, out_s, halo_s, halo_r, back_s, back_r, core_s, core_r, s1_s, s1_r, s2_s, s2_r, z_s, z_r, g2_s, g2_r, g1_s, g1_r,
    sib_s, sib_r, mc_s, mc_r, mx_s, mx_r, my_s, my_r, mz_s, mz_r,
):
    half_lat = WLAT // 2
    half_lon = WLON // 2
    lon_cols = tokens.shape[2]
    channels = tokens.shape[3]
    main = 2 * WPL * half_lat * lon_cols
    groups = channels // 128
    heads = groups * GROUP
    windows = lon_cols // WLON
    span = GROUP * WINDOW
    head_dim = 128 // GROUP
    scale = head_dim ** -0.5
    x, y, z, core = place()
    other = 1 - core
    beside = x + 1 - 2 * lax.rem(x, 2)
    across = lax.rem(y + 2, Y_SIZE)
    y_up = lax.rem(y + 2 * other, Y_SIZE)
    y_down = lax.rem(y + 2 * core, Y_SIZE)
    sibling = device(x, y, z, other)

    loads = [
        pltpu.make_async_copy(src, dst, load_s.at[i])
        for i, (src, dst) in enumerate((
            (table_h, table), (order_h, order), (reorder_h, reorder), (perm_h, perm),
            (tokens.at[:, pl.ds(half_lat, half_lat)], cat.at[0, :, :, :, pl.ds(0, channels)]),
            (cotangent.at[:, pl.ds(half_lat, half_lat)], cat.at[0, :, :, :, pl.ds(channels, channels)]),
            (route_h, route), (w_proj_h, w_proj), (blocks_h, blocks), (gather_h, gather),
            (unroute_h, unroute), (cotangent, cot_own),
            *(
                (
                    w_qkv_h.at[:, pl.ds(b * channels + g * 128, 128)],
                    w_qkv.at[:, pl.ds((3 * g + b) * 128, 128)],
                )
                for g in range(groups)
                for b in range(3)
            ),
        ))
    ]
    barrier = pltpu.get_barrier_semaphore()
    friends = [sibling, device(x, across, z, other), device(beside, y, z, other), device(beside, across, z, other)]
    friends += [device(lax.rem(x + i, X_SIZE), y, z, core) for i in range(1, X_SIZE)]
    friends += [device(x, lax.rem(y + i, Y_SIZE), z, core) for i in range(1, Y_SIZE)]
    friends += [device(x, y, lax.rem(z + i, Z_SIZE), core) for i in range(1, Z_SIZE)]
    for friend in friends:
        pl.semaphore_signal(barrier, inc=1, device_id=friend, device_id_type=MESH)
    for load in loads:
        load.start()
    pl.semaphore_wait(barrier, len(friends))

    def remote(src, dst, send, recv, target):
        return pltpu.make_async_remote_copy(
            src_ref=src, dst_ref=dst, send_sem=send, recv_sem=recv, device_id=target, device_id_type=MESH
        )

    first, last = pl.ds(0, half_lat), pl.ds(half_lat, half_lat)
    halos = []
    for i, array in enumerate((tokens, cotangent)):
        lanes = pl.ds(i * channels, channels)
        up = device(x, y_up, z, other)
        halos += [
            (array.at[:, first], cat.at[1, :, :, :, lanes], up),
            (array.at[:, last, pl.ds(0, EDGE)], edge.at[0, :, :, :, lanes], device(beside, y, z, core)),
            (array.at[:, first, pl.ds(0, EDGE)], edge.at[1, :, :, :, lanes], device(beside, y_up, z, other)),
        ]
    halos = [remote(src, dst, halo_s.at[i], halo_r.at[i], to) for i, (src, dst, to) in enumerate(halos)]
    for copy in halos:
        copy.start()

    for load in loads[:4]:
        load.wait()
    own_type = types[lax.axis_index("lat")]
    picked = (lax.broadcasted_iota(jnp.int32, (1, 4, 1), 1) == own_type).astype(F32)
    rows_of_type = jnp.sum(table[...].astype(F32) * picked, axis=1)
    tall[...] = jnp.zeros_like(tall)
    for lq in range(WPL):
        for lk in range(WPL):
            for a in range(WLAT):
                start = ((lq * WPL + lk) * WLAT + a) * WLAT * SPREAD
                row = (lq * WLAT + a) * heads
                tall[row : row + heads, lk * 256 : lk * 256 + WLAT * SPREAD] = rows_of_type[:, start : start + WLAT * SPREAD]
    laid = nt(order[...], tall[...].astype(BF)).astype(BF)
    folded[...] = nn(laid, reorder[...])
    lane = lax.rem(lax.broadcasted_iota(jnp.int32, (1, span), 1), ROWS)
    sub = lax.rem(lax.broadcasted_iota(jnp.int32, (WINDOW, 1), 0), ROWS)
    id_q = jnp.zeros((1, span), jnp.int32)
    id_k = jnp.zeros((WINDOW, 1), jnp.int32)
    for l in range(WPL):
        for a in range(WLAT):
            value = ids[l, a]
            id_q = jnp.where(lane == l * WLAT + a, value, id_q)
            id_k = jnp.where(sub == l * WLAT + a, value, id_k)
    masked = jnp.where(id_k == id_q, 0.0, -1e30)
    for g in range(groups):
        pieces = [
            folded[(WLON - 1 - o) * ROWS : (WLON - 1 - o) * ROWS + WINDOW, g * GROUP * ROWS : (g + 1) * GROUP * ROWS]
            for o in range(WLON)
        ]
        spread = jnp.concatenate(pieces, axis=1).astype(BF)
        bias[g] = nn(spread, perm[...]) * LOG2E + masked

    gain = gain_v[...].reshape(1, channels)
    shift = shift_v[...].reshape(1, channels)
    for load in loads[4:]:
        load.wait()
    for copy in halos[:3]:
        copy.wait_recv()
    x_in = nn(route[:, :main], cat[..., :channels].reshape(main, channels))
    x_in = x_in + nn(route[:, main:], edge[..., :channels].reshape(-1, channels))
    average = jnp.mean(x_in, axis=1, keepdims=True)
    centred = x_in - average
    variance = jnp.mean(centred * centred, axis=1, keepdims=True)
    inv_std = lax.rsqrt(variance + EPSILON)
    inv[...] = inv_std
    norm = centred * inv_std
    normed[...] = norm
    ln_out = (norm * gain + shift).astype(BF)
    ln[...] = ln_out
    ln_t[...] = ln_out.T
    qkv[...] = nn(ln[...], w_qkv[...]).astype(BF)
    for copy in halos[3:]:
        copy.wait_recv()
    moved = nn(route[:, :main], cat[..., channels:].reshape(main, channels))
    moved = moved + nn(route[:, main:], edge[..., channels:].reshape(-1, channels))
    cot[...] = moved.astype(BF)
    d_att[...] = nt(cot[...], w_proj[...]).astype(BF)

    lanes = lax.broadcasted_iota(jnp.int32, (1, 128), 1) // head_dim
    own = [(lanes == h).astype(F32).astype(BF) for h in range(GROUP)]
    eye = (
        lax.broadcasted_iota(jnp.int32, (128, 128), 0) == lax.broadcasted_iota(jnp.int32, (128, 128), 1)
    ).astype(F32).astype(BF)

    def attend(g, w):
        rows = pl.ds(pl.multiple_of(w * WINDOW, WINDOW), WINDOW)
        q_cols, k_cols, v_cols = (slice((3 * g + b) * 128, (3 * g + b + 1) * 128) for b in range(3))
        cols = slice(g * 128, (g + 1) * 128)
        q, k, v, da = qkv[rows, q_cols], qkv[rows, k_cols], qkv[rows, v_cols], d_att[rows, cols]
        q_heads = jnp.concatenate([q * own[h] for h in range(GROUP)], axis=0)
        da_heads = jnp.concatenate([da * own[h] for h in range(GROUP)], axis=0)
        raised = jnp.exp2(nt(k, q_heads) * (scale * LOG2E) + bias[g])
        probs = raised * (1.0 / jnp.sum(raised, axis=0, keepdims=True))
        probs_b = probs.astype(BF)
        v_t = nt(eye, v).astype(BF)
        k_t = nt(eye, k).astype(BF)
        weighted = probs * nt(v, da_heads)
        d_scores = weighted - probs * jnp.sum(weighted, axis=0, keepdims=True)
        d_scores_b = d_scores.astype(BF)
        mask = blocks[...]
        att_t = nn(v_t, probs_b).astype(BF) * mask
        dq_t = (nn(k_t, d_scores_b) * scale).astype(BF) * mask

        def store():
            att[rows, cols] = nt(gather[...], att_t).astype(BF)
            d_qkv[rows, q_cols] = nt(gather[...], dq_t).astype(BF)
            d_qkv[rows, k_cols] = (nn(d_scores_b, q_heads) * scale).astype(BF)
            d_qkv[rows, v_cols] = nn(probs_b, da_heads).astype(BF)

        return d_scores, store

    def two_windows(g, w):
        left, store_left = attend(g, w)
        right, store_right = attend(g, w + 1)
        store_left()
        store_right()
        return left + right

    def gradients(g):
        weights = nn(ln_t[...], d_qkv[:, 3 * g * 128 : 3 * (g + 1) * 128]).astype(BF)
        for b in range(3):
            grads[g, b] = weights[:, b * 128 : (b + 1) * 128]
        proj = tn(att[:, g * 128 : (g + 1) * 128], cot[...]).astype(BF)
        for t in range(groups):
            grads[g, 3, t * 128 : (t + 1) * 128] = proj[:, t * 128 : (t + 1) * 128]
        high = d_bias[...].astype(BF)
        low = (d_bias[...] - high.astype(F32)).astype(BF)
        spread = nt(high, perm[...]) + nt(low, perm[...])
        folded[:, :128] = jnp.zeros((folded.shape[0], 128), F32)
        for o in range(WLON):
            start = (WLON - 1 - o) * ROWS
            folded[start : start + WINDOW, : GROUP * ROWS] += spread[:, o * GROUP * ROWS : (o + 1) * GROUP * ROWS]
        rows = tn(folded[:, : GROUP * ROWS].astype(BF), order[...])
        rest = WLAT * SPREAD - 128
        ends = jnp.concatenate([rows[:, 128 : 128 + rest], rows[:, 384 : 384 + rest]], axis=1)
        count = GROUP * ROWS // UNIT
        packed = [ends[i * UNIT : (i + 1) * UNIT] for i in range(count)]
        packed = jnp.concatenate([*packed, jnp.zeros((UNIT, 128 - count * 2 * rest), F32)], axis=1)
        laid = jnp.concatenate(
            [rows[:, :128], rows[:, 256:384], packed, jnp.zeros((16 * UNIT - (2 * count + 1) * UNIT, 128), F32)], axis=0
        ).astype(BF)
        for j in range(4):
            tables[g, j] = laid[j * 2 * SLOT : (j + 1) * 2 * SLOT]

    p1 = jnp.where(core == 0, x, y)
    p2 = jnp.where(core == 0, y, x)

    def on1(p):
        return device(jnp.where(core == 0, p, x), jnp.where(core == 0, y, p), z, core)

    def on2(p):
        return device(jnp.where(core == 0, x, p), jnp.where(core == 0, p, y), z, core)

    def after1(i):
        return lax.rem(p1 + i, 4)

    def after2(i):
        return lax.rem(p2 + i, 4)

    def core_copy(g):
        return remote(grads.at[g, pl.ds(2 * other, 2)], core_in.at[g], core_s.at[g], core_r.at[g], sibling)

    def s1_copy(g, peer):
        return remote(s1_out.at[g, peer], s1_in.at[g, p1], s1_s.at[g, peer], s1_r.at[g, p1], on1(peer))

    def s1_take(g, peer):
        return remote(s1_out.at[g, peer], s1_in.at[g, peer], s1_s.at[g, peer], s1_r.at[g, peer], on1(peer))

    def s2_copy(g, peer):
        return remote(s2_out.at[g, peer], s2_in.at[g, p2], s2_s.at[g, peer], s2_r.at[g, p2], on2(peer))

    def s2_take(g, peer):
        return remote(s2_out.at[g, peer], s2_in.at[g, peer], s2_s.at[g, peer], s2_r.at[g, peer], on2(peer))

    def z_copy(g, peer, slot):
        return remote(z_in.at[g, slot], z_in.at[g, slot], z_s.at[g, peer], z_r.at[g, slot], device(x, y, peer, core))

    def g2_copy(g, peer, slot):
        here = full.at[g, core, p1, slot]
        return remote(here, here, g2_s.at[g, peer], g2_r.at[g, slot], on2(peer))

    def g1_copy(g, peer, slot):
        here = full.at[g, core, slot]
        return remote(here, here, g1_s.at[g, peer], g1_r.at[g, slot], on1(peer))

    def sib_copy(g, half, slot):
        here = full.at[g, half, slot]
        return remote(here, here, sib_s.at[g, slot], sib_r.at[g, slot], sibling)

    def step0(g):
        core_copy(g).start()

    def step1(g):
        core_copy(g).wait_recv()
        def fill(j):
            half = j // 2
            rows = pl.ds(pl.multiple_of((j - 2 * half) * PART, PART), PART)
            added = grads[g, 2 * core + half, rows].astype(F32) + core_in[g, half, rows].astype(F32)
            s1_out[g, j, :PART] = added.astype(BF)
            s1_out[g, j, PART:] = tables[g, j]

        for i in (2, 1, 3):
            fill(after1(i))
            s1_copy(g, after1(i)).start()
        fill(p1)

    def step2(g):
        def split(part, source):
            high = jnp.where(core == 0, y, source) // 2
            low_rows = jnp.where(high == 0, part[PART:], jnp.zeros_like(part[PART:]))
            return part[:PART], low_rows, part[PART:] - low_rows

        w, t0, t1 = split(s1_out[g, p1].astype(F32), p1)
        for i in (1, 3, 2):
            source = after1(i)
            s1_take(g, source).wait_recv()
            more = split(s1_in[g, source].astype(F32), source)
            w, t0, t1 = w + more[0], t0 + more[1], t1 + more[2]
        for j in range(4):
            s2_out[g, j] = jnp.concatenate(
                [w[j * PIECE : (j + 1) * PIECE], t0[j * UNIT : (j + 1) * UNIT], t1[j * UNIT : (j + 1) * UNIT]], axis=0
            ).astype(BF)
        for i in (2, 1, 3):
            s2_copy(g, after2(i)).start()

    def step3(g):
        total = s2_out[g, p2].astype(F32)
        for i in (1, 3, 2):
            source = after2(i)
            s2_take(g, source).wait_recv()
            total = total + s2_in[g, source].astype(F32)
        z_in[g, z] = total.astype(BF)
        for i in (4, 3, 5, 2, 6, 1, 7):
            z_copy(g, lax.rem(z + i, Z_SIZE), z).start()

    def step4(g):
        for i in (1, 7, 2, 6, 3, 5, 4):
            source = lax.rem(z + i, Z_SIZE)
            z_copy(g, source, source).wait_recv()
        total = z_in[g, 0].astype(F32)
        for i in range(1, Z_SIZE):
            total = total + z_in[g, i].astype(F32)
        full[g, core, p1, p2] = total.astype(BF)
        for i in (2, 1, 3):
            g2_copy(g, after2(i), p2).start()

    def step5(g):
        for i in (1, 3, 2):
            source = after2(i)
            g2_copy(g, source, source).wait_recv()
        for i in (2, 1, 3):
            g1_copy(g, after1(i), p1).start()
        sib_copy(g, core, p1).start()

    def step6(g):
        for i in (1, 3, 2):
            source = after1(i)
            g1_copy(g, source, source).wait_recv()
            sib_copy(g, core, source).start()

    def step7(g):
        for i in range(4):
            sib_copy(g, other, i).wait_recv()
        full_copy(g).start()

    def full_copy(g):
        return pltpu.make_async_copy(full.at[g], o_full.at[g], out_s.at[g])

    def tokens_copy():
        return pltpu.make_async_copy(joined, o_tokens, out_s.at[groups])

    def finish(g):
        core_copy(g).wait_send()
        for i in range(1, 4):
            s1_copy(g, after1(i)).wait_send()
            s2_copy(g, after2(i)).wait_send()
            g2_copy(g, after2(i), p2).wait_send()
            g1_copy(g, after1(i), p1).wait_send()
        for i in range(1, Z_SIZE):
            z_copy(g, lax.rem(z + i, Z_SIZE), z).wait_send()
        for i in range(4):
            sib_copy(g, core, i).wait_send()

    def mc_copy():
        return remote(small, small_core, mc_s.at[0], mc_r.at[0], sibling)

    def mx_copy(peer, slot):
        return remote(small_x.at[slot], small_x.at[slot], mx_s.at[peer], mx_r.at[slot], device(peer, y, z, core))

    def my_copy(peer, slot):
        return remote(small_y.at[slot], small_y.at[slot], my_s.at[peer], my_r.at[slot], device(x, peer, z, core))

    def mz_copy(peer, slot):
        return remote(small_z.at[slot], small_z.at[slot], mz_s.at[peer], mz_r.at[slot], device(x, y, peer, core))

    def small_share(copy, buffer, place_here, size, value):
        buffer[place_here] = value
        for i in range(1, size):
            copy(lax.rem(place_here + i, size), place_here).start()

    def small_sum(copy, buffer, place_here, size):
        for i in range(1, size):
            source = lax.rem(place_here + i, size)
            copy(source, source).wait_recv()
        total = buffer[0]
        for i in range(1, size):
            total = total + buffer[i]
        return total

    def small_finish():
        mc_copy().wait_send()
        for copy, here, size in ((mx_copy, x, X_SIZE), (my_copy, y, Y_SIZE), (mz_copy, z, Z_SIZE)):
            for i in range(1, size):
                copy(lax.rem(here + i, size), here).wait_send()

    def group(g, between):
        d_bias[...] = two_windows(g, 0)
        between()
        d_bias[...] += two_windows(g, 2)
        gradients(g)
        step0(g)

    def mid1():
        step1(0)

    def mid2():
        step1(1)
        step2(0)

    group(0, lambda: None)
    group(1, mid1)
    group(2, mid2)
    step3(0)
    step2(1)
    step1(2)

    d_ln = nt(d_qkv[...], w_qkv[...])
    norm = normed[...]
    small[...] = jnp.zeros_like(small)
    for g in range(groups):
        cols = slice(g * 128, (g + 1) * 128)
        small[g : g + 1] = jnp.sum(d_ln[:, cols] * norm[:, cols], axis=0, keepdims=True)
        small[groups + g : groups + g + 1] = jnp.sum(d_ln[:, cols], axis=0, keepdims=True)
    mc_copy().start()
    scaled = d_ln * gain
    d_flat = inv[...] * (
        scaled
        - jnp.mean(scaled, axis=1, keepdims=True)
        - norm * jnp.mean(scaled * norm, axis=1, keepdims=True)
    )
    d_flat = d_flat.astype(BF)
    d_main[...] = nn(unroute[:main], d_flat).astype(BF).reshape(d_main.shape)
    d_edge[...] = nn(unroute[main:], d_flat).astype(BF).reshape(d_edge.shape)
    backs = [
        remote(d_main.at[1], back_main, back_s.at[0], back_r.at[0], device(x, y_down, z, other)),
        remote(d_edge.at[0], back_edge.at[0], back_s.at[1], back_r.at[1], device(beside, y, z, core)),
        remote(d_edge.at[1], back_edge.at[1], back_s.at[2], back_r.at[2], device(beside, y_down, z, other)),
    ]
    for copy in backs:
        copy.start()
    step3(1)
    step2(2)
    mc_copy().wait_recv()
    small_share(mx_copy, small_x, x, X_SIZE, small[...] + small_core[...])
    step4(0)
    step3(2)
    small_share(my_copy, small_y, y, Y_SIZE, small_sum(mx_copy, small_x, x, X_SIZE))
    step5(0)
    small_share(mz_copy, small_z, z, Z_SIZE, small_sum(my_copy, small_y, y, Y_SIZE))

    for copy in backs:
        copy.wait_recv()
    for l in range(WPL):
        for a in range(WLAT):
            if a < half_lat:
                inner, outer = back_main[l, a], back_edge[1, l, a]
            else:
                inner, outer = d_main[0, l, a - half_lat], back_edge[0, l, a - half_lat]
            value = cot_own[l, a].astype(F32) + inner.astype(F32)
            joined[l, a, EDGE:] = value[EDGE:].astype(BF)
            joined[l, a, :EDGE] = (value[:EDGE] + outer.astype(F32)).astype(BF)
    tokens_copy().start()
    step4(1)
    step6(0)
    step4(2)
    step5(1)
    step7(0)
    o_small[...] = small_sum(mz_copy, small_z, z, Z_SIZE)
    step5(2)
    step6(1)
    step7(1)
    step6(2)
    step7(2)

    for copy in halos + backs:
        copy.wait_send()
    for g in range(groups):
        finish(g)
    small_finish()
    tokens_copy().wait()
    for g in range(groups):
        full_copy(g).wait()


def assemble_kernel(
    types, full_h, joined_h, small, reorder,
    o_tokens, o_qkv, o_proj, o_table, o_gain, o_shift,
    full, wide, typed, sem,
):
    channels = o_proj.shape[0]
    groups = channels // 128
    heads = groups * GROUP
    loads = [pltpu.make_async_copy(full_h.at[g], full.at[g], sem.at[g]) for g in range(groups)]
    through = pltpu.make_async_copy(joined_h, o_tokens, sem.at[groups])
    for load in loads:
        load.start()
    through.start()
    o_gain[...] = jnp.concatenate([small[g : g + 1] for g in range(groups)], axis=1).reshape(channels)
    o_shift[...] = jnp.concatenate([small[g : g + 1] for g in range(groups, 2 * groups)], axis=1).reshape(channels)
    for g in range(groups):
        loads[g].wait()
        for half in range(2):
            for j in range(4):
                for i in range(4):
                    part = full[g, half, j, i, :PIECE]
                    block = 2 * half + j // 2
                    row = (j % 2) * PART + i * PIECE
                    if block < 3:
                        cols = slice(block * channels + g * 128, block * channels + (g + 1) * 128)
                        o_qkv[row : row + PIECE, cols] = part
                    else:
                        for u in range(0, PIECE, SLOT):
                            at = row + u
                            tile = at // 128
                            o_proj[g * 128 + at % 128 : g * 128 + at % 128 + SLOT, tile * 128 : (tile + 1) * 128] = (
                                part[u : u + SLOT]
                            )

    count = GROUP * ROWS // UNIT
    rest = WLAT * SPREAD - 128
    for b in range(4):
        at = (b // 2) * UNIT
        units = [
            [full[g, b % 2, u // 4, u % 4, PIECE:].astype(F32)[at : at + UNIT] for u in range(2 * count + 1)]
            for g in range(groups)
        ]
        for t in range(2):
            tile = jnp.concatenate([u for g in range(groups) for u in units[g][t * count : (t + 1) * count]], axis=0)
            wide[b, :, t * 256 : t * 256 + 128] = nn(reorder[...], tile.astype(BF))
        ends = jnp.concatenate(
            [units[g][2 * count][:, i * 2 * rest : (i + 1) * 2 * rest] for g in range(groups) for i in range(count)],
            axis=0,
        )
        ends = nn(reorder[...], ends.astype(BF))
        wide[b, :, 128 : 128 + rest] = ends[:, :rest]
        wide[b, :, 384 : 384 + rest] = ends[:, rest:]
    for kind in range(4):
        band = jnp.int32(0)
        for b in range(1, 4):
            band = jnp.where(types[b] == kind, b, band)
        table_rows = wide[band]
        parts = []
        for lq in range(WPL):
            for lk in range(WPL):
                for a in range(WLAT):
                    row = (lq * WLAT + a) * heads
                    parts.append(table_rows[row : row + heads, lk * 256 : lk * 256 + WLAT * SPREAD])
        typed[:, kind, :] = jnp.concatenate(parts, axis=1)
    o_table[...] = typed[...].astype(BF)
    through.wait()


def local(tokens, cotangent, mask_ids, band_type, bias_table, w_qkv, w_proj, ln_gain, ln_shift):
    lon_cols, channels = tokens.shape[2:]
    groups = channels // 128
    heads = groups * GROUP
    half_lat = WLAT // 2
    count = WPL * WLAT * lon_cols
    span = GROUP * WINDOW
    route = token_route(lon_cols)
    constants = [
        jnp.asarray(c, BF)
        for c in (
            route, route.T, head_order(), table_order(), head_blocks(128 // GROUP), gather_heads(), row_order(heads)
        )
    ]
    anywhere = pl.BlockSpec(memory_space=pl.ANY)
    scalars = pl.BlockSpec(memory_space=pltpu.SMEM)
    vmem = pl.BlockSpec(memory_space=pltpu.VMEM)
    dma = pltpu.SemaphoreType.DMA
    bf = lambda *shape: pltpu.VMEM(shape, BF)
    f32 = lambda *shape: pltpu.VMEM(shape, F32)
    pairs = lambda *shape: [dma(shape), dma(shape)]
    pieces = (groups, 2, 4, 4, PIECE + SLOT, 128)
    table = bias_table.transpose(1, 0, 2)
    joined, full, small = pl.pallas_call(
        whole_kernel,
        out_shape=(
            jax.ShapeDtypeStruct(tokens.shape, BF),
            jax.ShapeDtypeStruct(pieces, BF),
            jax.ShapeDtypeStruct((8, 128), F32),
        ),
        in_specs=[scalars] * 2 + [anywhere] * 5 + [vmem] * 2 + [anywhere] * 7,
        out_specs=(anywhere, anywhere, vmem),
        scratch_shapes=[
            bf(2, WPL, half_lat, lon_cols, 2 * channels),
            bf(2, WPL, half_lat, EDGE, 2 * channels),
            bf(*tokens.shape),
            bf(*tokens.shape),
            bf(*table.shape),
            bf(channels, 3 * channels),
            bf(channels, channels),
            *[bf(*c.shape) for c in constants],
            f32(heads * ROWS, 512),
            f32(SPREAD * ROWS, heads * ROWS),
            f32(groups, WINDOW, span),
            f32(WINDOW, span),
            f32(count, channels),
            f32(count, 1),
            bf(count, channels),
            bf(channels, count),
            bf(count, channels),
            bf(count, 3 * channels),
            bf(count, channels),
            bf(count, channels),
            bf(count, 3 * channels),
            bf(2, WPL, half_lat, lon_cols, channels),
            bf(2, WPL, half_lat, EDGE, channels),
            bf(WPL, half_lat, lon_cols, channels),
            bf(2, WPL, half_lat, EDGE, channels),
            bf(groups, 4, channels, 128),
            bf(groups, 4, 2 * SLOT, 128),
            bf(groups, 2, channels, 128),
            bf(groups, 4, PART + 2 * SLOT, 128),
            bf(groups, 4, PART + 2 * SLOT, 128),
            bf(groups, 4, PIECE + SLOT, 128),
            bf(groups, 4, PIECE + SLOT, 128),
            bf(groups, Z_SIZE, PIECE + SLOT, 128),
            bf(*pieces),
            f32(8, 128),
            f32(8, 128),
            f32(X_SIZE, 8, 128),
            f32(Y_SIZE, 8, 128),
            f32(Z_SIZE, 8, 128),
            dma((12 + 3 * groups,)),
            dma((groups + 1,)),
            *pairs(6), *pairs(3), *pairs(groups), *pairs(groups, 4), *pairs(groups, 4), *pairs(groups, Z_SIZE),
            *pairs(groups, 4), *pairs(groups, 4), *pairs(groups, 4),
            *pairs(1), *pairs(X_SIZE), *pairs(Y_SIZE), *pairs(Z_SIZE),
        ],
        compiler_params=pltpu.CompilerParams(
            collective_id=0, has_side_effects=True, vmem_limit_bytes=56 * 1024 * 1024
        ),
        cost_estimate=pl.CostEstimate(flops=6_000_000_000, bytes_accessed=10_000_000, transcendentals=1_000_000),
    )(mask_ids, band_type, tokens, cotangent, table, w_qkv, w_proj, ln_gain, ln_shift, *constants)
    d_tokens, g_qkv, g_proj, g_table, g_gain, g_shift = pl.pallas_call(
        assemble_kernel,
        out_shape=(
            jax.ShapeDtypeStruct(tokens.shape, BF),
            jax.ShapeDtypeStruct((channels, 3 * channels), BF),
            jax.ShapeDtypeStruct((channels, channels), BF),
            jax.ShapeDtypeStruct(table.shape, BF),
            jax.ShapeDtypeStruct((channels,), F32),
            jax.ShapeDtypeStruct((channels,), F32),
        ),
        in_specs=[scalars, anywhere, anywhere, vmem, vmem],
        out_specs=(anywhere, vmem, vmem, vmem, vmem, vmem),
        scratch_shapes=[
            bf(*pieces),
            f32(4, heads * ROWS, 512),
            f32(*table.shape),
            dma((groups + 1,)),
        ],
        compiler_params=pltpu.CompilerParams(vmem_limit_bytes=60 * 1024 * 1024),
        cost_estimate=pl.CostEstimate(flops=100_000_000, bytes_accessed=6_000_000, transcendentals=0),
    )(band_type, full, joined, small, constants[-1])
    return d_tokens, g_qkv, g_proj, g_gain, g_shift, g_table.transpose(1, 0, 2)


def solution(mesh):
    placed = (P(None, "lat", "lon", None),) * 2 + (P(None, "lat"),) + (P(),) * 6
    return jax.shard_map(
        local,
        mesh=mesh,
        in_specs=placed,
        out_specs=(P(None, "lat", "lon", None), P(), P(), P(), P(), P()),
        check_vma=False,
    )
```

```python
import jax
import jax.numpy as jnp
import numpy as np
from jax import lax
from jax.experimental import pallas as pl
from jax.experimental.pallas import tpu as pltpu
from jax.sharding import PartitionSpec as P

WPL, WLAT, WLON = 2, 6, 12
WINDOW = WPL * WLAT * WLON
ROWS = WPL * WLAT
SPREAD = 2 * WLON - 1
EDGE = 16
X_SIZE, Y_SIZE, Z_SIZE = 4, 4, 8
PART = 192
PIECE = 48
SLOT = 16
UNIT = 8
MESH = pl.DeviceIdType.MESH
GROUP = 4
EPSILON = 1e-05
LOG2E = 1.4426950408889634
BF = jnp.bfloat16
F32 = jnp.float32


def token_route(lon_cols):
    half_lat, half_lon = WLAT // 2, WLON // 2
    windows = lon_cols // WLON
    near = WPL * half_lat * lon_cols
    far = WPL * half_lat * EDGE
    route = np.zeros((windows * WINDOW, 2 * near + 2 * far), np.float32)
    for w in range(windows):
        for o in range(WLON):
            for l in range(WPL):
                for a in range(WLAT):
                    level = (l + 1) % WPL
                    col = w * WLON + o + half_lon
                    row = level * half_lat + a % half_lat
                    if col < lon_cols:
                        source = row * lon_cols + col + (near if a >= half_lat else 0)
                    else:
                        source = 2 * near + row * EDGE + col - lon_cols
                        source += far if a >= half_lat else 0
                    route[w * WINDOW + o * ROWS + l * WLAT + a, source] = 1.0
    return route


def head_order():
    perm = np.zeros((GROUP * WINDOW, GROUP * WINDOW), np.float32)
    for o in range(WLON):
        for h in range(GROUP):
            for r in range(ROWS):
                perm[(o * GROUP + h) * ROWS + r, (h * WLON + o) * ROWS + r] = 1.0
    return perm


def table_order():
    order = np.zeros((SPREAD * ROWS, 512), np.float32)
    for d in range(SPREAD):
        for l in range(WPL):
            for a in range(WLAT):
                order[(SPREAD - 1 - d) * ROWS + l * WLAT + a, l * 256 + a * SPREAD + d] = 1.0
    return order


def row_order(heads):
    order = np.zeros((heads * ROWS, heads * ROWS), np.float32)
    for h in range(heads):
        for r in range(ROWS):
            order[r * heads + h, h * ROWS + r] = 1.0
    return order


def head_blocks(head_dim):
    rows = np.arange(GROUP * head_dim)[:, None] // head_dim
    cols = np.arange(GROUP * WINDOW)[None, :] // WINDOW
    return (rows == cols).astype(np.float32)


def gather_heads():
    return np.tile(np.eye(WINDOW, dtype=np.float32), (1, GROUP))


def nn(a, b):
    return lax.dot_general(a, b, (((1,), (0,)), ((), ())), preferred_element_type=F32)


def nt(a, b):
    return lax.dot_general(a, b, (((1,), (1,)), ((), ())), preferred_element_type=F32)


def tn(a, b):
    return lax.dot_general(a, b, (((0,), (0,)), ((), ())), preferred_element_type=F32)


def place():
    lon = lax.axis_index("lon")
    lat = lax.axis_index("lat")
    x = lax.rem(lon, X_SIZE)
    z = lax.rem(lon // X_SIZE, Z_SIZE)
    y = (lat // 2) * 2 + lon // (X_SIZE * Z_SIZE)
    return x, y, z, lax.rem(lat, 2)


def device(x, y, z, core):
    return ((lax.rem(y, 2) * Z_SIZE + z) * X_SIZE + x, (y // 2) * 2 + core)


def whole_kernel(
    ids, types, tokens, cotangent, table_h, w_qkv_h, w_proj_h, gain_v, shift_v,
    route_h, unroute_h, perm_h, order_h, blocks_h, gather_h, reorder_h,
    o_tokens, o_full, o_small,
    cat, edge, cot_own, joined, table, w_qkv, w_proj, route, unroute, perm, order, blocks, gather, reorder,
    tall, folded, bias, d_bias, normed, inv, ln, ln_t, cot, qkv, d_att, att, d_qkv,
    d_main, d_edge, back_main, back_edge,
    grads, tables, core_in, s1_out, s1_in, s2_out, s2_in, z_in, full, small, small_core, small_x, small_y, small_z,
    load_s, out_s, halo_s, halo_r, back_s, back_r, core_s, core_r, s1_s, s1_r, s2_s, s2_r, z_s, z_r, g2_s, g2_r, g1_s, g1_r,
    sib_s, sib_r, mc_s, mc_r, mx_s, mx_r, my_s, my_r, mz_s, mz_r,
):
    half_lat = WLAT // 2
    half_lon = WLON // 2
    lon_cols = tokens.shape[2]
    channels = tokens.shape[3]
    main = 2 * WPL * half_lat * lon_cols
    groups = channels // 128
    heads = groups * GROUP
    windows = lon_cols // WLON
    span = GROUP * WINDOW
    head_dim = 128 // GROUP
    scale = head_dim ** -0.5
    x, y, z, core = place()
    other = 1 - core
    beside = x + 1 - 2 * lax.rem(x, 2)
    across = lax.rem(y + 2, Y_SIZE)
    y_up = lax.rem(y + 2 * other, Y_SIZE)
    y_down = lax.rem(y + 2 * core, Y_SIZE)
    sibling = device(x, y, z, other)

    loads = [
        pltpu.make_async_copy(src, dst, load_s.at[i])
        for i, (src, dst) in enumerate((
            (table_h, table), (order_h, order), (reorder_h, reorder), (perm_h, perm),
            (tokens.at[:, pl.ds(half_lat, half_lat)], cat.at[0, :, :, :, pl.ds(0, channels)]),
            (cotangent.at[:, pl.ds(half_lat, half_lat)], cat.at[0, :, :, :, pl.ds(channels, channels)]),
            (route_h, route), (w_proj_h, w_proj), (blocks_h, blocks), (gather_h, gather),
            (unroute_h, unroute), (cotangent, cot_own),
            *(
                (
                    w_qkv_h.at[:, pl.ds(b * channels + g * 128, 128)],
                    w_qkv.at[:, pl.ds((3 * g + b) * 128, 128)],
                )
                for g in range(groups)
                for b in range(3)
            ),
        ))
    ]
    barrier = pltpu.get_barrier_semaphore()
    friends = [sibling, device(x, across, z, other), device(beside, y, z, other), device(beside, across, z, other)]
    friends += [device(lax.rem(x + i, X_SIZE), y, z, core) for i in range(1, X_SIZE)]
    friends += [device(x, lax.rem(y + i, Y_SIZE), z, core) for i in range(1, Y_SIZE)]
    friends += [device(x, y, lax.rem(z + i, Z_SIZE), core) for i in range(1, Z_SIZE)]
    for friend in friends:
        pl.semaphore_signal(barrier, inc=1, device_id=friend, device_id_type=MESH)
    for load in loads:
        load.start()
    pl.semaphore_wait(barrier, len(friends))

    def remote(src, dst, send, recv, target):
        return pltpu.make_async_remote_copy(
            src_ref=src, dst_ref=dst, send_sem=send, recv_sem=recv, device_id=target, device_id_type=MESH
        )

    first, last = pl.ds(0, half_lat), pl.ds(half_lat, half_lat)
    halos = []
    for i, array in enumerate((tokens, cotangent)):
        lanes = pl.ds(i * channels, channels)
        up = device(x, y_up, z, other)
        halos += [
            (array.at[:, first], cat.at[1, :, :, :, lanes], up),
            (array.at[:, last, pl.ds(0, EDGE)], edge.at[0, :, :, :, lanes], device(beside, y, z, core)),
            (array.at[:, first, pl.ds(0, EDGE)], edge.at[1, :, :, :, lanes], device(beside, y_up, z, other)),
        ]
    halos = [remote(src, dst, halo_s.at[i], halo_r.at[i], to) for i, (src, dst, to) in enumerate(halos)]
    for copy in halos:
        copy.start()

    for load in loads[:4]:
        load.wait()
    own_type = types[lax.axis_index("lat")]
    picked = (lax.broadcasted_iota(jnp.int32, (1, 4, 1), 1) == own_type).astype(F32)
    rows_of_type = jnp.sum(table[...].astype(F32) * picked, axis=1)
    tall[...] = jnp.zeros_like(tall)
    for lq in range(WPL):
        for lk in range(WPL):
            for a in range(WLAT):
                start = ((lq * WPL + lk) * WLAT + a) * WLAT * SPREAD
                row = (lq * WLAT + a) * heads
                tall[row : row + heads, lk * 256 : lk * 256 + WLAT * SPREAD] = rows_of_type[:, start : start + WLAT * SPREAD]
    laid = nt(order[...], tall[...].astype(BF)).astype(BF)
    folded[...] = nn(laid, reorder[...])
    lane = lax.rem(lax.broadcasted_iota(jnp.int32, (1, span), 1), ROWS)
    sub = lax.rem(lax.broadcasted_iota(jnp.int32, (WINDOW, 1), 0), ROWS)
    id_q = jnp.zeros((1, span), jnp.int32)
    id_k = jnp.zeros((WINDOW, 1), jnp.int32)
    for l in range(WPL):
        for a in range(WLAT):
            value = ids[l, a]
            id_q = jnp.where(lane == l * WLAT + a, value, id_q)
            id_k = jnp.where(sub == l * WLAT + a, value, id_k)
    masked = jnp.where(id_k == id_q, 0.0, -1e30)
    for g in range(groups):
        pieces = [
            folded[(WLON - 1 - o) * ROWS : (WLON - 1 - o) * ROWS + WINDOW, g * GROUP * ROWS : (g + 1) * GROUP * ROWS]
            for o in range(WLON)
        ]
        spread = jnp.concatenate(pieces, axis=1).astype(BF)
        bias[g] = nn(spread, perm[...]) * LOG2E + masked

    gain = gain_v[...].reshape(1, channels)
    shift = shift_v[...].reshape(1, channels)
    for load in loads[4:]:
        load.wait()
    for copy in halos[:3]:
        copy.wait_recv()
    x_in = nn(route[:, :main], cat[..., :channels].reshape(main, channels))
    x_in = x_in + nn(route[:, main:], edge[..., :channels].reshape(-1, channels))
    average = jnp.mean(x_in, axis=1, keepdims=True)
    centred = x_in - average
    variance = jnp.mean(centred * centred, axis=1, keepdims=True)
    inv_std = lax.rsqrt(variance + EPSILON)
    inv[...] = inv_std
    norm = centred * inv_std
    normed[...] = norm
    ln_out = (norm * gain + shift).astype(BF)
    ln[...] = ln_out
    ln_t[...] = ln_out.T
    qkv[...] = nn(ln[...], w_qkv[...]).astype(BF)
    for copy in halos[3:]:
        copy.wait_recv()
    moved = nn(route[:, :main], cat[..., channels:].reshape(main, channels))
    moved = moved + nn(route[:, main:], edge[..., channels:].reshape(-1, channels))
    cot[...] = moved.astype(BF)
    d_att[...] = nt(cot[...], w_proj[...]).astype(BF)

    lanes = lax.broadcasted_iota(jnp.int32, (1, 128), 1) // head_dim
    own = [(lanes == h).astype(F32).astype(BF) for h in range(GROUP)]
    eye = (
        lax.broadcasted_iota(jnp.int32, (128, 128), 0) == lax.broadcasted_iota(jnp.int32, (128, 128), 1)
    ).astype(F32).astype(BF)

    def attend(g, w):
        rows = pl.ds(pl.multiple_of(w * WINDOW, WINDOW), WINDOW)
        q_cols, k_cols, v_cols = (slice((3 * g + b) * 128, (3 * g + b + 1) * 128) for b in range(3))
        cols = slice(g * 128, (g + 1) * 128)
        q, k, v, da = qkv[rows, q_cols], qkv[rows, k_cols], qkv[rows, v_cols], d_att[rows, cols]
        q_heads = jnp.concatenate([q * own[h] for h in range(GROUP)], axis=0)
        da_heads = jnp.concatenate([da * own[h] for h in range(GROUP)], axis=0)
        raised = jnp.exp2(nt(k, q_heads) * (scale * LOG2E) + bias[g])
        probs = raised * (1.0 / jnp.sum(raised, axis=0, keepdims=True))
        probs_b = probs.astype(BF)
        v_t = nt(eye, v).astype(BF)
        k_t = nt(eye, k).astype(BF)
        weighted = probs * nt(v, da_heads)
        d_scores = weighted - probs * jnp.sum(weighted, axis=0, keepdims=True)
        d_scores_b = d_scores.astype(BF)
        mask = blocks[...]
        att_t = nn(v_t, probs_b).astype(BF) * mask
        dq_t = (nn(k_t, d_scores_b) * scale).astype(BF) * mask

        def store():
            att[rows, cols] = nt(gather[...], att_t).astype(BF)
            d_qkv[rows, q_cols] = nt(gather[...], dq_t).astype(BF)
            d_qkv[rows, k_cols] = (nn(d_scores_b, q_heads) * scale).astype(BF)
            d_qkv[rows, v_cols] = nn(probs_b, da_heads).astype(BF)

        return d_scores, store

    def two_windows(g, w):
        left, store_left = attend(g, w)
        right, store_right = attend(g, w + 1)
        store_left()
        store_right()
        return left + right

    def gradients(g):
        weights = nn(ln_t[...], d_qkv[:, 3 * g * 128 : 3 * (g + 1) * 128]).astype(BF)
        for b in range(3):
            grads[g, b] = weights[:, b * 128 : (b + 1) * 128]
        proj = tn(att[:, g * 128 : (g + 1) * 128], cot[...]).astype(BF)
        for t in range(groups):
            grads[g, 3, t * 128 : (t + 1) * 128] = proj[:, t * 128 : (t + 1) * 128]

    def fold(g):
        high = d_bias[...].astype(BF)
        low = (d_bias[...] - high.astype(F32)).astype(BF)
        spread = nt(high, perm[...]) + nt(low, perm[...])
        folded[:, :128] = jnp.zeros((folded.shape[0], 128), F32)
        for o in range(WLON):
            start = (WLON - 1 - o) * ROWS
            folded[start : start + WINDOW, : GROUP * ROWS] += spread[:, o * GROUP * ROWS : (o + 1) * GROUP * ROWS]
        rows = tn(folded[:, : GROUP * ROWS].astype(BF), order[...])
        rest = WLAT * SPREAD - 128
        ends = jnp.concatenate([rows[:, 128 : 128 + rest], rows[:, 384 : 384 + rest]], axis=1)
        count = GROUP * ROWS // UNIT
        packed = [ends[i * UNIT : (i + 1) * UNIT] for i in range(count)]
        packed = jnp.concatenate([*packed, jnp.zeros((UNIT, 128 - count * 2 * rest), F32)], axis=1)
        laid = jnp.concatenate(
            [rows[:, :128], rows[:, 256:384], packed, jnp.zeros((16 * UNIT - (2 * count + 1) * UNIT, 128), F32)], axis=0
        ).astype(BF)
        for j in range(4):
            tables[g, j] = laid[j * 2 * SLOT : (j + 1) * 2 * SLOT]

    p1 = jnp.where(core == 0, x, y)
    p2 = jnp.where(core == 0, y, x)

    def on1(p):
        return device(jnp.where(core == 0, p, x), jnp.where(core == 0, y, p), z, core)

    def on2(p):
        return device(jnp.where(core == 0, x, p), jnp.where(core == 0, p, y), z, core)

    def after1(i):
        return lax.rem(p1 + i, 4)

    def after2(i):
        return lax.rem(p2 + i, 4)

    def core_copy(g):
        return remote(grads.at[g, pl.ds(2 * other, 2)], core_in.at[g], core_s.at[g], core_r.at[g], sibling)

    def s1_copy(g, peer):
        return remote(s1_out.at[g, peer], s1_in.at[g, p1], s1_s.at[g, peer], s1_r.at[g, p1], on1(peer))

    def s1_take(g, peer):
        return remote(s1_out.at[g, peer], s1_in.at[g, peer], s1_s.at[g, peer], s1_r.at[g, peer], on1(peer))

    def s2_copy(g, peer):
        return remote(s2_out.at[g, peer], s2_in.at[g, p2], s2_s.at[g, peer], s2_r.at[g, p2], on2(peer))

    def s2_take(g, peer):
        return remote(s2_out.at[g, peer], s2_in.at[g, peer], s2_s.at[g, peer], s2_r.at[g, peer], on2(peer))

    def z_copy(g, peer, slot):
        return remote(z_in.at[g, slot], z_in.at[g, slot], z_s.at[g, peer], z_r.at[g, slot], device(x, y, peer, core))

    def g2_copy(g, peer, slot):
        here = full.at[g, core, p1, slot]
        return remote(here, here, g2_s.at[g, peer], g2_r.at[g, slot], on2(peer))

    def g1_copy(g, peer, slot):
        here = full.at[g, core, slot]
        return remote(here, here, g1_s.at[g, peer], g1_r.at[g, slot], on1(peer))

    def sib_copy(g, half, slot):
        here = full.at[g, half, slot]
        return remote(here, here, sib_s.at[g, slot], sib_r.at[g, slot], sibling)

    def step0(g):
        core_copy(g).start()

    def step1(g):
        core_copy(g).wait_recv()
        def fill(j):
            half = j // 2
            rows = pl.ds(pl.multiple_of((j - 2 * half) * PART, PART), PART)
            added = grads[g, 2 * core + half, rows].astype(F32) + core_in[g, half, rows].astype(F32)
            s1_out[g, j, :PART] = added.astype(BF)
            s1_out[g, j, PART:] = tables[g, j]

        for i in (2, 1, 3):
            fill(after1(i))
            s1_copy(g, after1(i)).start()
        fill(p1)

    def step2(g):
        def split(part, source):
            high = jnp.where(core == 0, y, source) // 2
            low_rows = jnp.where(high == 0, part[PART:], jnp.zeros_like(part[PART:]))
            return part[:PART], low_rows, part[PART:] - low_rows

        w, t0, t1 = split(s1_out[g, p1].astype(F32), p1)
        for i in (1, 3, 2):
            source = after1(i)
            s1_take(g, source).wait_recv()
            more = split(s1_in[g, source].astype(F32), source)
            w, t0, t1 = w + more[0], t0 + more[1], t1 + more[2]
        for j in range(4):
            s2_out[g, j] = jnp.concatenate(
                [w[j * PIECE : (j + 1) * PIECE], t0[j * UNIT : (j + 1) * UNIT], t1[j * UNIT : (j + 1) * UNIT]], axis=0
            ).astype(BF)
        for i in (2, 1, 3):
            s2_copy(g, after2(i)).start()

    def step3(g):
        total = s2_out[g, p2].astype(F32)
        for i in (1, 3, 2):
            source = after2(i)
            s2_take(g, source).wait_recv()
            total = total + s2_in[g, source].astype(F32)
        z_in[g, z] = total.astype(BF)
        for i in (4, 3, 5, 2, 6, 1, 7):
            z_copy(g, lax.rem(z + i, Z_SIZE), z).start()

    def step4(g):
        for i in (1, 7, 2, 6, 3, 5, 4):
            source = lax.rem(z + i, Z_SIZE)
            z_copy(g, source, source).wait_recv()
        total = z_in[g, 0].astype(F32)
        for i in range(1, Z_SIZE):
            total = total + z_in[g, i].astype(F32)
        full[g, core, p1, p2] = total.astype(BF)
        for i in (2, 1, 3):
            g2_copy(g, after2(i), p2).start()

    def step5(g):
        for i in (1, 3, 2):
            source = after2(i)
            g2_copy(g, source, source).wait_recv()
        for i in (2, 1, 3):
            g1_copy(g, after1(i), p1).start()
        sib_copy(g, core, p1).start()

    def step6(g):
        for i in (1, 3, 2):
            source = after1(i)
            g1_copy(g, source, source).wait_recv()
            sib_copy(g, core, source).start()

    def step7(g):
        for i in range(4):
            sib_copy(g, other, i).wait_recv()
        full_copy(g).start()

    def full_copy(g):
        return pltpu.make_async_copy(full.at[g], o_full.at[g], out_s.at[g])

    def tokens_copy():
        return pltpu.make_async_copy(joined, o_tokens, out_s.at[groups])

    def finish(g):
        core_copy(g).wait_send()
        for i in range(1, 4):
            s1_copy(g, after1(i)).wait_send()
            s2_copy(g, after2(i)).wait_send()
            g2_copy(g, after2(i), p2).wait_send()
            g1_copy(g, after1(i), p1).wait_send()
        for i in range(1, Z_SIZE):
            z_copy(g, lax.rem(z + i, Z_SIZE), z).wait_send()
        for i in range(4):
            sib_copy(g, core, i).wait_send()

    def mc_copy():
        return remote(small, small_core, mc_s.at[0], mc_r.at[0], sibling)

    def mx_copy(peer, slot):
        return remote(small_x.at[slot], small_x.at[slot], mx_s.at[peer], mx_r.at[slot], device(peer, y, z, core))

    def my_copy(peer, slot):
        return remote(small_y.at[slot], small_y.at[slot], my_s.at[peer], my_r.at[slot], device(x, peer, z, core))

    def mz_copy(peer, slot):
        return remote(small_z.at[slot], small_z.at[slot], mz_s.at[peer], mz_r.at[slot], device(x, y, peer, core))

    def small_share(copy, buffer, place_here, size, value):
        buffer[place_here] = value
        for i in range(1, size):
            copy(lax.rem(place_here + i, size), place_here).start()

    def small_sum(copy, buffer, place_here, size):
        for i in range(1, size):
            source = lax.rem(place_here + i, size)
            copy(source, source).wait_recv()
        total = buffer[0]
        for i in range(1, size):
            total = total + buffer[i]
        return total

    def small_finish():
        mc_copy().wait_send()
        for copy, here, size in ((mx_copy, x, X_SIZE), (my_copy, y, Y_SIZE), (mz_copy, z, Z_SIZE)):
            for i in range(1, size):
                copy(lax.rem(here + i, size), here).wait_send()

    def group(g, between):
        d_bias[...] = two_windows(g, 0)
        between()
        d_bias[...] += two_windows(g, 2)
        gradients(g)
        step0(g)
        fold(g)

    def mid1():
        step1(0)

    def mid2():
        step1(1)
        step2(0)

    group(0, lambda: None)
    group(1, mid1)
    group(2, mid2)
    step3(0)
    step1(2)
    step2(1)

    d_ln = nt(d_qkv[...], w_qkv[...])
    norm = normed[...]
    small[...] = jnp.zeros_like(small)
    for g in range(groups):
        cols = slice(g * 128, (g + 1) * 128)
        small[g : g + 1] = jnp.sum(d_ln[:, cols] * norm[:, cols], axis=0, keepdims=True)
        small[groups + g : groups + g + 1] = jnp.sum(d_ln[:, cols], axis=0, keepdims=True)
    mc_copy().start()
    scaled = d_ln * gain
    d_flat = inv[...] * (
        scaled
        - jnp.mean(scaled, axis=1, keepdims=True)
        - norm * jnp.mean(scaled * norm, axis=1, keepdims=True)
    )
    d_flat = d_flat.astype(BF)
    d_main[...] = nn(unroute[:main], d_flat).astype(BF).reshape(d_main.shape)
    d_edge[...] = nn(unroute[main:], d_flat).astype(BF).reshape(d_edge.shape)
    backs = [
        remote(d_main.at[1], back_main, back_s.at[0], back_r.at[0], device(x, y_down, z, other)),
        remote(d_edge.at[0], back_edge.at[0], back_s.at[1], back_r.at[1], device(beside, y, z, core)),
        remote(d_edge.at[1], back_edge.at[1], back_s.at[2], back_r.at[2], device(beside, y_down, z, other)),
    ]
    for copy in backs:
        copy.start()
    step3(1)
    step2(2)
    mc_copy().wait_recv()
    small_share(mx_copy, small_x, x, X_SIZE, small[...] + small_core[...])
    step4(0)
    step3(2)
    small_share(my_copy, small_y, y, Y_SIZE, small_sum(mx_copy, small_x, x, X_SIZE))
    step5(0)
    small_share(mz_copy, small_z, z, Z_SIZE, small_sum(my_copy, small_y, y, Y_SIZE))

    for copy in backs:
        copy.wait_recv()
    for l in range(WPL):
        for a in range(WLAT):
            if a < half_lat:
                inner, outer = back_main[l, a], back_edge[1, l, a]
            else:
                inner, outer = d_main[0, l, a - half_lat], back_edge[0, l, a - half_lat]
            value = cot_own[l, a].astype(F32) + inner.astype(F32)
            joined[l, a, EDGE:] = value[EDGE:].astype(BF)
            joined[l, a, :EDGE] = (value[:EDGE] + outer.astype(F32)).astype(BF)
    tokens_copy().start()
    step4(1)
    step6(0)
    step4(2)
    step5(1)
    step7(0)
    o_small[...] = small_sum(mz_copy, small_z, z, Z_SIZE)
    step5(2)
    step6(1)
    step7(1)
    step6(2)
    step7(2)

    for copy in halos + backs:
        copy.wait_send()
    for g in range(groups):
        finish(g)
    small_finish()
    tokens_copy().wait()
    for g in range(groups):
        full_copy(g).wait()


def assemble_kernel(
    types, full_h, joined_h, small, reorder,
    o_tokens, o_qkv, o_proj, o_table, o_gain, o_shift,
    full, joined, wide, typed, sem,
):
    channels = o_proj.shape[0]
    groups = channels // 128
    heads = groups * GROUP
    loads = [pltpu.make_async_copy(full_h.at[g], full.at[g], sem.at[g]) for g in range(groups)]
    inward = pltpu.make_async_copy(joined_h, joined, sem.at[groups])
    outward = pltpu.make_async_copy(joined, o_tokens, sem.at[groups + 1])
    for load in loads:
        load.start()
    inward.start()
    o_gain[...] = jnp.concatenate([small[g : g + 1] for g in range(groups)], axis=1).reshape(channels)
    o_shift[...] = jnp.concatenate([small[g : g + 1] for g in range(groups, 2 * groups)], axis=1).reshape(channels)
    inward.wait()
    outward.start()
    for g in range(groups):
        loads[g].wait()
        for half in range(2):
            for j in range(4):
                for i in range(4):
                    part = full[g, half, j, i, :PIECE]
                    block = 2 * half + j // 2
                    row = (j % 2) * PART + i * PIECE
                    if block < 3:
                        cols = slice(block * channels + g * 128, block * channels + (g + 1) * 128)
                        o_qkv[row : row + PIECE, cols] = part
                    else:
                        for u in range(0, PIECE, SLOT):
                            at = row + u
                            tile = at // 128
                            o_proj[g * 128 + at % 128 : g * 128 + at % 128 + SLOT, tile * 128 : (tile + 1) * 128] = (
                                part[u : u + SLOT]
                            )

    count = GROUP * ROWS // UNIT
    rest = WLAT * SPREAD - 128
    for b in range(4):
        at = (b // 2) * UNIT
        units = [
            [full[g, b % 2, u // 4, u % 4, PIECE:].astype(F32)[at : at + UNIT] for u in range(2 * count + 1)]
            for g in range(groups)
        ]
        for t in range(2):
            tile = jnp.concatenate([u for g in range(groups) for u in units[g][t * count : (t + 1) * count]], axis=0)
            wide[b, :, t * 256 : t * 256 + 128] = nn(reorder[...], tile.astype(BF))
        ends = jnp.concatenate(
            [units[g][2 * count][:, i * 2 * rest : (i + 1) * 2 * rest] for g in range(groups) for i in range(count)],
            axis=0,
        )
        ends = nn(reorder[...], ends.astype(BF))
        wide[b, :, 128 : 128 + rest] = ends[:, :rest]
        wide[b, :, 384 : 384 + rest] = ends[:, rest:]
    for kind in range(4):
        band = jnp.int32(0)
        for b in range(1, 4):
            band = jnp.where(types[b] == kind, b, band)
        table_rows = wide[band]
        parts = []
        for lq in range(WPL):
            for lk in range(WPL):
                for a in range(WLAT):
                    row = (lq * WLAT + a) * heads
                    parts.append(table_rows[row : row + heads, lk * 256 : lk * 256 + WLAT * SPREAD])
        typed[:, kind, :] = jnp.concatenate(parts, axis=1)
    o_table[...] = typed[...].astype(BF)
    outward.wait()


def local(tokens, cotangent, mask_ids, band_type, bias_table, w_qkv, w_proj, ln_gain, ln_shift):
    lon_cols, channels = tokens.shape[2:]
    groups = channels // 128
    heads = groups * GROUP
    half_lat = WLAT // 2
    count = WPL * WLAT * lon_cols
    span = GROUP * WINDOW
    route = token_route(lon_cols)
    constants = [
        jnp.asarray(c, BF)
        for c in (
            route, route.T, head_order(), table_order(), head_blocks(128 // GROUP), gather_heads(), row_order(heads)
        )
    ]
    anywhere = pl.BlockSpec(memory_space=pl.ANY)
    scalars = pl.BlockSpec(memory_space=pltpu.SMEM)
    vmem = pl.BlockSpec(memory_space=pltpu.VMEM)
    dma = pltpu.SemaphoreType.DMA
    bf = lambda *shape: pltpu.VMEM(shape, BF)
    f32 = lambda *shape: pltpu.VMEM(shape, F32)
    pairs = lambda *shape: [dma(shape), dma(shape)]
    pieces = (groups, 2, 4, 4, PIECE + SLOT, 128)
    table = bias_table.transpose(1, 0, 2)
    joined, full, small = pl.pallas_call(
        whole_kernel,
        out_shape=(
            jax.ShapeDtypeStruct(tokens.shape, BF),
            jax.ShapeDtypeStruct(pieces, BF),
            jax.ShapeDtypeStruct((8, 128), F32),
        ),
        in_specs=[scalars] * 2 + [anywhere] * 5 + [vmem] * 2 + [anywhere] * 7,
        out_specs=(anywhere, anywhere, vmem),
        scratch_shapes=[
            bf(2, WPL, half_lat, lon_cols, 2 * channels),
            bf(2, WPL, half_lat, EDGE, 2 * channels),
            bf(*tokens.shape),
            bf(*tokens.shape),
            bf(*table.shape),
            bf(channels, 3 * channels),
            bf(channels, channels),
            *[bf(*c.shape) for c in constants],
            f32(heads * ROWS, 512),
            f32(SPREAD * ROWS, heads * ROWS),
            f32(groups, WINDOW, span),
            f32(WINDOW, span),
            f32(count, channels),
            f32(count, 1),
            bf(count, channels),
            bf(channels, count),
            bf(count, channels),
            bf(count, 3 * channels),
            bf(count, channels),
            bf(count, channels),
            bf(count, 3 * channels),
            bf(2, WPL, half_lat, lon_cols, channels),
            bf(2, WPL, half_lat, EDGE, channels),
            bf(WPL, half_lat, lon_cols, channels),
            bf(2, WPL, half_lat, EDGE, channels),
            bf(groups, 4, channels, 128),
            bf(groups, 4, 2 * SLOT, 128),
            bf(groups, 2, channels, 128),
            bf(groups, 4, PART + 2 * SLOT, 128),
            bf(groups, 4, PART + 2 * SLOT, 128),
            bf(groups, 4, PIECE + SLOT, 128),
            bf(groups, 4, PIECE + SLOT, 128),
            bf(groups, Z_SIZE, PIECE + SLOT, 128),
            bf(*pieces),
            f32(8, 128),
            f32(8, 128),
            f32(X_SIZE, 8, 128),
            f32(Y_SIZE, 8, 128),
            f32(Z_SIZE, 8, 128),
            dma((12 + 3 * groups,)),
            dma((groups + 1,)),
            *pairs(6), *pairs(3), *pairs(groups), *pairs(groups, 4), *pairs(groups, 4), *pairs(groups, Z_SIZE),
            *pairs(groups, 4), *pairs(groups, 4), *pairs(groups, 4),
            *pairs(1), *pairs(X_SIZE), *pairs(Y_SIZE), *pairs(Z_SIZE),
        ],
        compiler_params=pltpu.CompilerParams(
            collective_id=0, has_side_effects=True, vmem_limit_bytes=56 * 1024 * 1024
        ),
        cost_estimate=pl.CostEstimate(flops=6_000_000_000, bytes_accessed=10_000_000, transcendentals=1_000_000),
    )(mask_ids, band_type, tokens, cotangent, table, w_qkv, w_proj, ln_gain, ln_shift, *constants)
    d_tokens, g_qkv, g_proj, g_table, g_gain, g_shift = pl.pallas_call(
        assemble_kernel,
        out_shape=(
            jax.ShapeDtypeStruct(tokens.shape, BF),
            jax.ShapeDtypeStruct((channels, 3 * channels), BF),
            jax.ShapeDtypeStruct((channels, channels), BF),
            jax.ShapeDtypeStruct(table.shape, BF),
            jax.ShapeDtypeStruct((channels,), F32),
            jax.ShapeDtypeStruct((channels,), F32),
        ),
        in_specs=[scalars, anywhere, anywhere, vmem, vmem],
        out_specs=(anywhere, vmem, vmem, vmem, vmem, vmem),
        scratch_shapes=[
            bf(*pieces),
            bf(*tokens.shape),
            f32(4, heads * ROWS, 512),
            f32(*table.shape),
            dma((groups + 2,)),
        ],
        compiler_params=pltpu.CompilerParams(vmem_limit_bytes=60 * 1024 * 1024),
        cost_estimate=pl.CostEstimate(flops=100_000_000, bytes_accessed=6_000_000, transcendentals=0),
    )(band_type, full, joined, small, constants[-1])
    return d_tokens, g_qkv, g_proj, g_gain, g_shift, g_table.transpose(1, 0, 2)


def solution(mesh):
    placed = (P(None, "lat", "lon", None),) * 2 + (P(None, "lat"),) + (P(),) * 6
    return jax.shard_map(
        local,
        mesh=mesh,
        in_specs=placed,
        out_specs=(P(None, "lat", "lon", None), P(), P(), P(), P(), P()),
        check_vma=False,
    )
```

```python
import jax
import jax.numpy as jnp
import numpy as np
from jax import lax
from jax.experimental import pallas as pl
from jax.experimental.pallas import tpu as pltpu
from jax.sharding import PartitionSpec as P

WPL, WLAT, WLON = 2, 6, 12
WINDOW = WPL * WLAT * WLON
ROWS = WPL * WLAT
SPREAD = 2 * WLON - 1
EDGE = 16
X_SIZE, Y_SIZE, Z_SIZE = 4, 4, 8
PART = 192
PIECE = 48
SLOT = 16
UNIT = 8
MESH = pl.DeviceIdType.MESH
GROUP = 4
EPSILON = 1e-05
LOG2E = 1.4426950408889634
BF = jnp.bfloat16
F32 = jnp.float32


def token_route(lon_cols):
    half_lat, half_lon = WLAT // 2, WLON // 2
    windows = lon_cols // WLON
    near = WPL * half_lat * lon_cols
    far = WPL * half_lat * EDGE
    route = np.zeros((windows * WINDOW, 2 * near + 2 * far), np.float32)
    for w in range(windows):
        for o in range(WLON):
            for l in range(WPL):
                for a in range(WLAT):
                    level = (l + 1) % WPL
                    col = w * WLON + o + half_lon
                    row = level * half_lat + a % half_lat
                    if col < lon_cols:
                        source = row * lon_cols + col + (near if a >= half_lat else 0)
                    else:
                        source = 2 * near + row * EDGE + col - lon_cols
                        source += far if a >= half_lat else 0
                    route[w * WINDOW + o * ROWS + l * WLAT + a, source] = 1.0
    return route


def head_order():
    perm = np.zeros((GROUP * WINDOW, GROUP * WINDOW), np.float32)
    for o in range(WLON):
        for h in range(GROUP):
            for r in range(ROWS):
                perm[(o * GROUP + h) * ROWS + r, (h * WLON + o) * ROWS + r] = 1.0
    return perm


def table_order():
    order = np.zeros((SPREAD * ROWS, 512), np.float32)
    for d in range(SPREAD):
        for l in range(WPL):
            for a in range(WLAT):
                order[(SPREAD - 1 - d) * ROWS + l * WLAT + a, l * 256 + a * SPREAD + d] = 1.0
    return order


def row_order(heads):
    order = np.zeros((heads * ROWS, heads * ROWS), np.float32)
    for h in range(heads):
        for r in range(ROWS):
            order[r * heads + h, h * ROWS + r] = 1.0
    return order


def head_blocks(head_dim):
    rows = np.arange(GROUP * head_dim)[:, None] // head_dim
    cols = np.arange(GROUP * WINDOW)[None, :] // WINDOW
    return (rows == cols).astype(np.float32)


def gather_heads():
    return np.tile(np.eye(WINDOW, dtype=np.float32), (1, GROUP))


def nn(a, b):
    return lax.dot_general(a, b, (((1,), (0,)), ((), ())), preferred_element_type=F32)


def nt(a, b):
    return lax.dot_general(a, b, (((1,), (1,)), ((), ())), preferred_element_type=F32)


def tn(a, b):
    return lax.dot_general(a, b, (((0,), (0,)), ((), ())), preferred_element_type=F32)


def place():
    lon = lax.axis_index("lon")
    lat = lax.axis_index("lat")
    x = lax.rem(lon, X_SIZE)
    z = lax.rem(lon // X_SIZE, Z_SIZE)
    y = (lat // 2) * 2 + lon // (X_SIZE * Z_SIZE)
    return x, y, z, lax.rem(lat, 2)


def device(x, y, z, core):
    return ((lax.rem(y, 2) * Z_SIZE + z) * X_SIZE + x, (y // 2) * 2 + core)


def whole_kernel(
    ids, types, tokens, cotangent, table_h, w_qkv_h, w_proj_h, gain_v, shift_v,
    route_h, unroute_h, perm_h, order_h, blocks_h, gather_h, reorder_h,
    o_tokens, o_full, o_small,
    cat, edge, cot_own, joined, table, w_qkv, w_proj, route, unroute, perm, order, blocks, gather, reorder,
    tall, folded, summed, bias, d_bias, normed, inv, ln, ln_t, cot, qkv, d_att, att, d_qkv,
    d_main, d_edge, back_main, back_edge,
    grads, tables, core_in, s1_out, s1_in, s2_out, s2_in, z_in, full, small, small_core, small_x, small_y, small_z,
    load_s, out_s, halo_s, halo_r, back_s, back_r, core_s, core_r, s1_s, s1_r, s2_s, s2_r, z_s, z_r, g2_s, g2_r, g1_s, g1_r,
    sib_s, sib_r, mc_s, mc_r, mx_s, mx_r, my_s, my_r, mz_s, mz_r,
):
    half_lat = WLAT // 2
    half_lon = WLON // 2
    lon_cols = tokens.shape[2]
    channels = tokens.shape[3]
    main = 2 * WPL * half_lat * lon_cols
    groups = channels // 128
    heads = groups * GROUP
    windows = lon_cols // WLON
    span = GROUP * WINDOW
    head_dim = 128 // GROUP
    scale = head_dim ** -0.5
    x, y, z, core = place()
    other = 1 - core
    beside = x + 1 - 2 * lax.rem(x, 2)
    across = lax.rem(y + 2, Y_SIZE)
    y_up = lax.rem(y + 2 * other, Y_SIZE)
    y_down = lax.rem(y + 2 * core, Y_SIZE)
    sibling = device(x, y, z, other)

    loads = [
        pltpu.make_async_copy(src, dst, load_s.at[i])
        for i, (src, dst) in enumerate((
            (table_h, table), (order_h, order), (reorder_h, reorder), (perm_h, perm),
            (tokens.at[:, pl.ds(half_lat, half_lat)], cat.at[0, :, :, :, pl.ds(0, channels)]),
            (cotangent.at[:, pl.ds(half_lat, half_lat)], cat.at[0, :, :, :, pl.ds(channels, channels)]),
            (route_h, route), (w_proj_h, w_proj), (blocks_h, blocks), (gather_h, gather),
            (unroute_h, unroute), (cotangent, cot_own),
            *(
                (
                    w_qkv_h.at[:, pl.ds(b * channels + g * 128, 128)],
                    w_qkv.at[:, pl.ds((3 * g + b) * 128, 128)],
                )
                for g in range(groups)
                for b in range(3)
            ),
        ))
    ]
    barrier = pltpu.get_barrier_semaphore()
    friends = [sibling, device(x, across, z, other), device(beside, y, z, other), device(beside, across, z, other)]
    friends += [device(lax.rem(x + i, X_SIZE), y, z, core) for i in range(1, X_SIZE)]
    friends += [device(x, lax.rem(y + i, Y_SIZE), z, core) for i in range(1, Y_SIZE)]
    friends += [device(x, y, lax.rem(z + i, Z_SIZE), core) for i in range(1, Z_SIZE)]
    for friend in friends:
        pl.semaphore_signal(barrier, inc=1, device_id=friend, device_id_type=MESH)
    for load in loads:
        load.start()
    pl.semaphore_wait(barrier, len(friends))

    def remote(src, dst, send, recv, target):
        return pltpu.make_async_remote_copy(
            src_ref=src, dst_ref=dst, send_sem=send, recv_sem=recv, device_id=target, device_id_type=MESH
        )

    first, last = pl.ds(0, half_lat), pl.ds(half_lat, half_lat)
    halos = []
    for i, array in enumerate((tokens, cotangent)):
        lanes = pl.ds(i * channels, channels)
        up = device(x, y_up, z, other)
        halos += [
            (array.at[:, first], cat.at[1, :, :, :, lanes], up),
            (array.at[:, last, pl.ds(0, EDGE)], edge.at[0, :, :, :, lanes], device(beside, y, z, core)),
            (array.at[:, first, pl.ds(0, EDGE)], edge.at[1, :, :, :, lanes], device(beside, y_up, z, other)),
        ]
    halos = [remote(src, dst, halo_s.at[i], halo_r.at[i], to) for i, (src, dst, to) in enumerate(halos)]
    for copy in halos:
        copy.start()

    for load in loads[:4]:
        load.wait()
    own_type = types[lax.axis_index("lat")]
    picked = (lax.broadcasted_iota(jnp.int32, (1, 4, 1), 1) == own_type).astype(F32)
    rows_of_type = jnp.sum(table[...].astype(F32) * picked, axis=1)
    tall[...] = jnp.zeros_like(tall)
    for lq in range(WPL):
        for lk in range(WPL):
            for a in range(WLAT):
                start = ((lq * WPL + lk) * WLAT + a) * WLAT * SPREAD
                row = (lq * WLAT + a) * heads
                tall[row : row + heads, lk * 256 : lk * 256 + WLAT * SPREAD] = rows_of_type[:, start : start + WLAT * SPREAD]
    laid = nt(order[...], tall[...].astype(BF)).astype(BF)
    folded[...] = nn(laid, reorder[...])
    lane = lax.rem(lax.broadcasted_iota(jnp.int32, (1, span), 1), ROWS)
    sub = lax.rem(lax.broadcasted_iota(jnp.int32, (WINDOW, 1), 0), ROWS)
    id_q = jnp.zeros((1, span), jnp.int32)
    id_k = jnp.zeros((WINDOW, 1), jnp.int32)
    for l in range(WPL):
        for a in range(WLAT):
            value = ids[l, a]
            id_q = jnp.where(lane == l * WLAT + a, value, id_q)
            id_k = jnp.where(sub == l * WLAT + a, value, id_k)
    masked = jnp.where(id_k == id_q, 0.0, -1e30)
    for g in range(groups):
        pieces = [
            folded[(WLON - 1 - o) * ROWS : (WLON - 1 - o) * ROWS + WINDOW, g * GROUP * ROWS : (g + 1) * GROUP * ROWS]
            for o in range(WLON)
        ]
        spread = jnp.concatenate(pieces, axis=1).astype(BF)
        bias[g] = nn(spread, perm[...]) * LOG2E + masked

    gain = gain_v[...].reshape(1, channels)
    shift = shift_v[...].reshape(1, channels)
    for load in loads[4:]:
        load.wait()
    for copy in halos[:3]:
        copy.wait_recv()
    x_in = nn(route[:, :main], cat[..., :channels].reshape(main, channels))
    x_in = x_in + nn(route[:, main:], edge[..., :channels].reshape(-1, channels))
    average = jnp.mean(x_in, axis=1, keepdims=True)
    centred = x_in - average
    variance = jnp.mean(centred * centred, axis=1, keepdims=True)
    inv_std = lax.rsqrt(variance + EPSILON)
    inv[...] = inv_std
    norm = centred * inv_std
    normed[...] = norm
    ln_out = (norm * gain + shift).astype(BF)
    ln[...] = ln_out
    ln_t[...] = ln_out.T
    qkv[...] = nn(ln[...], w_qkv[...]).astype(BF)
    for copy in halos[3:]:
        copy.wait_recv()
    moved = nn(route[:, :main], cat[..., channels:].reshape(main, channels))
    moved = moved + nn(route[:, main:], edge[..., channels:].reshape(-1, channels))
    cot[...] = moved.astype(BF)
    d_att[...] = nt(cot[...], w_proj[...]).astype(BF)

    lanes = lax.broadcasted_iota(jnp.int32, (1, 128), 1) // head_dim
    own = [(lanes == h).astype(F32).astype(BF) for h in range(GROUP)]
    eye = (
        lax.broadcasted_iota(jnp.int32, (128, 128), 0) == lax.broadcasted_iota(jnp.int32, (128, 128), 1)
    ).astype(F32).astype(BF)

    def attend(g, w):
        rows = pl.ds(pl.multiple_of(w * WINDOW, WINDOW), WINDOW)
        q_cols, k_cols, v_cols = (slice((3 * g + b) * 128, (3 * g + b + 1) * 128) for b in range(3))
        cols = slice(g * 128, (g + 1) * 128)
        q, k, v, da = qkv[rows, q_cols], qkv[rows, k_cols], qkv[rows, v_cols], d_att[rows, cols]
        q_heads = jnp.concatenate([q * own[h] for h in range(GROUP)], axis=0)
        da_heads = jnp.concatenate([da * own[h] for h in range(GROUP)], axis=0)
        raised = jnp.exp2(nt(k, q_heads) * (scale * LOG2E) + bias[g])
        probs = raised * (1.0 / jnp.sum(raised, axis=0, keepdims=True))
        probs_b = probs.astype(BF)
        weighted = probs * nt(v, da_heads)
        d_scores = weighted - probs * jnp.sum(weighted, axis=0, keepdims=True)
        d_scores_b = d_scores.astype(BF)
        mask = blocks[...]
        att_t = tn(v, probs_b).astype(BF) * mask
        dq_t = (tn(k, d_scores_b) * scale).astype(BF) * mask

        def store():
            joint = nt(gather[...], jnp.concatenate([att_t, dq_t], axis=0)).astype(BF)
            att[rows, cols] = joint[:, :128]
            d_qkv[rows, q_cols] = joint[:, 128:]
            d_qkv[rows, k_cols] = (nn(d_scores_b, q_heads) * scale).astype(BF)
            d_qkv[rows, v_cols] = nn(probs_b, da_heads).astype(BF)

        return d_scores, store

    def two_windows(g, w):
        left, store_left = attend(g, w)
        right, store_right = attend(g, w + 1)
        store_left()
        store_right()
        return left + right

    def gradients(g):
        weights = nn(ln_t[...], d_qkv[:, 3 * g * 128 : 3 * (g + 1) * 128]).astype(BF)
        for b in range(3):
            grads[g, b] = weights[:, b * 128 : (b + 1) * 128]
        proj = tn(att[:, g * 128 : (g + 1) * 128], cot[...]).astype(BF)
        for t in range(groups):
            grads[g, 3, t * 128 : (t + 1) * 128] = proj[:, t * 128 : (t + 1) * 128]

    def fold(g):
        spread = nt(d_bias[...].astype(BF), perm[...])
        for part in range(2):
            summed[part] = jnp.zeros(summed.shape[1:], F32)
        for o in range(WLON):
            start = (WLON - 1 - o) * ROWS
            summed[o % 2, start : start + WINDOW, : GROUP * ROWS] += spread[:, o * GROUP * ROWS : (o + 1) * GROUP * ROWS]
        laid = summed[0, :, : GROUP * ROWS] + summed[1, :, : GROUP * ROWS]
        rows = tn(laid.astype(BF), order[...])
        rest = WLAT * SPREAD - 128
        ends = jnp.concatenate([rows[:, 128 : 128 + rest], rows[:, 384 : 384 + rest]], axis=1)
        count = GROUP * ROWS // UNIT
        packed = [ends[i * UNIT : (i + 1) * UNIT] for i in range(count)]
        packed = jnp.concatenate([*packed, jnp.zeros((UNIT, 128 - count * 2 * rest), F32)], axis=1)
        laid = jnp.concatenate(
            [rows[:, :128], rows[:, 256:384], packed, jnp.zeros((16 * UNIT - (2 * count + 1) * UNIT, 128), F32)], axis=0
        ).astype(BF)
        for j in range(4):
            tables[g, j] = laid[j * 2 * SLOT : (j + 1) * 2 * SLOT]

    p1 = jnp.where(core == 0, x, y)
    p2 = jnp.where(core == 0, y, x)

    def on1(p):
        return device(jnp.where(core == 0, p, x), jnp.where(core == 0, y, p), z, core)

    def on2(p):
        return device(jnp.where(core == 0, x, p), jnp.where(core == 0, p, y), z, core)

    def after1(i):
        return lax.rem(p1 + i, 4)

    def after2(i):
        return lax.rem(p2 + i, 4)

    def core_copy(g):
        return remote(grads.at[g, pl.ds(2 * other, 2)], core_in.at[g], core_s.at[g], core_r.at[g], sibling)

    def s1_copy(g, peer):
        return remote(s1_out.at[g, peer], s1_in.at[g, p1], s1_s.at[g, peer], s1_r.at[g, p1], on1(peer))

    def s1_take(g, peer):
        return remote(s1_out.at[g, peer], s1_in.at[g, peer], s1_s.at[g, peer], s1_r.at[g, peer], on1(peer))

    def s2_copy(g, peer):
        return remote(s2_out.at[g, peer], s2_in.at[g, p2], s2_s.at[g, peer], s2_r.at[g, p2], on2(peer))

    def s2_take(g, peer):
        return remote(s2_out.at[g, peer], s2_in.at[g, peer], s2_s.at[g, peer], s2_r.at[g, peer], on2(peer))

    def z_copy(g, peer, slot):
        return remote(z_in.at[g, slot], z_in.at[g, slot], z_s.at[g, peer], z_r.at[g, slot], device(x, y, peer, core))

    def g2_copy(g, peer, slot):
        here = full.at[g, core, p1, slot]
        return remote(here, here, g2_s.at[g, peer], g2_r.at[g, slot], on2(peer))

    def g1_copy(g, peer, slot):
        here = full.at[g, core, slot]
        return remote(here, here, g1_s.at[g, peer], g1_r.at[g, slot], on1(peer))

    def sib_copy(g, half, slot):
        here = full.at[g, half, slot]
        return remote(here, here, sib_s.at[g, slot], sib_r.at[g, slot], sibling)

    def step0(g):
        core_copy(g).start()

    def step1(g):
        core_copy(g).wait_recv()
        def fill(j):
            half = j // 2
            rows = pl.ds(pl.multiple_of((j - 2 * half) * PART, PART), PART)
            added = grads[g, 2 * core + half, rows].astype(F32) + core_in[g, half, rows].astype(F32)
            s1_out[g, j, :PART] = added.astype(BF)
            s1_out[g, j, PART:] = tables[g, j]

        for i in (2, 1, 3):
            fill(after1(i))
            s1_copy(g, after1(i)).start()
        fill(p1)

    def step2(g):
        def split(part, source):
            high = jnp.where(core == 0, y, source) // 2
            low_rows = jnp.where(high == 0, part[PART:], jnp.zeros_like(part[PART:]))
            return part[:PART], low_rows, part[PART:] - low_rows

        w, t0, t1 = split(s1_out[g, p1].astype(F32), p1)
        for i in (1, 3, 2):
            source = after1(i)
            s1_take(g, source).wait_recv()
            more = split(s1_in[g, source].astype(F32), source)
            w, t0, t1 = w + more[0], t0 + more[1], t1 + more[2]
        for j in range(4):
            s2_out[g, j] = jnp.concatenate(
                [w[j * PIECE : (j + 1) * PIECE], t0[j * UNIT : (j + 1) * UNIT], t1[j * UNIT : (j + 1) * UNIT]], axis=0
            ).astype(BF)
        for i in (2, 1, 3):
            s2_copy(g, after2(i)).start()

    def step3(g):
        total = s2_out[g, p2].astype(F32)
        for i in (1, 3, 2):
            source = after2(i)
            s2_take(g, source).wait_recv()
            total = total + s2_in[g, source].astype(F32)
        z_in[g, z] = total.astype(BF)
        for i in (4, 3, 5, 2, 6, 1, 7):
            z_copy(g, lax.rem(z + i, Z_SIZE), z).start()

    def step4(g):
        for i in (1, 7, 2, 6, 3, 5, 4):
            source = lax.rem(z + i, Z_SIZE)
            z_copy(g, source, source).wait_recv()
        total = z_in[g, 0].astype(F32)
        for i in range(1, Z_SIZE):
            total = total + z_in[g, i].astype(F32)
        full[g, core, p1, p2] = total.astype(BF)
        for i in (2, 1, 3):
            g2_copy(g, after2(i), p2).start()

    def step5(g):
        for i in (1, 3, 2):
            source = after2(i)
            g2_copy(g, source, source).wait_recv()
        for i in (2, 1, 3):
            g1_copy(g, after1(i), p1).start()
        sib_copy(g, core, p1).start()

    def step6(g):
        for i in (1, 3, 2):
            source = after1(i)
            g1_copy(g, source, source).wait_recv()
            sib_copy(g, core, source).start()

    def step7(g):
        for i in range(4):
            sib_copy(g, other, i).wait_recv()
        full_copy(g).start()

    def full_copy(g):
        return pltpu.make_async_copy(full.at[g], o_full.at[g], out_s.at[g])

    def tokens_copy():
        return pltpu.make_async_copy(joined, o_tokens, out_s.at[groups])

    def finish(g):
        core_copy(g).wait_send()
        for i in range(1, 4):
            s1_copy(g, after1(i)).wait_send()
            s2_copy(g, after2(i)).wait_send()
            g2_copy(g, after2(i), p2).wait_send()
            g1_copy(g, after1(i), p1).wait_send()
        for i in range(1, Z_SIZE):
            z_copy(g, lax.rem(z + i, Z_SIZE), z).wait_send()
        for i in range(4):
            sib_copy(g, core, i).wait_send()

    def mc_copy():
        return remote(small, small_core, mc_s.at[0], mc_r.at[0], sibling)

    def mx_copy(peer, slot):
        return remote(small_x.at[slot], small_x.at[slot], mx_s.at[peer], mx_r.at[slot], device(peer, y, z, core))

    def my_copy(peer, slot):
        return remote(small_y.at[slot], small_y.at[slot], my_s.at[peer], my_r.at[slot], device(x, peer, z, core))

    def mz_copy(peer, slot):
        return remote(small_z.at[slot], small_z.at[slot], mz_s.at[peer], mz_r.at[slot], device(x, y, peer, core))

    def small_share(copy, buffer, place_here, size, value):
        buffer[place_here] = value
        for i in range(1, size):
            copy(lax.rem(place_here + i, size), place_here).start()

    def small_sum(copy, buffer, place_here, size):
        for i in range(1, size):
            source = lax.rem(place_here + i, size)
            copy(source, source).wait_recv()
        total = buffer[0]
        for i in range(1, size):
            total = total + buffer[i]
        return total

    def small_finish():
        mc_copy().wait_send()
        for copy, here, size in ((mx_copy, x, X_SIZE), (my_copy, y, Y_SIZE), (mz_copy, z, Z_SIZE)):
            for i in range(1, size):
                copy(lax.rem(here + i, size), here).wait_send()

    def group(g, between):
        d_bias[...] = two_windows(g, 0)
        between()
        d_bias[...] += two_windows(g, 2)
        gradients(g)
        step0(g)
        fold(g)

    def mid1():
        step1(0)

    def mid2():
        step1(1)
        step2(0)

    group(0, lambda: None)
    group(1, mid1)
    group(2, mid2)
    step3(0)
    step1(2)
    step2(1)

    d_ln = nt(d_qkv[...], w_qkv[...])
    norm = normed[...]
    small[...] = jnp.zeros_like(small)
    for g in range(groups):
        cols = slice(g * 128, (g + 1) * 128)
        small[g : g + 1] = jnp.sum(d_ln[:, cols] * norm[:, cols], axis=0, keepdims=True)
        small[groups + g : groups + g + 1] = jnp.sum(d_ln[:, cols], axis=0, keepdims=True)
    mc_copy().start()
    scaled = d_ln * gain
    d_flat = inv[...] * (
        scaled
        - jnp.mean(scaled, axis=1, keepdims=True)
        - norm * jnp.mean(scaled * norm, axis=1, keepdims=True)
    )
    d_flat = d_flat.astype(BF)
    d_main[...] = nn(unroute[:main], d_flat).astype(BF).reshape(d_main.shape)
    d_edge[...] = nn(unroute[main:], d_flat).astype(BF).reshape(d_edge.shape)
    backs = [
        remote(d_main.at[1], back_main, back_s.at[0], back_r.at[0], device(x, y_down, z, other)),
        remote(d_edge.at[0], back_edge.at[0], back_s.at[1], back_r.at[1], device(beside, y, z, core)),
        remote(d_edge.at[1], back_edge.at[1], back_s.at[2], back_r.at[2], device(beside, y_down, z, other)),
    ]
    for copy in backs:
        copy.start()
    step3(1)
    step2(2)
    mc_copy().wait_recv()
    small_share(mx_copy, small_x, x, X_SIZE, small[...] + small_core[...])
    step4(0)
    step3(2)
    small_share(my_copy, small_y, y, Y_SIZE, small_sum(mx_copy, small_x, x, X_SIZE))
    step5(0)
    small_share(mz_copy, small_z, z, Z_SIZE, small_sum(my_copy, small_y, y, Y_SIZE))

    for copy in backs:
        copy.wait_recv()
    for l in range(WPL):
        for a in range(WLAT):
            if a < half_lat:
                inner, outer = back_main[l, a], back_edge[1, l, a]
            else:
                inner, outer = d_main[0, l, a - half_lat], back_edge[0, l, a - half_lat]
            value = cot_own[l, a].astype(F32) + inner.astype(F32)
            joined[l, a, EDGE:] = value[EDGE:].astype(BF)
            joined[l, a, :EDGE] = (value[:EDGE] + outer.astype(F32)).astype(BF)
    tokens_copy().start()
    step4(1)
    step6(0)
    step4(2)
    step5(1)
    step7(0)
    o_small[...] = small_sum(mz_copy, small_z, z, Z_SIZE)
    step5(2)
    step6(1)
    step7(1)
    step6(2)
    step7(2)

    for copy in halos + backs:
        copy.wait_send()
    for g in range(groups):
        finish(g)
    small_finish()
    tokens_copy().wait()
    for g in range(groups):
        full_copy(g).wait()


def assemble_kernel(
    types, full_h, joined_h, small, reorder,
    o_tokens, qkv_h, proj_h, o_table, o_gain, o_shift,
    full, joined, o_qkv, o_proj, wide, typed, sem,
):
    channels = o_proj.shape[0]
    groups = channels // 128
    heads = groups * GROUP
    loads = [pltpu.make_async_copy(full_h.at[g], full.at[g], sem.at[g]) for g in range(groups)]
    inward = pltpu.make_async_copy(joined_h, joined, sem.at[groups])
    outward = pltpu.make_async_copy(joined, o_tokens, sem.at[groups + 1])
    for load in loads:
        load.start()
    inward.start()
    o_gain[...] = jnp.concatenate([small[g : g + 1] for g in range(groups)], axis=1).reshape(channels)
    o_shift[...] = jnp.concatenate([small[g : g + 1] for g in range(groups, 2 * groups)], axis=1).reshape(channels)
    inward.wait()
    outward.start()
    for g in range(groups):
        loads[g].wait()
        for half in range(2):
            for j in range(4):
                for i in range(4):
                    part = full[g, half, j, i, :PIECE]
                    block = 2 * half + j // 2
                    row = (j % 2) * PART + i * PIECE
                    if block < 3:
                        cols = slice(block * channels + g * 128, block * channels + (g + 1) * 128)
                        o_qkv[row : row + PIECE, cols] = part
                    else:
                        for u in range(0, PIECE, SLOT):
                            at = row + u
                            tile = at // 128
                            o_proj[g * 128 + at % 128 : g * 128 + at % 128 + SLOT, tile * 128 : (tile + 1) * 128] = (
                                part[u : u + SLOT]
                            )

    results = [
        pltpu.make_async_copy(o_qkv, qkv_h, sem.at[groups + 2]), pltpu.make_async_copy(o_proj, proj_h, sem.at[groups + 3])
    ]
    for result in results:
        result.start()

    count = GROUP * ROWS // UNIT
    rest = WLAT * SPREAD - 128
    for b in range(4):
        at = (b // 2) * UNIT
        units = [
            [full[g, b % 2, u // 4, u % 4, PIECE:].astype(F32)[at : at + UNIT] for u in range(2 * count + 1)]
            for g in range(groups)
        ]
        for t in range(2):
            tile = jnp.concatenate([u for g in range(groups) for u in units[g][t * count : (t + 1) * count]], axis=0)
            wide[b, :, t * 256 : t * 256 + 128] = nn(reorder[...], tile.astype(BF))
        ends = jnp.concatenate(
            [units[g][2 * count][:, i * 2 * rest : (i + 1) * 2 * rest] for g in range(groups) for i in range(count)],
            axis=0,
        )
        ends = nn(reorder[...], ends.astype(BF))
        wide[b, :, 128 : 128 + rest] = ends[:, :rest]
        wide[b, :, 384 : 384 + rest] = ends[:, rest:]
    for kind in range(4):
        band = jnp.int32(0)
        for b in range(1, 4):
            band = jnp.where(types[b] == kind, b, band)
        table_rows = wide[band]
        parts = []
        for lq in range(WPL):
            for lk in range(WPL):
                for a in range(WLAT):
                    row = (lq * WLAT + a) * heads
                    parts.append(table_rows[row : row + heads, lk * 256 : lk * 256 + WLAT * SPREAD])
        typed[:, kind, :] = jnp.concatenate(parts, axis=1)
    o_table[...] = typed[...].astype(BF)
    outward.wait()
    for result in results:
        result.wait()


def local(tokens, cotangent, mask_ids, band_type, bias_table, w_qkv, w_proj, ln_gain, ln_shift):
    lon_cols, channels = tokens.shape[2:]
    groups = channels // 128
    heads = groups * GROUP
    half_lat = WLAT // 2
    count = WPL * WLAT * lon_cols
    span = GROUP * WINDOW
    route = token_route(lon_cols)
    constants = [
        jnp.asarray(c, BF)
        for c in (
            route, route.T, head_order(), table_order(), head_blocks(128 // GROUP), gather_heads(), row_order(heads)
        )
    ]
    anywhere = pl.BlockSpec(memory_space=pl.ANY)
    scalars = pl.BlockSpec(memory_space=pltpu.SMEM)
    vmem = pl.BlockSpec(memory_space=pltpu.VMEM)
    dma = pltpu.SemaphoreType.DMA
    bf = lambda *shape: pltpu.VMEM(shape, BF)
    f32 = lambda *shape: pltpu.VMEM(shape, F32)
    pairs = lambda *shape: [dma(shape), dma(shape)]
    pieces = (groups, 2, 4, 4, PIECE + SLOT, 128)
    table = bias_table.transpose(1, 0, 2)
    joined, full, small = pl.pallas_call(
        whole_kernel,
        out_shape=(
            jax.ShapeDtypeStruct(tokens.shape, BF),
            jax.ShapeDtypeStruct(pieces, BF),
            jax.ShapeDtypeStruct((8, 128), F32),
        ),
        in_specs=[scalars] * 2 + [anywhere] * 5 + [vmem] * 2 + [anywhere] * 7,
        out_specs=(anywhere, anywhere, vmem),
        scratch_shapes=[
            bf(2, WPL, half_lat, lon_cols, 2 * channels),
            bf(2, WPL, half_lat, EDGE, 2 * channels),
            bf(*tokens.shape),
            bf(*tokens.shape),
            bf(*table.shape),
            bf(channels, 3 * channels),
            bf(channels, channels),
            *[bf(*c.shape) for c in constants],
            f32(heads * ROWS, 512),
            f32(SPREAD * ROWS, heads * ROWS),
            f32(2, SPREAD * ROWS, 128),
            f32(groups, WINDOW, span),
            f32(WINDOW, span),
            f32(count, channels),
            f32(count, 1),
            bf(count, channels),
            bf(channels, count),
            bf(count, channels),
            bf(count, 3 * channels),
            bf(count, channels),
            bf(count, channels),
            bf(count, 3 * channels),
            bf(2, WPL, half_lat, lon_cols, channels),
            bf(2, WPL, half_lat, EDGE, channels),
            bf(WPL, half_lat, lon_cols, channels),
            bf(2, WPL, half_lat, EDGE, channels),
            bf(groups, 4, channels, 128),
            bf(groups, 4, 2 * SLOT, 128),
            bf(groups, 2, channels, 128),
            bf(groups, 4, PART + 2 * SLOT, 128),
            bf(groups, 4, PART + 2 * SLOT, 128),
            bf(groups, 4, PIECE + SLOT, 128),
            bf(groups, 4, PIECE + SLOT, 128),
            bf(groups, Z_SIZE, PIECE + SLOT, 128),
            bf(*pieces),
            f32(8, 128),
            f32(8, 128),
            f32(X_SIZE, 8, 128),
            f32(Y_SIZE, 8, 128),
            f32(Z_SIZE, 8, 128),
            dma((12 + 3 * groups,)),
            dma((groups + 1,)),
            *pairs(6), *pairs(3), *pairs(groups), *pairs(groups, 4), *pairs(groups, 4), *pairs(groups, Z_SIZE),
            *pairs(groups, 4), *pairs(groups, 4), *pairs(groups, 4),
            *pairs(1), *pairs(X_SIZE), *pairs(Y_SIZE), *pairs(Z_SIZE),
        ],
        compiler_params=pltpu.CompilerParams(
            collective_id=0, has_side_effects=True, vmem_limit_bytes=56 * 1024 * 1024
        ),
        cost_estimate=pl.CostEstimate(flops=6_000_000_000, bytes_accessed=10_000_000, transcendentals=1_000_000),
    )(mask_ids, band_type, tokens, cotangent, table, w_qkv, w_proj, ln_gain, ln_shift, *constants)
    d_tokens, g_qkv, g_proj, g_table, g_gain, g_shift = pl.pallas_call(
        assemble_kernel,
        out_shape=(
            jax.ShapeDtypeStruct(tokens.shape, BF),
            jax.ShapeDtypeStruct((channels, 3 * channels), BF),
            jax.ShapeDtypeStruct((channels, channels), BF),
            jax.ShapeDtypeStruct(table.shape, BF),
            jax.ShapeDtypeStruct((channels,), F32),
            jax.ShapeDtypeStruct((channels,), F32),
        ),
        in_specs=[scalars, anywhere, anywhere, vmem, vmem],
        out_specs=(anywhere, anywhere, anywhere, vmem, vmem, vmem),
        scratch_shapes=[
            bf(*pieces),
            bf(*tokens.shape),
            bf(channels, 3 * channels),
            bf(channels, channels),
            f32(4, heads * ROWS, 512),
            f32(*table.shape),
            dma((groups + 4,)),
        ],
        compiler_params=pltpu.CompilerParams(vmem_limit_bytes=60 * 1024 * 1024),
        cost_estimate=pl.CostEstimate(flops=100_000_000, bytes_accessed=6_000_000, transcendentals=0),
    )(band_type, full, joined, small, constants[-1])
    return d_tokens, g_qkv, g_proj, g_gain, g_shift, g_table.transpose(1, 0, 2)


def solution(mesh):
    placed = (P(None, "lat", "lon", None),) * 2 + (P(None, "lat"),) + (P(),) * 6
    return jax.shard_map(
        local,
        mesh=mesh,
        in_specs=placed,
        out_specs=(P(None, "lat", "lon", None), P(), P(), P(), P(), P()),
        check_vma=False,
    )
```

```python
import jax
import jax.numpy as jnp
import numpy as np
from jax import lax
from jax.experimental import pallas as pl
from jax.experimental.pallas import tpu as pltpu
from jax.sharding import PartitionSpec as P

WPL, WLAT, WLON = 2, 6, 12
WINDOW = WPL * WLAT * WLON
ROWS = WPL * WLAT
SPREAD = 2 * WLON - 1
EDGE = 16
X_SIZE, Y_SIZE, Z_SIZE = 4, 4, 8
PART = 192
PIECE = 48
SLOT = 16
UNIT = 8
MESH = pl.DeviceIdType.MESH
GROUP = 4
EPSILON = 1e-05
LOG2E = 1.4426950408889634
BF = jnp.bfloat16
F32 = jnp.float32


def token_route(lon_cols):
    half_lat, half_lon = WLAT // 2, WLON // 2
    windows = lon_cols // WLON
    near = WPL * half_lat * lon_cols
    far = WPL * half_lat * EDGE
    route = np.zeros((windows * WINDOW, 2 * near + 2 * far), np.float32)
    for w in range(windows):
        for o in range(WLON):
            for l in range(WPL):
                for a in range(WLAT):
                    level = (l + 1) % WPL
                    col = w * WLON + o + half_lon
                    row = level * half_lat + a % half_lat
                    if col < lon_cols:
                        source = row * lon_cols + col + (near if a >= half_lat else 0)
                    else:
                        source = 2 * near + row * EDGE + col - lon_cols
                        source += far if a >= half_lat else 0
                    route[w * WINDOW + o * ROWS + l * WLAT + a, source] = 1.0
    return route


def head_order():
    perm = np.zeros((GROUP * WINDOW, GROUP * WINDOW), np.float32)
    for o in range(WLON):
        for h in range(GROUP):
            for r in range(ROWS):
                perm[(o * GROUP + h) * ROWS + r, (h * WLON + o) * ROWS + r] = 1.0
    return perm


def table_order():
    order = np.zeros((SPREAD * ROWS, 512), np.float32)
    for d in range(SPREAD):
        for l in range(WPL):
            for a in range(WLAT):
                order[(SPREAD - 1 - d) * ROWS + l * WLAT + a, l * 256 + a * SPREAD + d] = 1.0
    return order


def row_order(heads):
    order = np.zeros((heads * ROWS, heads * ROWS), np.float32)
    for h in range(heads):
        for r in range(ROWS):
            order[r * heads + h, h * ROWS + r] = 1.0
    return order


def head_blocks(head_dim):
    rows = np.arange(GROUP * head_dim)[:, None] // head_dim
    cols = np.arange(GROUP * WINDOW)[None, :] // WINDOW
    return (rows == cols).astype(np.float32)


def gather_heads():
    return np.tile(np.eye(WINDOW, dtype=np.float32), (1, GROUP))


def nn(a, b):
    return lax.dot_general(a, b, (((1,), (0,)), ((), ())), preferred_element_type=F32)


def nt(a, b):
    return lax.dot_general(a, b, (((1,), (1,)), ((), ())), preferred_element_type=F32)


def tn(a, b):
    return lax.dot_general(a, b, (((0,), (0,)), ((), ())), preferred_element_type=F32)


def place():
    lon = lax.axis_index("lon")
    lat = lax.axis_index("lat")
    x = lax.rem(lon, X_SIZE)
    z = lax.rem(lon // X_SIZE, Z_SIZE)
    y = (lat // 2) * 2 + lon // (X_SIZE * Z_SIZE)
    return x, y, z, lax.rem(lat, 2)


def device(x, y, z, core):
    return ((lax.rem(y, 2) * Z_SIZE + z) * X_SIZE + x, (y // 2) * 2 + core)


def whole_kernel(
    ids, types, tokens, cotangent, table_h, w_qkv_h, w_proj_h, gain_v, shift_v,
    route_h, unroute_h, perm_h, order_h, blocks_h, gather_h, reorder_h,
    o_tokens, o_full, o_small,
    cat, edge, cot_own, joined, table, w_qkv, w_proj, route, unroute, perm, order, blocks, gather, reorder,
    tall, folded, summed, bias, d_bias, normed, inv, ln, ln_t, cot, qkv, d_att, att, d_qkv,
    d_main, d_edge, back_main, back_edge,
    grads, tables, core_in, s1_out, s1_in, s2_out, s2_in, z_in, full, small, small_core, small_x, small_y, small_z,
    load_s, out_s, halo_s, halo_r, back_s, back_r, core_s, core_r, s1_s, s1_r, s2_s, s2_r, z_s, z_r, g2_s, g2_r, g1_s, g1_r,
    sib_s, sib_r, mc_s, mc_r, mx_s, mx_r, my_s, my_r, mz_s, mz_r,
):
    half_lat = WLAT // 2
    half_lon = WLON // 2
    lon_cols = tokens.shape[2]
    channels = tokens.shape[3]
    main = 2 * WPL * half_lat * lon_cols
    groups = channels // 128
    heads = groups * GROUP
    windows = lon_cols // WLON
    span = GROUP * WINDOW
    head_dim = 128 // GROUP
    scale = head_dim ** -0.5
    x, y, z, core = place()
    other = 1 - core
    beside = x + 1 - 2 * lax.rem(x, 2)
    across = lax.rem(y + 2, Y_SIZE)
    y_up = lax.rem(y + 2 * other, Y_SIZE)
    y_down = lax.rem(y + 2 * core, Y_SIZE)
    sibling = device(x, y, z, other)

    loads = [
        pltpu.make_async_copy(src, dst, load_s.at[i])
        for i, (src, dst) in enumerate((
            (table_h, table), (order_h, order), (reorder_h, reorder), (perm_h, perm),
            (tokens.at[:, pl.ds(half_lat, half_lat)], cat.at[0, :, :, :, pl.ds(0, channels)]),
            (cotangent.at[:, pl.ds(half_lat, half_lat)], cat.at[0, :, :, :, pl.ds(channels, channels)]),
            (route_h, route), (w_proj_h, w_proj), (blocks_h, blocks), (gather_h, gather),
            (unroute_h, unroute), (cotangent, cot_own),
            *(
                (
                    w_qkv_h.at[:, pl.ds(b * channels + g * 128, 128)],
                    w_qkv.at[:, pl.ds((3 * g + b) * 128, 128)],
                )
                for g in range(groups)
                for b in range(3)
            ),
        ))
    ]
    barrier = pltpu.get_barrier_semaphore()
    friends = [sibling, device(x, across, z, other), device(beside, y, z, other), device(beside, across, z, other)]
    friends += [device(lax.rem(x + i, X_SIZE), y, z, core) for i in range(1, X_SIZE)]
    friends += [device(x, lax.rem(y + i, Y_SIZE), z, core) for i in range(1, Y_SIZE)]
    friends += [device(x, y, lax.rem(z + i, Z_SIZE), core) for i in range(1, Z_SIZE)]
    for friend in friends:
        pl.semaphore_signal(barrier, inc=1, device_id=friend, device_id_type=MESH)
    for load in loads:
        load.start()
    pl.semaphore_wait(barrier, len(friends))

    def remote(src, dst, send, recv, target):
        return pltpu.make_async_remote_copy(
            src_ref=src, dst_ref=dst, send_sem=send, recv_sem=recv, device_id=target, device_id_type=MESH
        )

    first, last = pl.ds(0, half_lat), pl.ds(half_lat, half_lat)
    halos = []
    for i, array in enumerate((tokens, cotangent)):
        lanes = pl.ds(i * channels, channels)
        up = device(x, y_up, z, other)
        halos += [
            (array.at[:, first], cat.at[1, :, :, :, lanes], up),
            (array.at[:, last, pl.ds(0, EDGE)], edge.at[0, :, :, :, lanes], device(beside, y, z, core)),
            (array.at[:, first, pl.ds(0, EDGE)], edge.at[1, :, :, :, lanes], device(beside, y_up, z, other)),
        ]
    halos = [remote(src, dst, halo_s.at[i], halo_r.at[i], to) for i, (src, dst, to) in enumerate(halos)]
    for copy in halos:
        copy.start()

    for load in loads[:4]:
        load.wait()
    own_type = types[lax.axis_index("lat")]
    picked = (lax.broadcasted_iota(jnp.int32, (1, 4, 1), 1) == own_type).astype(F32)
    rows_of_type = jnp.sum(table[...].astype(F32) * picked, axis=1)
    tall[...] = jnp.zeros_like(tall)
    for lq in range(WPL):
        for lk in range(WPL):
            for a in range(WLAT):
                start = ((lq * WPL + lk) * WLAT + a) * WLAT * SPREAD
                row = (lq * WLAT + a) * heads
                tall[row : row + heads, lk * 256 : lk * 256 + WLAT * SPREAD] = rows_of_type[:, start : start + WLAT * SPREAD]
    laid = nt(order[...], tall[...].astype(BF)).astype(BF)
    folded[...] = nn(laid, reorder[...])
    lane = lax.rem(lax.broadcasted_iota(jnp.int32, (1, span), 1), ROWS)
    sub = lax.rem(lax.broadcasted_iota(jnp.int32, (WINDOW, 1), 0), ROWS)
    id_q = jnp.zeros((1, span), jnp.int32)
    id_k = jnp.zeros((WINDOW, 1), jnp.int32)
    for l in range(WPL):
        for a in range(WLAT):
            value = ids[l, a]
            id_q = jnp.where(lane == l * WLAT + a, value, id_q)
            id_k = jnp.where(sub == l * WLAT + a, value, id_k)
    masked = jnp.where(id_k == id_q, 0.0, -1e30)
    for g in range(groups):
        pieces = [
            folded[(WLON - 1 - o) * ROWS : (WLON - 1 - o) * ROWS + WINDOW, g * GROUP * ROWS : (g + 1) * GROUP * ROWS]
            for o in range(WLON)
        ]
        spread = jnp.concatenate(pieces, axis=1).astype(BF)
        bias[g] = nn(spread, perm[...]) * LOG2E + masked

    gain = gain_v[...].reshape(1, channels)
    shift = shift_v[...].reshape(1, channels)
    for load in loads[4:]:
        load.wait()
    for copy in halos[:3]:
        copy.wait_recv()
    x_in = nn(route[:, :main], cat[..., :channels].reshape(main, channels))
    x_in = x_in + nn(route[:, main:], edge[..., :channels].reshape(-1, channels))
    average = jnp.mean(x_in, axis=1, keepdims=True)
    centred = x_in - average
    variance = jnp.mean(centred * centred, axis=1, keepdims=True)
    inv_std = lax.rsqrt(variance + EPSILON)
    inv[...] = inv_std
    norm = centred * inv_std
    normed[...] = norm
    ln_out = (norm * gain + shift).astype(BF)
    ln[...] = ln_out
    ln_t[...] = ln_out.T
    qkv[...] = nn(ln[...], w_qkv[...]).astype(BF)
    for copy in halos[3:]:
        copy.wait_recv()
    moved = nn(route[:, :main], cat[..., channels:].reshape(main, channels))
    moved = moved + nn(route[:, main:], edge[..., channels:].reshape(-1, channels))
    cot[...] = moved.astype(BF)
    d_att[...] = nt(cot[...], w_proj[...]).astype(BF)

    lanes = lax.broadcasted_iota(jnp.int32, (1, 128), 1) // head_dim
    own = [(lanes == h).astype(F32).astype(BF) for h in range(GROUP)]
    eye = (
        lax.broadcasted_iota(jnp.int32, (128, 128), 0) == lax.broadcasted_iota(jnp.int32, (128, 128), 1)
    ).astype(F32).astype(BF)

    def attend(g, w):
        rows = pl.ds(pl.multiple_of(w * WINDOW, WINDOW), WINDOW)
        q_cols, k_cols, v_cols = (slice((3 * g + b) * 128, (3 * g + b + 1) * 128) for b in range(3))
        cols = slice(g * 128, (g + 1) * 128)
        q, k, v, da = qkv[rows, q_cols], qkv[rows, k_cols], qkv[rows, v_cols], d_att[rows, cols]
        q_heads = jnp.concatenate([q * own[h] for h in range(GROUP)], axis=0)
        da_heads = jnp.concatenate([da * own[h] for h in range(GROUP)], axis=0)
        raised = jnp.exp2(nt(k, q_heads) * (scale * LOG2E) + bias[g])
        probs = raised * (1.0 / jnp.sum(raised, axis=0, keepdims=True))
        probs_b = probs.astype(BF)
        weighted = probs * nt(v, da_heads)
        d_scores = weighted - probs * jnp.sum(weighted, axis=0, keepdims=True)
        d_scores_b = d_scores.astype(BF)
        mask = blocks[...]
        att_t = tn(v, probs_b).astype(BF) * mask
        dq_t = (tn(k, d_scores_b) * scale).astype(BF) * mask

        def store():
            joint = nt(gather[...], jnp.concatenate([att_t, dq_t], axis=0)).astype(BF)
            att[rows, cols] = joint[:, :128]
            d_qkv[rows, q_cols] = joint[:, 128:]
            d_qkv[rows, k_cols] = (nn(d_scores_b, q_heads) * scale).astype(BF)
            d_qkv[rows, v_cols] = nn(probs_b, da_heads).astype(BF)

        return d_scores, store

    def two_windows(g, w):
        left, store_left = attend(g, w)
        right, store_right = attend(g, w + 1)
        store_left()
        store_right()
        return left + right

    def gradients(g):
        weights = nn(ln_t[...], d_qkv[:, 3 * g * 128 : 3 * (g + 1) * 128]).astype(BF)
        for b in range(3):
            grads[g, b] = weights[:, b * 128 : (b + 1) * 128]
        proj = tn(att[:, g * 128 : (g + 1) * 128], cot[...]).astype(BF)
        for t in range(groups):
            grads[g, 3, t * 128 : (t + 1) * 128] = proj[:, t * 128 : (t + 1) * 128]

    def fold(g):
        spread = nt(d_bias[...].astype(BF), perm[...])
        for part in range(2):
            summed[part] = jnp.zeros(summed.shape[1:], F32)
        for o in range(WLON):
            start = (WLON - 1 - o) * ROWS
            summed[o % 2, start : start + WINDOW, : GROUP * ROWS] += spread[:, o * GROUP * ROWS : (o + 1) * GROUP * ROWS]
        laid = summed[0, :, : GROUP * ROWS] + summed[1, :, : GROUP * ROWS]
        rows = tn(laid.astype(BF), order[...])
        rest = WLAT * SPREAD - 128
        ends = jnp.concatenate([rows[:, 128 : 128 + rest], rows[:, 384 : 384 + rest]], axis=1)
        count = GROUP * ROWS // UNIT
        packed = [ends[i * UNIT : (i + 1) * UNIT] for i in range(count)]
        packed = jnp.concatenate([*packed, jnp.zeros((UNIT, 128 - count * 2 * rest), F32)], axis=1)
        laid = jnp.concatenate(
            [rows[:, :128], rows[:, 256:384], packed, jnp.zeros((16 * UNIT - (2 * count + 1) * UNIT, 128), F32)], axis=0
        ).astype(BF)
        for j in range(4):
            tables[g, j] = laid[j * 2 * SLOT : (j + 1) * 2 * SLOT]

    p1 = jnp.where(core == 0, x, y)
    p2 = jnp.where(core == 0, y, x)

    def on1(p):
        return device(jnp.where(core == 0, p, x), jnp.where(core == 0, y, p), z, core)

    def on2(p):
        return device(jnp.where(core == 0, x, p), jnp.where(core == 0, p, y), z, core)

    def after1(i):
        return lax.rem(p1 + i, 4)

    def after2(i):
        return lax.rem(p2 + i, 4)

    def core_copy(g):
        return remote(grads.at[g, pl.ds(2 * other, 2)], core_in.at[g], core_s.at[g], core_r.at[g], sibling)

    def s1_copy(g, peer):
        return remote(s1_out.at[g, peer], s1_in.at[g, p1], s1_s.at[g, peer], s1_r.at[g, p1], on1(peer))

    def s1_take(g, peer):
        return remote(s1_out.at[g, peer], s1_in.at[g, peer], s1_s.at[g, peer], s1_r.at[g, peer], on1(peer))

    def s2_copy(g, peer):
        return remote(s2_out.at[g, peer], s2_in.at[g, p2], s2_s.at[g, peer], s2_r.at[g, p2], on2(peer))

    def s2_take(g, peer):
        return remote(s2_out.at[g, peer], s2_in.at[g, peer], s2_s.at[g, peer], s2_r.at[g, peer], on2(peer))

    def z_copy(g, peer, slot):
        return remote(z_in.at[g, slot], z_in.at[g, slot], z_s.at[g, peer], z_r.at[g, slot], device(x, y, peer, core))

    def g2_copy(g, peer, slot):
        here = full.at[g, core, p1, slot]
        return remote(here, here, g2_s.at[g, peer], g2_r.at[g, slot], on2(peer))

    def g1_copy(g, peer, slot):
        here = full.at[g, core, slot]
        return remote(here, here, g1_s.at[g, peer], g1_r.at[g, slot], on1(peer))

    def sib_copy(g, half, slot):
        here = full.at[g, half, slot]
        return remote(here, here, sib_s.at[g, slot], sib_r.at[g, slot], sibling)

    def step0(g):
        core_copy(g).start()

    def step1(g):
        core_copy(g).wait_recv()
        def fill(j):
            half = j // 2
            rows = pl.ds(pl.multiple_of((j - 2 * half) * PART, PART), PART)
            added = grads[g, 2 * core + half, rows].astype(F32) + core_in[g, half, rows].astype(F32)
            s1_out[g, j, :PART] = added.astype(BF)
            s1_out[g, j, PART:] = tables[g, j]

        for i in (2, 1, 3):
            fill(after1(i))
            s1_copy(g, after1(i)).start()
        fill(p1)

    def step2(g):
        def split(part, source):
            high = jnp.where(core == 0, y, source) // 2
            low_rows = jnp.where(high == 0, part[PART:], jnp.zeros_like(part[PART:]))
            return part[:PART], low_rows, part[PART:] - low_rows

        w, t0, t1 = split(s1_out[g, p1].astype(F32), p1)
        for i in (1, 3, 2):
            source = after1(i)
            s1_take(g, source).wait_recv()
            more = split(s1_in[g, source].astype(F32), source)
            w, t0, t1 = w + more[0], t0 + more[1], t1 + more[2]
        for j in range(4):
            s2_out[g, j] = jnp.concatenate(
                [w[j * PIECE : (j + 1) * PIECE], t0[j * UNIT : (j + 1) * UNIT], t1[j * UNIT : (j + 1) * UNIT]], axis=0
            ).astype(BF)
        for i in (2, 1, 3):
            s2_copy(g, after2(i)).start()

    def step3(g):
        total = s2_out[g, p2].astype(F32)
        for i in (1, 3, 2):
            source = after2(i)
            s2_take(g, source).wait_recv()
            total = total + s2_in[g, source].astype(F32)
        z_in[g, z] = total.astype(BF)
        for i in (4, 3, 5, 2, 6, 1, 7):
            z_copy(g, lax.rem(z + i, Z_SIZE), z).start()

    def step4(g):
        for i in (1, 7, 2, 6, 3, 5, 4):
            source = lax.rem(z + i, Z_SIZE)
            z_copy(g, source, source).wait_recv()
        total = z_in[g, 0].astype(F32)
        for i in range(1, Z_SIZE):
            total = total + z_in[g, i].astype(F32)
        full[g, core, p1, p2] = total.astype(BF)
        for i in (2, 1, 3):
            g2_copy(g, after2(i), p2).start()

    def step5(g):
        for i in (1, 3, 2):
            source = after2(i)
            g2_copy(g, source, source).wait_recv()
        for i in (2, 1, 3):
            g1_copy(g, after1(i), p1).start()
        sib_copy(g, core, p1).start()

    def step6(g):
        for i in (1, 3, 2):
            source = after1(i)
            g1_copy(g, source, source).wait_recv()
            sib_copy(g, core, source).start()

    def step7(g):
        for i in range(4):
            sib_copy(g, other, i).wait_recv()
        full_copy(g).start()

    def full_copy(g):
        return pltpu.make_async_copy(full.at[g], o_full.at[g], out_s.at[g])

    def tokens_copy():
        return pltpu.make_async_copy(joined, o_tokens, out_s.at[groups])

    def finish(g):
        core_copy(g).wait_send()
        for i in range(1, 4):
            s1_copy(g, after1(i)).wait_send()
            s2_copy(g, after2(i)).wait_send()
            g2_copy(g, after2(i), p2).wait_send()
            g1_copy(g, after1(i), p1).wait_send()
        for i in range(1, Z_SIZE):
            z_copy(g, lax.rem(z + i, Z_SIZE), z).wait_send()
        for i in range(4):
            sib_copy(g, core, i).wait_send()

    def mc_copy():
        return remote(small, small_core, mc_s.at[0], mc_r.at[0], sibling)

    def mx_copy(peer, slot):
        return remote(small_x.at[slot], small_x.at[slot], mx_s.at[peer], mx_r.at[slot], device(peer, y, z, core))

    def my_copy(peer, slot):
        return remote(small_y.at[slot], small_y.at[slot], my_s.at[peer], my_r.at[slot], device(x, peer, z, core))

    def mz_copy(peer, slot):
        return remote(small_z.at[slot], small_z.at[slot], mz_s.at[peer], mz_r.at[slot], device(x, y, peer, core))

    def small_share(copy, buffer, place_here, size, value):
        buffer[place_here] = value
        for i in range(1, size):
            copy(lax.rem(place_here + i, size), place_here).start()

    def small_sum(copy, buffer, place_here, size):
        for i in range(1, size):
            source = lax.rem(place_here + i, size)
            copy(source, source).wait_recv()
        total = buffer[0]
        for i in range(1, size):
            total = total + buffer[i]
        return total

    def small_finish():
        mc_copy().wait_send()
        for copy, here, size in ((mx_copy, x, X_SIZE), (my_copy, y, Y_SIZE), (mz_copy, z, Z_SIZE)):
            for i in range(1, size):
                copy(lax.rem(here + i, size), here).wait_send()

    def group(g, between):
        d_bias[...] = two_windows(g, 0)
        between()
        d_bias[...] += two_windows(g, 2)
        gradients(g)
        step0(g)
        fold(g)

    def nothing():
        pass

    group(0, nothing)
    step1(0)
    group(1, nothing)
    step1(1)
    group(2, lambda: step2(0))
    step1(2)
    step3(0)
    step2(1)

    d_ln = nt(d_qkv[...], w_qkv[...])
    norm = normed[...]
    small[...] = jnp.zeros_like(small)
    for g in range(groups):
        cols = slice(g * 128, (g + 1) * 128)
        small[g : g + 1] = jnp.sum(d_ln[:, cols] * norm[:, cols], axis=0, keepdims=True)
        small[groups + g : groups + g + 1] = jnp.sum(d_ln[:, cols], axis=0, keepdims=True)
    mc_copy().start()
    scaled = d_ln * gain
    d_flat = inv[...] * (
        scaled
        - jnp.mean(scaled, axis=1, keepdims=True)
        - norm * jnp.mean(scaled * norm, axis=1, keepdims=True)
    )
    d_flat = d_flat.astype(BF)
    d_main[...] = nn(unroute[:main], d_flat).astype(BF).reshape(d_main.shape)
    d_edge[...] = nn(unroute[main:], d_flat).astype(BF).reshape(d_edge.shape)
    backs = [
        remote(d_main.at[1], back_main, back_s.at[0], back_r.at[0], device(x, y_down, z, other)),
        remote(d_edge.at[0], back_edge.at[0], back_s.at[1], back_r.at[1], device(beside, y, z, core)),
        remote(d_edge.at[1], back_edge.at[1], back_s.at[2], back_r.at[2], device(beside, y_down, z, other)),
    ]
    for copy in backs:
        copy.start()
    step3(1)
    step2(2)
    mc_copy().wait_recv()
    small_share(mx_copy, small_x, x, X_SIZE, small[...] + small_core[...])
    step4(0)
    step3(2)
    small_share(my_copy, small_y, y, Y_SIZE, small_sum(mx_copy, small_x, x, X_SIZE))
    step5(0)
    small_share(mz_copy, small_z, z, Z_SIZE, small_sum(my_copy, small_y, y, Y_SIZE))

    for copy in backs:
        copy.wait_recv()
    for l in range(WPL):
        for a in range(WLAT):
            if a < half_lat:
                inner, outer = back_main[l, a], back_edge[1, l, a]
            else:
                inner, outer = d_main[0, l, a - half_lat], back_edge[0, l, a - half_lat]
            value = cot_own[l, a].astype(F32) + inner.astype(F32)
            joined[l, a, EDGE:] = value[EDGE:].astype(BF)
            joined[l, a, :EDGE] = (value[:EDGE] + outer.astype(F32)).astype(BF)
    tokens_copy().start()
    step4(1)
    step6(0)
    step4(2)
    step5(1)
    step7(0)
    o_small[...] = small_sum(mz_copy, small_z, z, Z_SIZE)
    step5(2)
    step6(1)
    step7(1)
    step6(2)
    step7(2)

    for copy in halos + backs:
        copy.wait_send()
    for g in range(groups):
        finish(g)
    small_finish()
    tokens_copy().wait()
    for g in range(groups):
        full_copy(g).wait()


def assemble_kernel(
    types, full_h, joined_h, small, reorder,
    o_tokens, o_qkv, o_proj, o_table, o_gain, o_shift,
    full, joined, wide, typed, sem,
):
    channels = o_proj.shape[0]
    groups = channels // 128
    heads = groups * GROUP
    loads = [pltpu.make_async_copy(full_h.at[g], full.at[g], sem.at[g]) for g in range(groups)]
    inward = pltpu.make_async_copy(joined_h, joined, sem.at[groups])
    outward = pltpu.make_async_copy(joined, o_tokens, sem.at[groups + 1])
    for load in loads:
        load.start()
    inward.start()
    o_gain[...] = jnp.concatenate([small[g : g + 1] for g in range(groups)], axis=1).reshape(channels)
    o_shift[...] = jnp.concatenate([small[g : g + 1] for g in range(groups, 2 * groups)], axis=1).reshape(channels)
    inward.wait()
    outward.start()
    for g in range(groups):
        loads[g].wait()
        for half in range(2):
            for j in range(4):
                for i in range(4):
                    part = full[g, half, j, i, :PIECE]
                    block = 2 * half + j // 2
                    row = (j % 2) * PART + i * PIECE
                    if block < 3:
                        cols = slice(block * channels + g * 128, block * channels + (g + 1) * 128)
                        o_qkv[row : row + PIECE, cols] = part
                    else:
                        for u in range(0, PIECE, SLOT):
                            at = row + u
                            tile = at // 128
                            o_proj[g * 128 + at % 128 : g * 128 + at % 128 + SLOT, tile * 128 : (tile + 1) * 128] = (
                                part[u : u + SLOT]
                            )

    count = GROUP * ROWS // UNIT
    rest = WLAT * SPREAD - 128
    for b in range(4):
        at = (b // 2) * UNIT
        units = [
            [full[g, b % 2, u // 4, u % 4, PIECE:].astype(F32)[at : at + UNIT] for u in range(2 * count + 1)]
            for g in range(groups)
        ]
        for t in range(2):
            tile = jnp.concatenate([u for g in range(groups) for u in units[g][t * count : (t + 1) * count]], axis=0)
            wide[b, :, t * 256 : t * 256 + 128] = nn(reorder[...], tile.astype(BF))
        ends = jnp.concatenate(
            [units[g][2 * count][:, i * 2 * rest : (i + 1) * 2 * rest] for g in range(groups) for i in range(count)],
            axis=0,
        )
        ends = nn(reorder[...], ends.astype(BF))
        wide[b, :, 128 : 128 + rest] = ends[:, :rest]
        wide[b, :, 384 : 384 + rest] = ends[:, rest:]
    for kind in range(4):
        band = jnp.int32(0)
        for b in range(1, 4):
            band = jnp.where(types[b] == kind, b, band)
        table_rows = wide[band]
        parts = []
        for lq in range(WPL):
            for lk in range(WPL):
                for a in range(WLAT):
                    row = (lq * WLAT + a) * heads
                    parts.append(table_rows[row : row + heads, lk * 256 : lk * 256 + WLAT * SPREAD])
        typed[:, kind, :] = jnp.concatenate(parts, axis=1)
    o_table[...] = typed[...].astype(BF)
    outward.wait()


def local(tokens, cotangent, mask_ids, band_type, bias_table, w_qkv, w_proj, ln_gain, ln_shift):
    lon_cols, channels = tokens.shape[2:]
    groups = channels // 128
    heads = groups * GROUP
    half_lat = WLAT // 2
    count = WPL * WLAT * lon_cols
    span = GROUP * WINDOW
    route = token_route(lon_cols)
    constants = [
        jnp.asarray(c, BF)
        for c in (
            route, route.T, head_order(), table_order(), head_blocks(128 // GROUP), gather_heads(), row_order(heads)
        )
    ]
    anywhere = pl.BlockSpec(memory_space=pl.ANY)
    scalars = pl.BlockSpec(memory_space=pltpu.SMEM)
    vmem = pl.BlockSpec(memory_space=pltpu.VMEM)
    dma = pltpu.SemaphoreType.DMA
    bf = lambda *shape: pltpu.VMEM(shape, BF)
    f32 = lambda *shape: pltpu.VMEM(shape, F32)
    pairs = lambda *shape: [dma(shape), dma(shape)]
    pieces = (groups, 2, 4, 4, PIECE + SLOT, 128)
    table = bias_table.transpose(1, 0, 2)
    joined, full, small = pl.pallas_call(
        whole_kernel,
        out_shape=(
            jax.ShapeDtypeStruct(tokens.shape, BF),
            jax.ShapeDtypeStruct(pieces, BF),
            jax.ShapeDtypeStruct((8, 128), F32),
        ),
        in_specs=[scalars] * 2 + [anywhere] * 5 + [vmem] * 2 + [anywhere] * 7,
        out_specs=(anywhere, anywhere, vmem),
        scratch_shapes=[
            bf(2, WPL, half_lat, lon_cols, 2 * channels),
            bf(2, WPL, half_lat, EDGE, 2 * channels),
            bf(*tokens.shape),
            bf(*tokens.shape),
            bf(*table.shape),
            bf(channels, 3 * channels),
            bf(channels, channels),
            *[bf(*c.shape) for c in constants],
            f32(heads * ROWS, 512),
            f32(SPREAD * ROWS, heads * ROWS),
            f32(2, SPREAD * ROWS, 128),
            f32(groups, WINDOW, span),
            f32(WINDOW, span),
            f32(count, channels),
            f32(count, 1),
            bf(count, channels),
            bf(channels, count),
            bf(count, channels),
            bf(count, 3 * channels),
            bf(count, channels),
            bf(count, channels),
            bf(count, 3 * channels),
            bf(2, WPL, half_lat, lon_cols, channels),
            bf(2, WPL, half_lat, EDGE, channels),
            bf(WPL, half_lat, lon_cols, channels),
            bf(2, WPL, half_lat, EDGE, channels),
            bf(groups, 4, channels, 128),
            bf(groups, 4, 2 * SLOT, 128),
            bf(groups, 2, channels, 128),
            bf(groups, 4, PART + 2 * SLOT, 128),
            bf(groups, 4, PART + 2 * SLOT, 128),
            bf(groups, 4, PIECE + SLOT, 128),
            bf(groups, 4, PIECE + SLOT, 128),
            bf(groups, Z_SIZE, PIECE + SLOT, 128),
            bf(*pieces),
            f32(8, 128),
            f32(8, 128),
            f32(X_SIZE, 8, 128),
            f32(Y_SIZE, 8, 128),
            f32(Z_SIZE, 8, 128),
            dma((12 + 3 * groups,)),
            dma((groups + 1,)),
            *pairs(6), *pairs(3), *pairs(groups), *pairs(groups, 4), *pairs(groups, 4), *pairs(groups, Z_SIZE),
            *pairs(groups, 4), *pairs(groups, 4), *pairs(groups, 4),
            *pairs(1), *pairs(X_SIZE), *pairs(Y_SIZE), *pairs(Z_SIZE),
        ],
        compiler_params=pltpu.CompilerParams(
            collective_id=0, has_side_effects=True, vmem_limit_bytes=56 * 1024 * 1024
        ),
        cost_estimate=pl.CostEstimate(flops=6_000_000_000, bytes_accessed=10_000_000, transcendentals=1_000_000),
    )(mask_ids, band_type, tokens, cotangent, table, w_qkv, w_proj, ln_gain, ln_shift, *constants)
    d_tokens, g_qkv, g_proj, g_table, g_gain, g_shift = pl.pallas_call(
        assemble_kernel,
        out_shape=(
            jax.ShapeDtypeStruct(tokens.shape, BF),
            jax.ShapeDtypeStruct((channels, 3 * channels), BF),
            jax.ShapeDtypeStruct((channels, channels), BF),
            jax.ShapeDtypeStruct(table.shape, BF),
            jax.ShapeDtypeStruct((channels,), F32),
            jax.ShapeDtypeStruct((channels,), F32),
        ),
        in_specs=[scalars, anywhere, anywhere, vmem, vmem],
        out_specs=(anywhere, vmem, vmem, vmem, vmem, vmem),
        scratch_shapes=[
            bf(*pieces),
            bf(*tokens.shape),
            f32(4, heads * ROWS, 512),
            f32(*table.shape),
            dma((groups + 2,)),
        ],
        compiler_params=pltpu.CompilerParams(vmem_limit_bytes=60 * 1024 * 1024),
        cost_estimate=pl.CostEstimate(flops=100_000_000, bytes_accessed=6_000_000, transcendentals=0),
    )(band_type, full, joined, small, constants[-1])
    return d_tokens, g_qkv, g_proj, g_gain, g_shift, g_table.transpose(1, 0, 2)


def solution(mesh):
    placed = (P(None, "lat", "lon", None),) * 2 + (P(None, "lat"),) + (P(),) * 6
    return jax.shard_map(
        local,
        mesh=mesh,
        in_specs=placed,
        out_specs=(P(None, "lat", "lon", None), P(), P(), P(), P(), P()),
        check_vma=False,
    )
```

```python
import jax
import jax.numpy as jnp
import numpy as np
from jax import lax
from jax.experimental import pallas as pl
from jax.experimental.pallas import tpu as pltpu
from jax.sharding import PartitionSpec as P

WPL, WLAT, WLON = 2, 6, 12
WINDOW = WPL * WLAT * WLON
ROWS = WPL * WLAT
SPREAD = 2 * WLON - 1
EDGE = 16
X_SIZE, Y_SIZE, Z_SIZE = 4, 4, 8
PART = 192
PIECE = 48
SLOT = 16
UNIT = 8
MESH = pl.DeviceIdType.MESH
GROUP = 4
EPSILON = 1e-05
LOG2E = 1.4426950408889634
BF = jnp.bfloat16
F32 = jnp.float32


def token_route(lon_cols):
    half_lat, half_lon = WLAT // 2, WLON // 2
    windows = lon_cols // WLON
    near = WPL * half_lat * lon_cols
    far = WPL * half_lat * EDGE
    route = np.zeros((windows * WINDOW, 2 * near + 2 * far), np.float32)
    for w in range(windows):
        for o in range(WLON):
            for l in range(WPL):
                for a in range(WLAT):
                    level = (l + 1) % WPL
                    col = w * WLON + o + half_lon
                    row = level * half_lat + a % half_lat
                    if col < lon_cols:
                        source = row * lon_cols + col + (near if a >= half_lat else 0)
                    else:
                        source = 2 * near + row * EDGE + col - lon_cols
                        source += far if a >= half_lat else 0
                    route[w * WINDOW + o * ROWS + l * WLAT + a, source] = 1.0
    return route


def head_order():
    perm = np.zeros((GROUP * WINDOW, GROUP * WINDOW), np.float32)
    for o in range(WLON):
        for h in range(GROUP):
            for r in range(ROWS):
                perm[(o * GROUP + h) * ROWS + r, (h * WLON + o) * ROWS + r] = 1.0
    return perm


def table_order():
    order = np.zeros((SPREAD * ROWS, 512), np.float32)
    for d in range(SPREAD):
        for l in range(WPL):
            for a in range(WLAT):
                order[(SPREAD - 1 - d) * ROWS + l * WLAT + a, l * 256 + a * SPREAD + d] = 1.0
    return order


def row_order(heads):
    order = np.zeros((heads * ROWS, heads * ROWS), np.float32)
    for h in range(heads):
        for r in range(ROWS):
            order[r * heads + h, h * ROWS + r] = 1.0
    return order


def head_blocks(head_dim):
    rows = np.arange(GROUP * head_dim)[:, None] // head_dim
    cols = np.arange(GROUP * WINDOW)[None, :] // WINDOW
    return (rows == cols).astype(np.float32)


def gather_heads():
    return np.tile(np.eye(WINDOW, dtype=np.float32), (1, GROUP))


def nn(a, b):
    return lax.dot_general(a, b, (((1,), (0,)), ((), ())), preferred_element_type=F32)


def nt(a, b):
    return lax.dot_general(a, b, (((1,), (1,)), ((), ())), preferred_element_type=F32)


def tn(a, b):
    return lax.dot_general(a, b, (((0,), (0,)), ((), ())), preferred_element_type=F32)


def place():
    lon = lax.axis_index("lon")
    lat = lax.axis_index("lat")
    x = lax.rem(lon, X_SIZE)
    z = lax.rem(lon // X_SIZE, Z_SIZE)
    y = (lat // 2) * 2 + lon // (X_SIZE * Z_SIZE)
    return x, y, z, lax.rem(lat, 2)


def device(x, y, z, core):
    return ((lax.rem(y, 2) * Z_SIZE + z) * X_SIZE + x, (y // 2) * 2 + core)


def whole_kernel(
    ids, types, tokens, cotangent, table_h, w_qkv_h, w_proj_h, gain_v, shift_v,
    route_h, unroute_h, perm_h, order_h, blocks_h, gather_h, reorder_h,
    o_tokens, o_full, o_small,
    cat, edge, cot_own, joined, table, w_qkv, w_proj, route, unroute, perm, order, blocks, gather, reorder,
    tall, folded, summed, bias, d_bias, normed, inv, ln, ln_t, cot, qkv, d_att, att, d_qkv,
    d_main, d_edge, back_main, back_edge,
    grads, tables, core_in, s1_out, s1_in, s2_out, s2_in, z_in, full, small, small_core, small_x, small_y, small_z,
    load_s, out_s, halo_s, halo_r, back_s, back_r, core_s, core_r, s1_s, s1_r, s2_s, s2_r, z_s, z_r, g2_s, g2_r, g1_s, g1_r,
    sib_s, sib_r, mc_s, mc_r, mx_s, mx_r, my_s, my_r, mz_s, mz_r,
):
    half_lat = WLAT // 2
    half_lon = WLON // 2
    lon_cols = tokens.shape[2]
    channels = tokens.shape[3]
    main = 2 * WPL * half_lat * lon_cols
    groups = channels // 128
    heads = groups * GROUP
    windows = lon_cols // WLON
    span = GROUP * WINDOW
    head_dim = 128 // GROUP
    scale = head_dim ** -0.5
    x, y, z, core = place()
    other = 1 - core
    beside = x + 1 - 2 * lax.rem(x, 2)
    across = lax.rem(y + 2, Y_SIZE)
    y_up = lax.rem(y + 2 * other, Y_SIZE)
    y_down = lax.rem(y + 2 * core, Y_SIZE)
    sibling = device(x, y, z, other)

    loads = [
        pltpu.make_async_copy(src, dst, load_s.at[i])
        for i, (src, dst) in enumerate((
            (table_h, table), (order_h, order), (reorder_h, reorder), (perm_h, perm),
            (tokens.at[:, pl.ds(half_lat, half_lat)], cat.at[0, :, :, :, pl.ds(0, channels)]),
            (cotangent.at[:, pl.ds(half_lat, half_lat)], cat.at[0, :, :, :, pl.ds(channels, channels)]),
            (route_h, route), (w_proj_h, w_proj), (blocks_h, blocks), (gather_h, gather),
            (unroute_h, unroute), (cotangent, cot_own),
            *(
                (
                    w_qkv_h.at[:, pl.ds(b * channels + g * 128, 128)],
                    w_qkv.at[:, pl.ds((3 * g + b) * 128, 128)],
                )
                for g in range(groups)
                for b in range(3)
            ),
        ))
    ]
    barrier = pltpu.get_barrier_semaphore()
    friends = [sibling, device(x, across, z, other), device(beside, y, z, other), device(beside, across, z, other)]
    friends += [device(lax.rem(x + i, X_SIZE), y, z, core) for i in range(1, X_SIZE)]
    friends += [device(x, lax.rem(y + i, Y_SIZE), z, core) for i in range(1, Y_SIZE)]
    friends += [device(x, y, lax.rem(z + i, Z_SIZE), core) for i in range(1, Z_SIZE)]
    for friend in friends:
        pl.semaphore_signal(barrier, inc=1, device_id=friend, device_id_type=MESH)
    for load in loads:
        load.start()
    pl.semaphore_wait(barrier, len(friends))

    def remote(src, dst, send, recv, target):
        return pltpu.make_async_remote_copy(
            src_ref=src, dst_ref=dst, send_sem=send, recv_sem=recv, device_id=target, device_id_type=MESH
        )

    first, last = pl.ds(0, half_lat), pl.ds(half_lat, half_lat)
    halos = []
    for i, array in enumerate((tokens, cotangent)):
        lanes = pl.ds(i * channels, channels)
        up = device(x, y_up, z, other)
        halos += [
            (array.at[:, first], cat.at[1, :, :, :, lanes], up),
            (array.at[:, last, pl.ds(0, EDGE)], edge.at[0, :, :, :, lanes], device(beside, y, z, core)),
            (array.at[:, first, pl.ds(0, EDGE)], edge.at[1, :, :, :, lanes], device(beside, y_up, z, other)),
        ]
    halos = [remote(src, dst, halo_s.at[i], halo_r.at[i], to) for i, (src, dst, to) in enumerate(halos)]
    for copy in halos:
        copy.start()

    for load in loads[:4]:
        load.wait()
    own_type = types[lax.axis_index("lat")]
    picked = (lax.broadcasted_iota(jnp.int32, (1, 4, 1), 1) == own_type).astype(F32)
    rows_of_type = jnp.sum(table[...].astype(F32) * picked, axis=1)
    tall[...] = jnp.zeros_like(tall)
    for lq in range(WPL):
        for lk in range(WPL):
            for a in range(WLAT):
                start = ((lq * WPL + lk) * WLAT + a) * WLAT * SPREAD
                row = (lq * WLAT + a) * heads
                tall[row : row + heads, lk * 256 : lk * 256 + WLAT * SPREAD] = rows_of_type[:, start : start + WLAT * SPREAD]
    laid = nt(order[...], tall[...].astype(BF)).astype(BF)
    folded[...] = nn(laid, reorder[...])
    lane = lax.rem(lax.broadcasted_iota(jnp.int32, (1, span), 1), ROWS)
    sub = lax.rem(lax.broadcasted_iota(jnp.int32, (WINDOW, 1), 0), ROWS)
    id_q = jnp.zeros((1, span), jnp.int32)
    id_k = jnp.zeros((WINDOW, 1), jnp.int32)
    for l in range(WPL):
        for a in range(WLAT):
            value = ids[l, a]
            id_q = jnp.where(lane == l * WLAT + a, value, id_q)
            id_k = jnp.where(sub == l * WLAT + a, value, id_k)
    masked = jnp.where(id_k == id_q, 0.0, -1e30)
    for g in range(groups):
        pieces = [
            folded[(WLON - 1 - o) * ROWS : (WLON - 1 - o) * ROWS + WINDOW, g * GROUP * ROWS : (g + 1) * GROUP * ROWS]
            for o in range(WLON)
        ]
        spread = jnp.concatenate(pieces, axis=1).astype(BF)
        bias[g] = nn(spread, perm[...]) * LOG2E + masked

    gain = gain_v[...].reshape(1, channels)
    shift = shift_v[...].reshape(1, channels)
    for load in loads[4:]:
        load.wait()
    for copy in halos[:3]:
        copy.wait_recv()
    x_in = nn(route[:, :main], cat[..., :channels].reshape(main, channels))
    x_in = x_in + nn(route[:, main:], edge[..., :channels].reshape(-1, channels))
    average = jnp.mean(x_in, axis=1, keepdims=True)
    centred = x_in - average
    variance = jnp.mean(centred * centred, axis=1, keepdims=True)
    inv_std = lax.rsqrt(variance + EPSILON)
    inv[...] = inv_std
    norm = centred * inv_std
    normed[...] = norm
    ln_out = (norm * gain + shift).astype(BF)
    ln[...] = ln_out
    ln_t[...] = ln_out.T
    qkv[...] = nn(ln[...], w_qkv[...]).astype(BF)
    for copy in halos[3:]:
        copy.wait_recv()
    moved = nn(route[:, :main], cat[..., channels:].reshape(main, channels))
    moved = moved + nn(route[:, main:], edge[..., channels:].reshape(-1, channels))
    cot[...] = moved.astype(BF)
    d_att[...] = nt(cot[...], w_proj[...]).astype(BF)

    lanes = lax.broadcasted_iota(jnp.int32, (1, 128), 1) // head_dim
    own = [(lanes == h).astype(F32).astype(BF) for h in range(GROUP)]
    eye = (
        lax.broadcasted_iota(jnp.int32, (128, 128), 0) == lax.broadcasted_iota(jnp.int32, (128, 128), 1)
    ).astype(F32).astype(BF)

    def attend(g, w):
        rows = pl.ds(pl.multiple_of(w * WINDOW, WINDOW), WINDOW)
        q_cols, k_cols, v_cols = (slice((3 * g + b) * 128, (3 * g + b + 1) * 128) for b in range(3))
        cols = slice(g * 128, (g + 1) * 128)
        q, k, v, da = qkv[rows, q_cols], qkv[rows, k_cols], qkv[rows, v_cols], d_att[rows, cols]
        q_heads = jnp.concatenate([q * own[h] for h in range(GROUP)], axis=0)
        da_heads = jnp.concatenate([da * own[h] for h in range(GROUP)], axis=0)
        raised = jnp.exp2(nt(k, q_heads) * (scale * LOG2E) + bias[g])
        probs = raised * (1.0 / jnp.sum(raised, axis=0, keepdims=True))
        probs_b = probs.astype(BF)
        weighted = probs * nt(v, da_heads)
        d_scores = weighted - probs * jnp.sum(weighted, axis=0, keepdims=True)
        d_scores_b = d_scores.astype(BF)
        mask = blocks[...]
        att_t = tn(v, probs_b).astype(BF) * mask
        dq_t = (tn(k, d_scores_b) * scale).astype(BF) * mask

        def store():
            joint = nt(gather[...], jnp.concatenate([att_t, dq_t], axis=0)).astype(BF)
            att[rows, cols] = joint[:, :128]
            d_qkv[rows, q_cols] = joint[:, 128:]
            d_qkv[rows, k_cols] = (nn(d_scores_b, q_heads) * scale).astype(BF)
            d_qkv[rows, v_cols] = nn(probs_b, da_heads).astype(BF)

        return d_scores, store

    def two_windows(g, w):
        left, store_left = attend(g, w)
        right, store_right = attend(g, w + 1)
        store_left()
        store_right()
        return left + right

    def gradients(g):
        weights = nn(ln_t[...], d_qkv[:, 3 * g * 128 : 3 * (g + 1) * 128]).astype(BF)
        for b in range(3):
            grads[g, b] = weights[:, b * 128 : (b + 1) * 128]
        proj = tn(att[:, g * 128 : (g + 1) * 128], cot[...]).astype(BF)
        for t in range(groups):
            grads[g, 3, t * 128 : (t + 1) * 128] = proj[:, t * 128 : (t + 1) * 128]

    def fold(g):
        spread = nt(d_bias[...].astype(BF), perm[...])
        for part in range(2):
            summed[part] = jnp.zeros(summed.shape[1:], F32)
        for o in range(WLON):
            start = (WLON - 1 - o) * ROWS
            summed[o % 2, start : start + WINDOW, : GROUP * ROWS] += spread[:, o * GROUP * ROWS : (o + 1) * GROUP * ROWS]
        laid = summed[0, :, : GROUP * ROWS] + summed[1, :, : GROUP * ROWS]
        rows = tn(laid.astype(BF), order[...])
        rest = WLAT * SPREAD - 128
        ends = jnp.concatenate([rows[:, 128 : 128 + rest], rows[:, 384 : 384 + rest]], axis=1)
        count = GROUP * ROWS // UNIT
        packed = [ends[i * UNIT : (i + 1) * UNIT] for i in range(count)]
        packed = jnp.concatenate([*packed, jnp.zeros((UNIT, 128 - count * 2 * rest), F32)], axis=1)
        laid = jnp.concatenate(
            [rows[:, :128], rows[:, 256:384], packed, jnp.zeros((16 * UNIT - (2 * count + 1) * UNIT, 128), F32)], axis=0
        ).astype(BF)
        for j in range(4):
            tables[g, j] = laid[j * 2 * SLOT : (j + 1) * 2 * SLOT]

    p1 = jnp.where(core == 0, x, y)
    p2 = jnp.where(core == 0, y, x)

    def on1(p):
        return device(jnp.where(core == 0, p, x), jnp.where(core == 0, y, p), z, core)

    def on2(p):
        return device(jnp.where(core == 0, x, p), jnp.where(core == 0, p, y), z, core)

    def after1(i):
        return lax.rem(p1 + i, 4)

    def after2(i):
        return lax.rem(p2 + i, 4)

    def core_copy(g):
        return remote(grads.at[g, pl.ds(2 * other, 2)], core_in.at[g], core_s.at[g], core_r.at[g], sibling)

    def s1_copy(g, peer):
        return remote(s1_out.at[g, peer], s1_in.at[g, p1], s1_s.at[g, peer], s1_r.at[g, p1], on1(peer))

    def s1_take(g, peer):
        return remote(s1_out.at[g, peer], s1_in.at[g, peer], s1_s.at[g, peer], s1_r.at[g, peer], on1(peer))

    def s2_copy(g, peer):
        return remote(s2_out.at[g, peer], s2_in.at[g, p2], s2_s.at[g, peer], s2_r.at[g, p2], on2(peer))

    def s2_take(g, peer):
        return remote(s2_out.at[g, peer], s2_in.at[g, peer], s2_s.at[g, peer], s2_r.at[g, peer], on2(peer))

    def z_copy(g, peer, slot):
        return remote(z_in.at[g, slot], z_in.at[g, slot], z_s.at[g, peer], z_r.at[g, slot], device(x, y, peer, core))

    def g2_copy(g, peer, slot):
        here = full.at[g, core, p1, slot]
        return remote(here, here, g2_s.at[g, peer], g2_r.at[g, slot], on2(peer))

    def g1_copy(g, peer, slot):
        here = full.at[g, core, slot]
        return remote(here, here, g1_s.at[g, peer], g1_r.at[g, slot], on1(peer))

    def sib_copy(g, half, slot):
        here = full.at[g, half, slot]
        return remote(here, here, sib_s.at[g, slot], sib_r.at[g, slot], sibling)

    def step0(g):
        core_copy(g).start()

    def step1(g):
        core_copy(g).wait_recv()
        def fill(j):
            half = j // 2
            rows = pl.ds(pl.multiple_of((j - 2 * half) * PART, PART), PART)
            added = grads[g, 2 * core + half, rows].astype(F32) + core_in[g, half, rows].astype(F32)
            s1_out[g, j, :PART] = added.astype(BF)
            s1_out[g, j, PART:] = tables[g, j]

        for i in (2, 1, 3):
            fill(after1(i))
            s1_copy(g, after1(i)).start()
        fill(p1)

    def step2(g):
        def split(part, source):
            high = jnp.where(core == 0, y, source) // 2
            low_rows = jnp.where(high == 0, part[PART:], jnp.zeros_like(part[PART:]))
            return part[:PART], low_rows, part[PART:] - low_rows

        w, t0, t1 = split(s1_out[g, p1].astype(F32), p1)
        for i in (1, 3, 2):
            source = after1(i)
            s1_take(g, source).wait_recv()
            more = split(s1_in[g, source].astype(F32), source)
            w, t0, t1 = w + more[0], t0 + more[1], t1 + more[2]
        for j in range(4):
            s2_out[g, j] = jnp.concatenate(
                [w[j * PIECE : (j + 1) * PIECE], t0[j * UNIT : (j + 1) * UNIT], t1[j * UNIT : (j + 1) * UNIT]], axis=0
            ).astype(BF)
        for i in (2, 1, 3):
            s2_copy(g, after2(i)).start()

    def step3(g):
        total = s2_out[g, p2].astype(F32)
        for i in (1, 3, 2):
            source = after2(i)
            s2_take(g, source).wait_recv()
            total = total + s2_in[g, source].astype(F32)
        z_in[g, z] = total.astype(BF)
        for i in (4, 3, 5, 2, 6, 1, 7):
            z_copy(g, lax.rem(z + i, Z_SIZE), z).start()

    def step4(g):
        for i in (1, 7, 2, 6, 3, 5, 4):
            source = lax.rem(z + i, Z_SIZE)
            z_copy(g, source, source).wait_recv()
        total = z_in[g, 0].astype(F32)
        for i in range(1, Z_SIZE):
            total = total + z_in[g, i].astype(F32)
        full[g, core, p1, p2] = total.astype(BF)
        for i in (2, 1, 3):
            g2_copy(g, after2(i), p2).start()

    def step5(g):
        for i in (1, 3, 2):
            source = after2(i)
            g2_copy(g, source, source).wait_recv()
        for i in (2, 1, 3):
            g1_copy(g, after1(i), p1).start()
        sib_copy(g, core, p1).start()

    def step6(g):
        for i in (1, 3, 2):
            source = after1(i)
            g1_copy(g, source, source).wait_recv()
            sib_copy(g, core, source).start()
        full_copy(g, core, 0).start()

    def step7(g):
        for i in range(4):
            sib_copy(g, other, i).wait_recv()
        full_copy(g, other, 1).start()

    def full_copy(g, half, i):
        return pltpu.make_async_copy(full.at[g, half], o_full.at[g, half], out_s.at[2 * g + i])

    def tokens_copy():
        return pltpu.make_async_copy(joined, o_tokens, out_s.at[2 * groups])

    def finish(g):
        core_copy(g).wait_send()
        for i in range(1, 4):
            s1_copy(g, after1(i)).wait_send()
            s2_copy(g, after2(i)).wait_send()
            g2_copy(g, after2(i), p2).wait_send()
        for i in range(1, Z_SIZE):
            z_copy(g, lax.rem(z + i, Z_SIZE), z).wait_send()

    def finish_gather(g):
        for i in range(1, 4):
            g1_copy(g, after1(i), p1).wait_send()
        for i in range(4):
            sib_copy(g, core, i).wait_send()

    def mc_copy():
        return remote(small, small_core, mc_s.at[0], mc_r.at[0], sibling)

    def mx_copy(peer, slot):
        return remote(small_x.at[slot], small_x.at[slot], mx_s.at[peer], mx_r.at[slot], device(peer, y, z, core))

    def my_copy(peer, slot):
        return remote(small_y.at[slot], small_y.at[slot], my_s.at[peer], my_r.at[slot], device(x, peer, z, core))

    def mz_copy(peer, slot):
        return remote(small_z.at[slot], small_z.at[slot], mz_s.at[peer], mz_r.at[slot], device(x, y, peer, core))

    def small_share(copy, buffer, place_here, size, value):
        buffer[place_here] = value
        for i in range(1, size):
            copy(lax.rem(place_here + i, size), place_here).start()

    def small_sum(copy, buffer, place_here, size):
        for i in range(1, size):
            source = lax.rem(place_here + i, size)
            copy(source, source).wait_recv()
        total = buffer[0]
        for i in range(1, size):
            total = total + buffer[i]
        return total

    def small_finish():
        mc_copy().wait_send()
        for copy, here, size in ((mx_copy, x, X_SIZE), (my_copy, y, Y_SIZE), (mz_copy, z, Z_SIZE)):
            for i in range(1, size):
                copy(lax.rem(here + i, size), here).wait_send()

    def group(g, between):
        d_bias[...] = two_windows(g, 0)
        between()
        d_bias[...] += two_windows(g, 2)
        gradients(g)
        step0(g)
        fold(g)

    def nothing():
        pass

    group(0, nothing)
    step1(0)
    group(1, nothing)
    step1(1)
    group(2, lambda: step2(0))
    step1(2)
    step3(0)
    step2(1)

    d_ln = nt(d_qkv[...], w_qkv[...])
    norm = normed[...]
    small[...] = jnp.zeros_like(small)
    for g in range(groups):
        cols = slice(g * 128, (g + 1) * 128)
        small[g : g + 1] = jnp.sum(d_ln[:, cols] * norm[:, cols], axis=0, keepdims=True)
        small[groups + g : groups + g + 1] = jnp.sum(d_ln[:, cols], axis=0, keepdims=True)
    mc_copy().start()
    scaled = d_ln * gain
    d_flat = inv[...] * (
        scaled
        - jnp.mean(scaled, axis=1, keepdims=True)
        - norm * jnp.mean(scaled * norm, axis=1, keepdims=True)
    )
    d_flat = d_flat.astype(BF)
    d_main[...] = nn(unroute[:main], d_flat).astype(BF).reshape(d_main.shape)
    d_edge[...] = nn(unroute[main:], d_flat).astype(BF).reshape(d_edge.shape)
    backs = [
        remote(d_main.at[1], back_main, back_s.at[0], back_r.at[0], device(x, y_down, z, other)),
        remote(d_edge.at[0], back_edge.at[0], back_s.at[1], back_r.at[1], device(beside, y, z, core)),
        remote(d_edge.at[1], back_edge.at[1], back_s.at[2], back_r.at[2], device(beside, y_down, z, other)),
    ]
    for copy in backs:
        copy.start()
    step3(1)
    step2(2)
    mc_copy().wait_recv()
    small_share(mx_copy, small_x, x, X_SIZE, small[...] + small_core[...])
    step4(0)
    step3(2)
    small_share(my_copy, small_y, y, Y_SIZE, small_sum(mx_copy, small_x, x, X_SIZE))
    step5(0)
    small_share(mz_copy, small_z, z, Z_SIZE, small_sum(my_copy, small_y, y, Y_SIZE))

    for copy in backs:
        copy.wait_recv()
    for l in range(WPL):
        for a in range(WLAT):
            if a < half_lat:
                inner, outer = back_main[l, a], back_edge[1, l, a]
            else:
                inner, outer = d_main[0, l, a - half_lat], back_edge[0, l, a - half_lat]
            value = cot_own[l, a].astype(F32) + inner.astype(F32)
            joined[l, a, EDGE:] = value[EDGE:].astype(BF)
            joined[l, a, :EDGE] = (value[:EDGE] + outer.astype(F32)).astype(BF)
    tokens_copy().start()
    step4(1)
    step6(0)
    step4(2)
    step5(1)
    step7(0)
    o_small[...] = small_sum(mz_copy, small_z, z, Z_SIZE)
    step5(2)
    step6(1)
    step7(1)

    for copy in halos + backs:
        copy.wait_send()
    small_finish()
    for g in range(groups):
        finish(g)
    finish_gather(0)
    finish_gather(1)
    step6(2)
    step7(2)
    finish_gather(2)
    tokens_copy().wait()
    for g in range(groups):
        full_copy(g, core, 0).wait()
        full_copy(g, other, 1).wait()


def assemble_kernel(
    types, full_h, joined_h, small, reorder,
    o_tokens, o_qkv, o_proj, o_table, o_gain, o_shift,
    full, joined, wide, typed, sem,
):
    channels = o_proj.shape[0]
    groups = channels // 128
    heads = groups * GROUP
    loads = [pltpu.make_async_copy(full_h.at[g], full.at[g], sem.at[g]) for g in range(groups)]
    inward = pltpu.make_async_copy(joined_h, joined, sem.at[groups])
    outward = pltpu.make_async_copy(joined, o_tokens, sem.at[groups + 1])
    for load in loads:
        load.start()
    inward.start()
    o_gain[...] = jnp.concatenate([small[g : g + 1] for g in range(groups)], axis=1).reshape(channels)
    o_shift[...] = jnp.concatenate([small[g : g + 1] for g in range(groups, 2 * groups)], axis=1).reshape(channels)
    inward.wait()
    outward.start()
    for g in range(groups):
        loads[g].wait()
        for half in range(2):
            for j in range(4):
                for i in range(4):
                    part = full[g, half, j, i, :PIECE]
                    block = 2 * half + j // 2
                    row = (j % 2) * PART + i * PIECE
                    if block < 3:
                        cols = slice(block * channels + g * 128, block * channels + (g + 1) * 128)
                        o_qkv[row : row + PIECE, cols] = part
                    else:
                        for u in range(0, PIECE, SLOT):
                            at = row + u
                            tile = at // 128
                            o_proj[g * 128 + at % 128 : g * 128 + at % 128 + SLOT, tile * 128 : (tile + 1) * 128] = (
                                part[u : u + SLOT]
                            )

    count = GROUP * ROWS // UNIT
    rest = WLAT * SPREAD - 128
    for b in range(4):
        at = (b // 2) * UNIT
        units = [
            [full[g, b % 2, u // 4, u % 4, PIECE:].astype(F32)[at : at + UNIT] for u in range(2 * count + 1)]
            for g in range(groups)
        ]
        for t in range(2):
            tile = jnp.concatenate([u for g in range(groups) for u in units[g][t * count : (t + 1) * count]], axis=0)
            wide[b, :, t * 256 : t * 256 + 128] = nn(reorder[...], tile.astype(BF))
        ends = jnp.concatenate(
            [units[g][2 * count][:, i * 2 * rest : (i + 1) * 2 * rest] for g in range(groups) for i in range(count)],
            axis=0,
        )
        ends = nn(reorder[...], ends.astype(BF))
        wide[b, :, 128 : 128 + rest] = ends[:, :rest]
        wide[b, :, 384 : 384 + rest] = ends[:, rest:]
    for kind in range(4):
        band = jnp.int32(0)
        for b in range(1, 4):
            band = jnp.where(types[b] == kind, b, band)
        table_rows = wide[band]
        parts = []
        for lq in range(WPL):
            for lk in range(WPL):
                for a in range(WLAT):
                    row = (lq * WLAT + a) * heads
                    parts.append(table_rows[row : row + heads, lk * 256 : lk * 256 + WLAT * SPREAD])
        typed[:, kind, :] = jnp.concatenate(parts, axis=1)
    o_table[...] = typed[...].astype(BF)
    outward.wait()


def local(tokens, cotangent, mask_ids, band_type, bias_table, w_qkv, w_proj, ln_gain, ln_shift):
    lon_cols, channels = tokens.shape[2:]
    groups = channels // 128
    heads = groups * GROUP
    half_lat = WLAT // 2
    count = WPL * WLAT * lon_cols
    span = GROUP * WINDOW
    route = token_route(lon_cols)
    constants = [
        jnp.asarray(c, BF)
        for c in (
            route, route.T, head_order(), table_order(), head_blocks(128 // GROUP), gather_heads(), row_order(heads)
        )
    ]
    anywhere = pl.BlockSpec(memory_space=pl.ANY)
    scalars = pl.BlockSpec(memory_space=pltpu.SMEM)
    vmem = pl.BlockSpec(memory_space=pltpu.VMEM)
    dma = pltpu.SemaphoreType.DMA
    bf = lambda *shape: pltpu.VMEM(shape, BF)
    f32 = lambda *shape: pltpu.VMEM(shape, F32)
    pairs = lambda *shape: [dma(shape), dma(shape)]
    pieces = (groups, 2, 4, 4, PIECE + SLOT, 128)
    table = bias_table.transpose(1, 0, 2)
    joined, full, small = pl.pallas_call(
        whole_kernel,
        out_shape=(
            jax.ShapeDtypeStruct(tokens.shape, BF),
            jax.ShapeDtypeStruct(pieces, BF),
            jax.ShapeDtypeStruct((8, 128), F32),
        ),
        in_specs=[scalars] * 2 + [anywhere] * 5 + [vmem] * 2 + [anywhere] * 7,
        out_specs=(anywhere, anywhere, vmem),
        scratch_shapes=[
            bf(2, WPL, half_lat, lon_cols, 2 * channels),
            bf(2, WPL, half_lat, EDGE, 2 * channels),
            bf(*tokens.shape),
            bf(*tokens.shape),
            bf(*table.shape),
            bf(channels, 3 * channels),
            bf(channels, channels),
            *[bf(*c.shape) for c in constants],
            f32(heads * ROWS, 512),
            f32(SPREAD * ROWS, heads * ROWS),
            f32(2, SPREAD * ROWS, 128),
            f32(groups, WINDOW, span),
            f32(WINDOW, span),
            f32(count, channels),
            f32(count, 1),
            bf(count, channels),
            bf(channels, count),
            bf(count, channels),
            bf(count, 3 * channels),
            bf(count, channels),
            bf(count, channels),
            bf(count, 3 * channels),
            bf(2, WPL, half_lat, lon_cols, channels),
            bf(2, WPL, half_lat, EDGE, channels),
            bf(WPL, half_lat, lon_cols, channels),
            bf(2, WPL, half_lat, EDGE, channels),
            bf(groups, 4, channels, 128),
            bf(groups, 4, 2 * SLOT, 128),
            bf(groups, 2, channels, 128),
            bf(groups, 4, PART + 2 * SLOT, 128),
            bf(groups, 4, PART + 2 * SLOT, 128),
            bf(groups, 4, PIECE + SLOT, 128),
            bf(groups, 4, PIECE + SLOT, 128),
            bf(groups, Z_SIZE, PIECE + SLOT, 128),
            bf(*pieces),
            f32(8, 128),
            f32(8, 128),
            f32(X_SIZE, 8, 128),
            f32(Y_SIZE, 8, 128),
            f32(Z_SIZE, 8, 128),
            dma((12 + 3 * groups,)),
            dma((2 * groups + 1,)),
            *pairs(6), *pairs(3), *pairs(groups), *pairs(groups, 4), *pairs(groups, 4), *pairs(groups, Z_SIZE),
            *pairs(groups, 4), *pairs(groups, 4), *pairs(groups, 4),
            *pairs(1), *pairs(X_SIZE), *pairs(Y_SIZE), *pairs(Z_SIZE),
        ],
        compiler_params=pltpu.CompilerParams(
            collective_id=0, has_side_effects=True, vmem_limit_bytes=56 * 1024 * 1024
        ),
        cost_estimate=pl.CostEstimate(flops=6_000_000_000, bytes_accessed=10_000_000, transcendentals=1_000_000),
    )(mask_ids, band_type, tokens, cotangent, table, w_qkv, w_proj, ln_gain, ln_shift, *constants)
    d_tokens, g_qkv, g_proj, g_table, g_gain, g_shift = pl.pallas_call(
        assemble_kernel,
        out_shape=(
            jax.ShapeDtypeStruct(tokens.shape, BF),
            jax.ShapeDtypeStruct((channels, 3 * channels), BF),
            jax.ShapeDtypeStruct((channels, channels), BF),
            jax.ShapeDtypeStruct(table.shape, BF),
            jax.ShapeDtypeStruct((channels,), F32),
            jax.ShapeDtypeStruct((channels,), F32),
        ),
        in_specs=[scalars, anywhere, anywhere, vmem, vmem],
        out_specs=(anywhere, vmem, vmem, vmem, vmem, vmem),
        scratch_shapes=[
            bf(*pieces),
            bf(*tokens.shape),
            f32(4, heads * ROWS, 512),
            f32(*table.shape),
            dma((groups + 2,)),
        ],
        compiler_params=pltpu.CompilerParams(vmem_limit_bytes=60 * 1024 * 1024),
        cost_estimate=pl.CostEstimate(flops=100_000_000, bytes_accessed=6_000_000, transcendentals=0),
    )(band_type, full, joined, small, constants[-1])
    return d_tokens, g_qkv, g_proj, g_gain, g_shift, g_table.transpose(1, 0, 2)


def solution(mesh):
    placed = (P(None, "lat", "lon", None),) * 2 + (P(None, "lat"),) + (P(),) * 6
    return jax.shard_map(
        local,
        mesh=mesh,
        in_specs=placed,
        out_specs=(P(None, "lat", "lon", None), P(), P(), P(), P(), P()),
        check_vma=False,
    )
```

```python
import jax
import jax.numpy as jnp
import numpy as np
from jax import lax
from jax.experimental import pallas as pl
from jax.experimental.pallas import tpu as pltpu
from jax.sharding import PartitionSpec as P

WPL, WLAT, WLON = 2, 6, 12
WINDOW = WPL * WLAT * WLON
ROWS = WPL * WLAT
SPREAD = 2 * WLON - 1
EDGE = 16
X_SIZE, Y_SIZE, Z_SIZE = 4, 4, 8
PART = 192
PIECE = 48
SLOT = 16
UNIT = 8
MESH = pl.DeviceIdType.MESH
GROUP = 4
EPSILON = 1e-05
LOG2E = 1.4426950408889634
BF = jnp.bfloat16
F32 = jnp.float32


def token_route(lon_cols):
    half_lat, half_lon = WLAT // 2, WLON // 2
    windows = lon_cols // WLON
    near = WPL * half_lat * lon_cols
    far = WPL * half_lat * EDGE
    route = np.zeros((windows * WINDOW, 2 * near + 2 * far), np.float32)
    for w in range(windows):
        for o in range(WLON):
            for l in range(WPL):
                for a in range(WLAT):
                    level = (l + 1) % WPL
                    col = w * WLON + o + half_lon
                    row = level * half_lat + a % half_lat
                    if col < lon_cols:
                        source = row * lon_cols + col + (near if a >= half_lat else 0)
                    else:
                        source = 2 * near + row * EDGE + col - lon_cols
                        source += far if a >= half_lat else 0
                    route[w * WINDOW + o * ROWS + l * WLAT + a, source] = 1.0
    return route


def head_order():
    perm = np.zeros((GROUP * WINDOW, GROUP * WINDOW), np.float32)
    for o in range(WLON):
        for h in range(GROUP):
            for r in range(ROWS):
                perm[(o * GROUP + h) * ROWS + r, (h * WLON + o) * ROWS + r] = 1.0
    return perm


def table_order():
    order = np.zeros((SPREAD * ROWS, 512), np.float32)
    for d in range(SPREAD):
        for l in range(WPL):
            for a in range(WLAT):
                order[(SPREAD - 1 - d) * ROWS + l * WLAT + a, l * 256 + a * SPREAD + d] = 1.0
    return order


def row_order(heads):
    order = np.zeros((heads * ROWS, heads * ROWS), np.float32)
    for h in range(heads):
        for r in range(ROWS):
            order[r * heads + h, h * ROWS + r] = 1.0
    return order


def head_blocks(head_dim):
    rows = np.arange(GROUP * head_dim)[:, None] // head_dim
    cols = np.arange(GROUP * WINDOW)[None, :] // WINDOW
    return (rows == cols).astype(np.float32)


def gather_heads():
    return np.tile(np.eye(WINDOW, dtype=np.float32), (1, GROUP))


def nn(a, b):
    return lax.dot_general(a, b, (((1,), (0,)), ((), ())), preferred_element_type=F32)


def nt(a, b):
    return lax.dot_general(a, b, (((1,), (1,)), ((), ())), preferred_element_type=F32)


def tn(a, b):
    return lax.dot_general(a, b, (((0,), (0,)), ((), ())), preferred_element_type=F32)


def place():
    lon = lax.axis_index("lon")
    lat = lax.axis_index("lat")
    x = lax.rem(lon, X_SIZE)
    z = lax.rem(lon // X_SIZE, Z_SIZE)
    y = (lat // 2) * 2 + lon // (X_SIZE * Z_SIZE)
    return x, y, z, lax.rem(lat, 2)


def device(x, y, z, core):
    return ((lax.rem(y, 2) * Z_SIZE + z) * X_SIZE + x, (y // 2) * 2 + core)


def whole_kernel(
    ids, types, tokens, cotangent, table_h, w_qkv_h, w_proj_h, gain_v, shift_v,
    route_h, unroute_h, perm_h, order_h, blocks_h, gather_h, reorder_h,
    o_tokens, o_full, o_small,
    cat, edge, cot_own, joined, table, w_qkv, w_proj, route, unroute, perm, order, blocks, gather, reorder,
    tall, folded, summed, bias, d_bias, normed, inv, ln, ln_t, cot, qkv, d_att, att, d_qkv,
    d_main, d_edge, back_main, back_edge,
    grads, tables, core_in, s1_out, s1_in, s2_out, s2_in, z_in, full, small, small_core, small_x, small_y, small_z,
    load_s, out_s, halo_s, halo_r, back_s, back_r, core_s, core_r, s1_s, s1_r, s2_s, s2_r, z_s, z_r, g2_s, g2_r, g1_s, g1_r,
    sib_s, sib_r, mc_s, mc_r, mx_s, mx_r, my_s, my_r, mz_s, mz_r,
):
    half_lat = WLAT // 2
    half_lon = WLON // 2
    lon_cols = tokens.shape[2]
    channels = tokens.shape[3]
    main = 2 * WPL * half_lat * lon_cols
    groups = channels // 128
    heads = groups * GROUP
    windows = lon_cols // WLON
    span = GROUP * WINDOW
    head_dim = 128 // GROUP
    scale = head_dim ** -0.5
    x, y, z, core = place()
    other = 1 - core
    beside = x + 1 - 2 * lax.rem(x, 2)
    across = lax.rem(y + 2, Y_SIZE)
    y_up = lax.rem(y + 2 * other, Y_SIZE)
    y_down = lax.rem(y + 2 * core, Y_SIZE)
    sibling = device(x, y, z, other)

    loads = [
        pltpu.make_async_copy(src, dst, load_s.at[i])
        for i, (src, dst) in enumerate((
            (table_h, table), (order_h, order), (reorder_h, reorder), (perm_h, perm),
            (tokens.at[:, pl.ds(half_lat, half_lat)], cat.at[0, :, :, :, pl.ds(0, channels)]),
            (cotangent.at[:, pl.ds(half_lat, half_lat)], cat.at[0, :, :, :, pl.ds(channels, channels)]),
            (route_h, route), (w_proj_h, w_proj), (blocks_h, blocks), (gather_h, gather),
            (unroute_h, unroute), (cotangent, cot_own),
            *(
                (
                    w_qkv_h.at[:, pl.ds(b * channels + g * 128, 128)],
                    w_qkv.at[:, pl.ds((3 * g + b) * 128, 128)],
                )
                for g in range(groups)
                for b in range(3)
            ),
        ))
    ]
    barrier = pltpu.get_barrier_semaphore()
    friends = [sibling, device(x, across, z, other), device(beside, y, z, other), device(beside, across, z, other)]
    friends += [device(lax.rem(x + i, X_SIZE), y, z, core) for i in range(1, X_SIZE)]
    friends += [device(x, lax.rem(y + i, Y_SIZE), z, core) for i in range(1, Y_SIZE)]
    friends += [device(x, y, lax.rem(z + i, Z_SIZE), core) for i in range(1, Z_SIZE)]
    for friend in friends:
        pl.semaphore_signal(barrier, inc=1, device_id=friend, device_id_type=MESH)
    for load in loads:
        load.start()
    pl.semaphore_wait(barrier, len(friends))

    def remote(src, dst, send, recv, target):
        return pltpu.make_async_remote_copy(
            src_ref=src, dst_ref=dst, send_sem=send, recv_sem=recv, device_id=target, device_id_type=MESH
        )

    first, last = pl.ds(0, half_lat), pl.ds(half_lat, half_lat)
    halos = []
    for i, array in enumerate((tokens, cotangent)):
        lanes = pl.ds(i * channels, channels)
        up = device(x, y_up, z, other)
        halos += [
            (array.at[:, first], cat.at[1, :, :, :, lanes], up),
            (array.at[:, last, pl.ds(0, EDGE)], edge.at[0, :, :, :, lanes], device(beside, y, z, core)),
            (array.at[:, first, pl.ds(0, EDGE)], edge.at[1, :, :, :, lanes], device(beside, y_up, z, other)),
        ]
    halos = [remote(src, dst, halo_s.at[i], halo_r.at[i], to) for i, (src, dst, to) in enumerate(halos)]
    for copy in halos:
        copy.start()

    for load in loads[:4]:
        load.wait()
    own_type = types[lax.axis_index("lat")]
    picked = (lax.broadcasted_iota(jnp.int32, (1, 4, 1), 1) == own_type).astype(F32)
    rows_of_type = jnp.sum(table[...].astype(F32) * picked, axis=1)
    tall[...] = jnp.zeros_like(tall)
    for lq in range(WPL):
        for lk in range(WPL):
            for a in range(WLAT):
                start = ((lq * WPL + lk) * WLAT + a) * WLAT * SPREAD
                row = (lq * WLAT + a) * heads
                tall[row : row + heads, lk * 256 : lk * 256 + WLAT * SPREAD] = rows_of_type[:, start : start + WLAT * SPREAD]
    laid = nt(order[...], tall[...].astype(BF)).astype(BF)
    folded[...] = nn(laid, reorder[...])
    lane = lax.rem(lax.broadcasted_iota(jnp.int32, (1, span), 1), ROWS)
    sub = lax.rem(lax.broadcasted_iota(jnp.int32, (WINDOW, 1), 0), ROWS)
    id_q = jnp.zeros((1, span), jnp.int32)
    id_k = jnp.zeros((WINDOW, 1), jnp.int32)
    for l in range(WPL):
        for a in range(WLAT):
            value = ids[l, a]
            id_q = jnp.where(lane == l * WLAT + a, value, id_q)
            id_k = jnp.where(sub == l * WLAT + a, value, id_k)
    masked = jnp.where(id_k == id_q, 0.0, -1e30)
    for g in range(groups):
        pieces = [
            folded[(WLON - 1 - o) * ROWS : (WLON - 1 - o) * ROWS + WINDOW, g * GROUP * ROWS : (g + 1) * GROUP * ROWS]
            for o in range(WLON)
        ]
        spread = jnp.concatenate(pieces, axis=1).astype(BF)
        bias[g] = nn(spread, perm[...]) * LOG2E + masked

    gain = gain_v[...].reshape(1, channels)
    shift = shift_v[...].reshape(1, channels)
    for load in loads[4:]:
        load.wait()
    for copy in halos[:3]:
        copy.wait_recv()
    x_in = nn(route[:, :main], cat[..., :channels].reshape(main, channels))
    x_in = x_in + nn(route[:, main:], edge[..., :channels].reshape(-1, channels))
    average = jnp.mean(x_in, axis=1, keepdims=True)
    centred = x_in - average
    variance = jnp.mean(centred * centred, axis=1, keepdims=True)
    inv_std = lax.rsqrt(variance + EPSILON)
    inv[...] = inv_std
    norm = centred * inv_std
    normed[...] = norm
    ln_out = (norm * gain + shift).astype(BF)
    ln[...] = ln_out
    ln_t[...] = ln_out.T
    qkv[...] = nn(ln[...], w_qkv[...]).astype(BF)
    for copy in halos[3:]:
        copy.wait_recv()
    moved = nn(route[:, :main], cat[..., channels:].reshape(main, channels))
    moved = moved + nn(route[:, main:], edge[..., channels:].reshape(-1, channels))
    cot[...] = moved.astype(BF)
    d_att[...] = nt(cot[...], w_proj[...]).astype(BF)

    lanes = lax.broadcasted_iota(jnp.int32, (1, 128), 1) // head_dim
    own = [(lanes == h).astype(F32).astype(BF) for h in range(GROUP)]
    eye = (
        lax.broadcasted_iota(jnp.int32, (128, 128), 0) == lax.broadcasted_iota(jnp.int32, (128, 128), 1)
    ).astype(F32).astype(BF)

    def attend(g, w):
        rows = pl.ds(pl.multiple_of(w * WINDOW, WINDOW), WINDOW)
        q_cols, k_cols, v_cols = (slice((3 * g + b) * 128, (3 * g + b + 1) * 128) for b in range(3))
        cols = slice(g * 128, (g + 1) * 128)
        q, k, v, da = qkv[rows, q_cols], qkv[rows, k_cols], qkv[rows, v_cols], d_att[rows, cols]
        q_heads = jnp.concatenate([q * own[h] for h in range(GROUP)], axis=0)
        da_heads = jnp.concatenate([da * own[h] for h in range(GROUP)], axis=0)
        raised = jnp.exp2(nt(k, q_heads) * (scale * LOG2E) + bias[g])
        probs = raised * (1.0 / jnp.sum(raised, axis=0, keepdims=True))
        probs_b = probs.astype(BF)
        weighted = probs * nt(v, da_heads)
        d_scores = weighted - probs * jnp.sum(weighted, axis=0, keepdims=True)
        d_scores_b = d_scores.astype(BF)
        mask = blocks[...]
        att_t = tn(v, probs_b).astype(BF) * mask
        dq_t = (tn(k, d_scores_b) * scale).astype(BF) * mask

        def store():
            joint = nt(gather[...], jnp.concatenate([att_t, dq_t], axis=0)).astype(BF)
            att[rows, cols] = joint[:, :128]
            d_qkv[rows, q_cols] = joint[:, 128:]
            d_qkv[rows, k_cols] = (nn(d_scores_b, q_heads) * scale).astype(BF)
            d_qkv[rows, v_cols] = nn(probs_b, da_heads).astype(BF)

        return d_scores, store

    def two_windows(g, w):
        left, store_left = attend(g, w)
        right, store_right = attend(g, w + 1)
        store_left()
        store_right()
        return left + right

    def gradients(g):
        weights = nn(ln_t[...], d_qkv[:, 3 * g * 128 : 3 * (g + 1) * 128]).astype(BF)
        for b in range(3):
            grads[g, b] = weights[:, b * 128 : (b + 1) * 128]
        proj = tn(att[:, g * 128 : (g + 1) * 128], cot[...]).astype(BF)
        for t in range(groups):
            grads[g, 3, t * 128 : (t + 1) * 128] = proj[:, t * 128 : (t + 1) * 128]

    def fold(g):
        spread = nt(d_bias[...].astype(BF), perm[...])
        for part in range(2):
            summed[part] = jnp.zeros(summed.shape[1:], F32)
        for o in range(WLON):
            start = (WLON - 1 - o) * ROWS
            start += start % UNIT
            summed[o % 2, start : start + WINDOW, : GROUP * ROWS] += spread[:, o * GROUP * ROWS : (o + 1) * GROUP * ROWS]
        shifted = UNIT // 2
        rows = SPREAD * ROWS
        laid = summed[0, shifted : shifted + rows, : GROUP * ROWS] + summed[1, :rows, : GROUP * ROWS]
        rows = tn(laid.astype(BF), order[...])
        rest = WLAT * SPREAD - 128
        ends = jnp.concatenate([rows[:, 128 : 128 + rest], rows[:, 384 : 384 + rest]], axis=1)
        count = GROUP * ROWS // UNIT
        packed = [ends[i * UNIT : (i + 1) * UNIT] for i in range(count)]
        packed = jnp.concatenate([*packed, jnp.zeros((UNIT, 128 - count * 2 * rest), F32)], axis=1)
        laid = jnp.concatenate(
            [rows[:, :128], rows[:, 256:384], packed, jnp.zeros((16 * UNIT - (2 * count + 1) * UNIT, 128), F32)], axis=0
        ).astype(BF)
        for j in range(4):
            tables[g, j] = laid[j * 2 * SLOT : (j + 1) * 2 * SLOT]

    p1 = jnp.where(core == 0, x, y)
    p2 = jnp.where(core == 0, y, x)

    def on1(p):
        return device(jnp.where(core == 0, p, x), jnp.where(core == 0, y, p), z, core)

    def on2(p):
        return device(jnp.where(core == 0, x, p), jnp.where(core == 0, p, y), z, core)

    def after1(i):
        return lax.rem(p1 + i, 4)

    def after2(i):
        return lax.rem(p2 + i, 4)

    def core_copy(g):
        return remote(grads.at[g, pl.ds(2 * other, 2)], core_in.at[g], core_s.at[g], core_r.at[g], sibling)

    def s1_copy(g, peer):
        return remote(s1_out.at[g, peer], s1_in.at[g, p1], s1_s.at[g, peer], s1_r.at[g, p1], on1(peer))

    def s1_take(g, peer):
        return remote(s1_out.at[g, peer], s1_in.at[g, peer], s1_s.at[g, peer], s1_r.at[g, peer], on1(peer))

    def s2_copy(g, peer):
        return remote(s2_out.at[g, peer], s2_in.at[g, p2], s2_s.at[g, peer], s2_r.at[g, p2], on2(peer))

    def s2_take(g, peer):
        return remote(s2_out.at[g, peer], s2_in.at[g, peer], s2_s.at[g, peer], s2_r.at[g, peer], on2(peer))

    def z_copy(g, peer, slot):
        return remote(z_in.at[g, slot], z_in.at[g, slot], z_s.at[g, peer], z_r.at[g, slot], device(x, y, peer, core))

    def g2_copy(g, peer, slot):
        here = full.at[g, core, p1, slot]
        return remote(here, here, g2_s.at[g, peer], g2_r.at[g, slot], on2(peer))

    def g1_copy(g, peer, slot):
        here = full.at[g, core, slot]
        return remote(here, here, g1_s.at[g, peer], g1_r.at[g, slot], on1(peer))

    def sib_copy(g, half, slot):
        here = full.at[g, half, slot]
        return remote(here, here, sib_s.at[g, slot], sib_r.at[g, slot], sibling)

    def step0(g):
        core_copy(g).start()

    def step1(g):
        core_copy(g).wait_recv()
        def fill(j):
            half = j // 2
            rows = pl.ds(pl.multiple_of((j - 2 * half) * PART, PART), PART)
            added = grads[g, 2 * core + half, rows].astype(F32) + core_in[g, half, rows].astype(F32)
            s1_out[g, j, :PART] = added.astype(BF)
            s1_out[g, j, PART:] = tables[g, j]

        for i in (2, 1, 3):
            fill(after1(i))
            s1_copy(g, after1(i)).start()
        fill(p1)

    def step2(g):
        def split(part, source):
            high = jnp.where(core == 0, y, source) // 2
            low_rows = jnp.where(high == 0, part[PART:], jnp.zeros_like(part[PART:]))
            return part[:PART], low_rows, part[PART:] - low_rows

        w, t0, t1 = split(s1_out[g, p1].astype(F32), p1)
        for i in (1, 3, 2):
            source = after1(i)
            s1_take(g, source).wait_recv()
            more = split(s1_in[g, source].astype(F32), source)
            w, t0, t1 = w + more[0], t0 + more[1], t1 + more[2]
        for j in range(4):
            s2_out[g, j] = jnp.concatenate(
                [w[j * PIECE : (j + 1) * PIECE], t0[j * UNIT : (j + 1) * UNIT], t1[j * UNIT : (j + 1) * UNIT]], axis=0
            ).astype(BF)
        for i in (2, 1, 3):
            s2_copy(g, after2(i)).start()

    def step3(g):
        total = s2_out[g, p2].astype(F32)
        for i in (1, 3, 2):
            source = after2(i)
            s2_take(g, source).wait_recv()
            total = total + s2_in[g, source].astype(F32)
        z_in[g, z] = total.astype(BF)
        for i in (4, 3, 5, 2, 6, 1, 7):
            z_copy(g, lax.rem(z + i, Z_SIZE), z).start()

    def step4(g):
        for i in (1, 7, 2, 6, 3, 5, 4):
            source = lax.rem(z + i, Z_SIZE)
            z_copy(g, source, source).wait_recv()
        total = z_in[g, 0].astype(F32)
        for i in range(1, Z_SIZE):
            total = total + z_in[g, i].astype(F32)
        full[g, core, p1, p2] = total.astype(BF)
        for i in (2, 1, 3):
            g2_copy(g, after2(i), p2).start()

    def step5(g):
        for i in (1, 3, 2):
            source = after2(i)
            g2_copy(g, source, source).wait_recv()
        for i in (2, 1, 3):
            g1_copy(g, after1(i), p1).start()
        sib_copy(g, core, p1).start()

    def step6(g):
        for i in (1, 3, 2):
            source = after1(i)
            g1_copy(g, source, source).wait_recv()
            sib_copy(g, core, source).start()
        full_copy(g, core, 0).start()

    def step7(g):
        for i in range(4):
            sib_copy(g, other, i).wait_recv()
        full_copy(g, other, 1).start()

    def full_copy(g, half, i):
        return pltpu.make_async_copy(full.at[g, half], o_full.at[g, half], out_s.at[2 * g + i])

    def tokens_copy():
        return pltpu.make_async_copy(joined, o_tokens, out_s.at[2 * groups])

    def finish(g):
        core_copy(g).wait_send()
        for i in range(1, 4):
            s1_copy(g, after1(i)).wait_send()
            s2_copy(g, after2(i)).wait_send()
            g2_copy(g, after2(i), p2).wait_send()
        for i in range(1, Z_SIZE):
            z_copy(g, lax.rem(z + i, Z_SIZE), z).wait_send()

    def finish_gather(g):
        for i in range(1, 4):
            g1_copy(g, after1(i), p1).wait_send()
        for i in range(4):
            sib_copy(g, core, i).wait_send()

    def mc_copy():
        return remote(small, small_core, mc_s.at[0], mc_r.at[0], sibling)

    def mx_copy(peer, slot):
        return remote(small_x.at[slot], small_x.at[slot], mx_s.at[peer], mx_r.at[slot], device(peer, y, z, core))

    def my_copy(peer, slot):
        return remote(small_y.at[slot], small_y.at[slot], my_s.at[peer], my_r.at[slot], device(x, peer, z, core))

    def mz_copy(peer, slot):
        return remote(small_z.at[slot], small_z.at[slot], mz_s.at[peer], mz_r.at[slot], device(x, y, peer, core))

    def small_share(copy, buffer, place_here, size, value):
        buffer[place_here] = value
        for i in range(1, size):
            copy(lax.rem(place_here + i, size), place_here).start()

    def small_sum(copy, buffer, place_here, size):
        for i in range(1, size):
            source = lax.rem(place_here + i, size)
            copy(source, source).wait_recv()
        total = buffer[0]
        for i in range(1, size):
            total = total + buffer[i]
        return total

    def small_finish():
        mc_copy().wait_send()
        for copy, here, size in ((mx_copy, x, X_SIZE), (my_copy, y, Y_SIZE), (mz_copy, z, Z_SIZE)):
            for i in range(1, size):
                copy(lax.rem(here + i, size), here).wait_send()

    def group(g, between):
        d_bias[...] = two_windows(g, 0)
        between()
        d_bias[...] += two_windows(g, 2)
        gradients(g)
        step0(g)
        fold(g)

    def nothing():
        pass

    group(0, nothing)
    step1(0)
    group(1, nothing)
    step1(1)
    group(2, lambda: step2(0))
    step1(2)
    step3(0)
    step2(1)

    d_ln = nt(d_qkv[...], w_qkv[...])
    norm = normed[...]
    small[...] = jnp.zeros_like(small)
    for g in range(groups):
        cols = slice(g * 128, (g + 1) * 128)
        small[g : g + 1] = jnp.sum(d_ln[:, cols] * norm[:, cols], axis=0, keepdims=True)
        small[groups + g : groups + g + 1] = jnp.sum(d_ln[:, cols], axis=0, keepdims=True)
    mc_copy().start()
    scaled = d_ln * gain
    d_flat = inv[...] * (
        scaled
        - jnp.mean(scaled, axis=1, keepdims=True)
        - norm * jnp.mean(scaled * norm, axis=1, keepdims=True)
    )
    d_flat = d_flat.astype(BF)
    d_main[...] = nn(unroute[:main], d_flat).astype(BF).reshape(d_main.shape)
    d_edge[...] = nn(unroute[main:], d_flat).astype(BF).reshape(d_edge.shape)
    backs = [
        remote(d_main.at[1], back_main, back_s.at[0], back_r.at[0], device(x, y_down, z, other)),
        remote(d_edge.at[0], back_edge.at[0], back_s.at[1], back_r.at[1], device(beside, y, z, core)),
        remote(d_edge.at[1], back_edge.at[1], back_s.at[2], back_r.at[2], device(beside, y_down, z, other)),
    ]
    for copy in backs:
        copy.start()
    step2(2)
    step3(1)
    mc_copy().wait_recv()
    small_share(mx_copy, small_x, x, X_SIZE, small[...] + small_core[...])
    step4(0)
    step3(2)
    small_share(my_copy, small_y, y, Y_SIZE, small_sum(mx_copy, small_x, x, X_SIZE))
    step5(0)
    small_share(mz_copy, small_z, z, Z_SIZE, small_sum(my_copy, small_y, y, Y_SIZE))

    for copy in backs:
        copy.wait_recv()
    for l in range(WPL):
        for a in range(WLAT):
            if a < half_lat:
                inner, outer = back_main[l, a], back_edge[1, l, a]
            else:
                inner, outer = d_main[0, l, a - half_lat], back_edge[0, l, a - half_lat]
            value = cot_own[l, a].astype(F32) + inner.astype(F32)
            joined[l, a, EDGE:] = value[EDGE:].astype(BF)
            joined[l, a, :EDGE] = (value[:EDGE] + outer.astype(F32)).astype(BF)
    tokens_copy().start()
    step4(1)
    step4(2)
    step6(0)
    step5(1)
    step7(0)
    o_small[...] = small_sum(mz_copy, small_z, z, Z_SIZE)
    step5(2)
    step6(1)
    step7(1)

    for copy in halos + backs:
        copy.wait_send()
    small_finish()
    for g in range(groups):
        finish(g)
    finish_gather(0)
    finish_gather(1)
    step6(2)
    step7(2)
    finish_gather(2)
    tokens_copy().wait()
    for g in range(groups):
        full_copy(g, core, 0).wait()
        full_copy(g, other, 1).wait()


def assemble_kernel(
    types, full_h, joined_h, small, reorder,
    o_tokens, o_qkv, o_proj, o_table, o_gain, o_shift,
    full, joined, wide, typed, sem,
):
    channels = o_proj.shape[0]
    groups = channels // 128
    heads = groups * GROUP
    loads = [pltpu.make_async_copy(full_h.at[g], full.at[g], sem.at[g]) for g in range(groups)]
    inward = pltpu.make_async_copy(joined_h, joined, sem.at[groups])
    outward = pltpu.make_async_copy(joined, o_tokens, sem.at[groups + 1])
    for load in loads:
        load.start()
    inward.start()
    o_gain[...] = jnp.concatenate([small[g : g + 1] for g in range(groups)], axis=1).reshape(channels)
    o_shift[...] = jnp.concatenate([small[g : g + 1] for g in range(groups, 2 * groups)], axis=1).reshape(channels)
    inward.wait()
    outward.start()
    for g in range(groups):
        loads[g].wait()
        for half in range(2):
            for j in range(4):
                for i in range(4):
                    part = full[g, half, j, i, :PIECE]
                    block = 2 * half + j // 2
                    row = (j % 2) * PART + i * PIECE
                    if block < 3:
                        cols = slice(block * channels + g * 128, block * channels + (g + 1) * 128)
                        o_qkv[row : row + PIECE, cols] = part
                    else:
                        for u in range(0, PIECE, SLOT):
                            at = row + u
                            tile = at // 128
                            o_proj[g * 128 + at % 128 : g * 128 + at % 128 + SLOT, tile * 128 : (tile + 1) * 128] = (
                                part[u : u + SLOT]
                            )

    count = GROUP * ROWS // UNIT
    rest = WLAT * SPREAD - 128
    for b in range(4):
        at = (b // 2) * UNIT
        units = [
            [full[g, b % 2, u // 4, u % 4, PIECE:].astype(F32)[at : at + UNIT] for u in range(2 * count + 1)]
            for g in range(groups)
        ]
        for t in range(2):
            tile = jnp.concatenate([u for g in range(groups) for u in units[g][t * count : (t + 1) * count]], axis=0)
            wide[b, :, t * 256 : t * 256 + 128] = nn(reorder[...], tile.astype(BF))
        ends = jnp.concatenate(
            [units[g][2 * count][:, i * 2 * rest : (i + 1) * 2 * rest] for g in range(groups) for i in range(count)],
            axis=0,
        )
        ends = nn(reorder[...], ends.astype(BF))
        wide[b, :, 128 : 128 + rest] = ends[:, :rest]
        wide[b, :, 384 : 384 + rest] = ends[:, rest:]
    for kind in range(4):
        band = jnp.int32(0)
        for b in range(1, 4):
            band = jnp.where(types[b] == kind, b, band)
        table_rows = wide[band]
        parts = []
        for lq in range(WPL):
            for lk in range(WPL):
                for a in range(WLAT):
                    row = (lq * WLAT + a) * heads
                    parts.append(table_rows[row : row + heads, lk * 256 : lk * 256 + WLAT * SPREAD])
        typed[:, kind, :] = jnp.concatenate(parts, axis=1)
    o_table[...] = typed[...].astype(BF)
    outward.wait()


def local(tokens, cotangent, mask_ids, band_type, bias_table, w_qkv, w_proj, ln_gain, ln_shift):
    lon_cols, channels = tokens.shape[2:]
    groups = channels // 128
    heads = groups * GROUP
    half_lat = WLAT // 2
    count = WPL * WLAT * lon_cols
    span = GROUP * WINDOW
    route = token_route(lon_cols)
    constants = [
        jnp.asarray(c, BF)
        for c in (
            route, route.T, head_order(), table_order(), head_blocks(128 // GROUP), gather_heads(), row_order(heads)
        )
    ]
    anywhere = pl.BlockSpec(memory_space=pl.ANY)
    scalars = pl.BlockSpec(memory_space=pltpu.SMEM)
    vmem = pl.BlockSpec(memory_space=pltpu.VMEM)
    dma = pltpu.SemaphoreType.DMA
    bf = lambda *shape: pltpu.VMEM(shape, BF)
    f32 = lambda *shape: pltpu.VMEM(shape, F32)
    pairs = lambda *shape: [dma(shape), dma(shape)]
    pieces = (groups, 2, 4, 4, PIECE + SLOT, 128)
    table = bias_table.transpose(1, 0, 2)
    joined, full, small = pl.pallas_call(
        whole_kernel,
        out_shape=(
            jax.ShapeDtypeStruct(tokens.shape, BF),
            jax.ShapeDtypeStruct(pieces, BF),
            jax.ShapeDtypeStruct((8, 128), F32),
        ),
        in_specs=[scalars] * 2 + [anywhere] * 5 + [vmem] * 2 + [anywhere] * 7,
        out_specs=(anywhere, anywhere, vmem),
        scratch_shapes=[
            bf(2, WPL, half_lat, lon_cols, 2 * channels),
            bf(2, WPL, half_lat, EDGE, 2 * channels),
            bf(*tokens.shape),
            bf(*tokens.shape),
            bf(*table.shape),
            bf(channels, 3 * channels),
            bf(channels, channels),
            *[bf(*c.shape) for c in constants],
            f32(heads * ROWS, 512),
            f32(SPREAD * ROWS, heads * ROWS),
            f32(2, SPREAD * ROWS + UNIT // 2, 128),
            f32(groups, WINDOW, span),
            f32(WINDOW, span),
            f32(count, channels),
            f32(count, 1),
            bf(count, channels),
            bf(channels, count),
            bf(count, channels),
            bf(count, 3 * channels),
            bf(count, channels),
            bf(count, channels),
            bf(count, 3 * channels),
            bf(2, WPL, half_lat, lon_cols, channels),
            bf(2, WPL, half_lat, EDGE, channels),
            bf(WPL, half_lat, lon_cols, channels),
            bf(2, WPL, half_lat, EDGE, channels),
            bf(groups, 4, channels, 128),
            bf(groups, 4, 2 * SLOT, 128),
            bf(groups, 2, channels, 128),
            bf(groups, 4, PART + 2 * SLOT, 128),
            bf(groups, 4, PART + 2 * SLOT, 128),
            bf(groups, 4, PIECE + SLOT, 128),
            bf(groups, 4, PIECE + SLOT, 128),
            bf(groups, Z_SIZE, PIECE + SLOT, 128),
            bf(*pieces),
            f32(8, 128),
            f32(8, 128),
            f32(X_SIZE, 8, 128),
            f32(Y_SIZE, 8, 128),
            f32(Z_SIZE, 8, 128),
            dma((12 + 3 * groups,)),
            dma((2 * groups + 1,)),
            *pairs(6), *pairs(3), *pairs(groups), *pairs(groups, 4), *pairs(groups, 4), *pairs(groups, Z_SIZE),
            *pairs(groups, 4), *pairs(groups, 4), *pairs(groups, 4),
            *pairs(1), *pairs(X_SIZE), *pairs(Y_SIZE), *pairs(Z_SIZE),
        ],
        compiler_params=pltpu.CompilerParams(
            collective_id=0, has_side_effects=True, vmem_limit_bytes=56 * 1024 * 1024
        ),
        cost_estimate=pl.CostEstimate(flops=6_000_000_000, bytes_accessed=10_000_000, transcendentals=1_000_000),
    )(mask_ids, band_type, tokens, cotangent, table, w_qkv, w_proj, ln_gain, ln_shift, *constants)
    d_tokens, g_qkv, g_proj, g_table, g_gain, g_shift = pl.pallas_call(
        assemble_kernel,
        out_shape=(
            jax.ShapeDtypeStruct(tokens.shape, BF),
            jax.ShapeDtypeStruct((channels, 3 * channels), BF),
            jax.ShapeDtypeStruct((channels, channels), BF),
            jax.ShapeDtypeStruct(table.shape, BF),
            jax.ShapeDtypeStruct((channels,), F32),
            jax.ShapeDtypeStruct((channels,), F32),
        ),
        in_specs=[scalars, anywhere, anywhere, vmem, vmem],
        out_specs=(anywhere, vmem, vmem, vmem, vmem, vmem),
        scratch_shapes=[
            bf(*pieces),
            bf(*tokens.shape),
            f32(4, heads * ROWS, 512),
            f32(*table.shape),
            dma((groups + 2,)),
        ],
        compiler_params=pltpu.CompilerParams(vmem_limit_bytes=60 * 1024 * 1024),
        cost_estimate=pl.CostEstimate(flops=100_000_000, bytes_accessed=6_000_000, transcendentals=0),
    )(band_type, full, joined, small, constants[-1])
    return d_tokens, g_qkv, g_proj, g_gain, g_shift, g_table.transpose(1, 0, 2)


def solution(mesh):
    placed = (P(None, "lat", "lon", None),) * 2 + (P(None, "lat"),) + (P(),) * 6
    return jax.shard_map(
        local,
        mesh=mesh,
        in_specs=placed,
        out_specs=(P(None, "lat", "lon", None), P(), P(), P(), P(), P()),
        check_vma=False,
    )
```
